128 devices in a mesh: pipe: 2 (over core), tensor: 4 (over y), dp: 16 (over z, x).
Axes of the slice: x: 4, y: 4, z: 4, core: 2. Of those that a mesh axis runs over, the one named last changes fastest.
Arguments:
- inputs: bfloat16 [2, 16, 197, 768], P(None, 'dp'), may hold values from -6 to 6
- out_grad: bfloat16 [2, 16, 197, 768], P(None, 'dp'), may hold values from -6 to 6
- routes: int32 [2, 2, 16, 197, 2], P('pipe', None, 'dp'), may hold values from 0 to 3, as said below
- positions: int32 [2, 2, 16, 197, 2], P('pipe', None, 'dp'), may hold values from 0 to 110, as said below
- norm1_gain: float32 [2, 768], P('pipe'), may hold values from 0.1 to 1.9
- norm1_bias: float32 [2, 768], P('pipe'), may hold values from -3 to 3
- qkv_weight: bfloat16 [2, 3, 768, 768], P('pipe', None, None, 'tensor'), may hold values from -0.21875 to 0.21875
- proj_weight: bfloat16 [2, 768, 768], P('pipe', 'tensor'), may hold values from -1.75 to 1.75
- norm2_gain: float32 [2, 768], P('pipe'), may hold values from 0.1 to 1.9
- norm2_bias: float32 [2, 768], P('pipe'), may hold values from -3 to 3
- router_weight: float32 [2, 768, 4], P('pipe'), may hold values from -0.15625 to 0.15625
- expert_in: bfloat16 [2, 4, 768, 3072], P('pipe', None, None, 'tensor'), may hold values from -0.21875 to 0.21875
- expert_out: bfloat16 [2, 4, 3072, 768], P('pipe', None, 'tensor'), may hold values from -0.875 to 0.875
Outputs:
- activations: bfloat16 [2, 2, 16, 197, 768], P('pipe', None, 'dp')
- input_grads: bfloat16 [2, 2, 16, 197, 768], P('pipe', None, 'dp')
- grad_norm1_gain: float32 [2, 768], P('pipe', 'dp')
- grad_norm1_bias: float32 [2, 768], P('pipe', 'dp')
- grad_qkv: float32 [2, 3, 768, 768], P('pipe', None, 'dp', 'tensor')
- grad_proj: float32 [2, 768, 768], P('pipe', 'tensor', 'dp')
- grad_norm2_gain: float32 [2, 768], P('pipe', 'dp')
- grad_norm2_bias: float32 [2, 768], P('pipe', 'dp')
- grad_router: float32 [2, 768, 4], P('pipe', 'dp')
- grad_expert_in: float32 [2, 4, 768, 3072], P('pipe', None, 'dp', 'tensor')
- grad_expert_out: float32 [2, 4, 3072, 768], P('pipe', None, 'tensor', 'dp')
The draws below stay inside these ranges and needn't reach their ends.
Inputs may be any that keep to these rules, and one draw needn't show every extreme that they name: `routes`: A token's two experts differ. In each aligned block of 197 tokens (one micro-batch of one section on one index of dp) an expert is named at most 111 times, and some expert exactly 111 times. Within an aligned block of 197 tokens the pairs (routes, positions) of all its tokens and both choices are all different.
All inputs are finite; a program needn't handle non-finite values.
Results may differ from the reference program's by a relative error of at most 0.034.
Values may be sent and summed in bfloat16 or wider, within the bound.
No kernel may reach another device: no remote copies, remote signals or barrier semaphores. Data moves between devices by JAX's collectives and lax.ppermute only.
A program may use at most 192 MiB of HBM per device.

```python
import math
import jax
import jax.numpy as jnp
from jax import lax

D = 768
HEADS = 12
HD = 64
FF = 3072
E = 4
SEQ = 197
MICRO = 2
IMG_MB = 1
TOK_MB = 197
IMAGES = 16
CAP = 111


def routing_table(key):
    block_count = 2 * MICRO * (IMAGES // IMG_MB)
    slot_ids = jnp.arange(E * CAP, dtype=jnp.int32)

    def one_block(block_key):
        key_full, key_order, key_tokens = jax.random.split(block_key, 3)
        full_expert = jax.random.randint(key_full, (), 0, E, dtype=jnp.int32)
        shuffled_ids = jax.random.permutation(key_order, E * CAP).astype(jnp.int32)
        priority = jnp.where(slot_ids // CAP == full_expert, -1, shuffled_ids)
        chosen = jnp.sort(jnp.argsort(priority, stable=True)[:2 * TOK_MB].astype(jnp.int32))
        paired = jnp.stack([chosen[:TOK_MB], chosen[TOK_MB:]], axis=-1)
        return paired[jax.random.permutation(key_tokens, TOK_MB)]
    route_table = jax.vmap(one_block)(jax.random.split(key, block_count))
    return route_table.reshape(2, MICRO, IMAGES, SEQ, 2).astype(jnp.int32)


def draw_routes(key, part):
    route_table = routing_table(key)
    return route_table // CAP


def draw_positions(key, part):
    route_table = routing_table(key)
    return route_table % CAP


def spiked(values, rng, source, target, blocks, factor):
    def block_of(axis_at):
        return (jnp.arange(values.shape[axis_at]) // (values.shape[axis_at] // blocks)).reshape((-1,) + (1,) * (values.ndim - 1 - axis_at))

    one_side = jax.random.permutation(rng, blocks)[block_of(target)]
    far = (block_of(target) + blocks // 2) % blocks
    return jnp.where((block_of(source) == one_side) | (block_of(source) == far), factor * values, values)


def levels(stream_key, shape, cuts, low, high):
    def one(dim, blocks):
        heights = jax.random.uniform(jax.random.fold_in(jax.random.fold_in(stream_key, 6), dim), (blocks,), jnp.float32, low / len(cuts), high / len(cuts))
        return jnp.repeat(jnp.exp(heights), shape[dim] // blocks).reshape((-1,) + (1,) * (len(shape) - dim - 1))

    factor_of = one(*cuts[0])
    for cut in cuts[1:]:
        factor_of = factor_of * one(*cut)
    return factor_of


def normal_values(own_key, shape, scale, most, cuts=(), kind=jnp.bfloat16):
    level = levels(own_key, shape, cuts, -0.22, 0.18) if cuts else 1.0
    entries = jax.random.normal(own_key, shape, jnp.float32) * scale * level
    return jnp.minimum(jnp.maximum(entries, -most), most).astype(kind)


def gaussian_with(rng, extent, spread, bound, pieces, heavy, kind=jnp.bfloat16):
    values = spread * jax.random.normal(rng, extent, jnp.float32)
    if pieces:
        values = values * levels(rng, extent, pieces, -0.22, 0.18)
    return jnp.clip(spiked(values, jax.random.fold_in(rng, 3), *heavy), -bound, bound).astype(kind)


def setup_inputs(seed: int = 0) -> dict:
    key_list = jax.random.split(jax.random.key(seed), 14)
    return {
        "inputs": normal_values(key_list[0], (MICRO, IMAGES, SEQ, D), 1.0, 6.0, ((1, 16),)),
        "out_grad": gaussian_with(key_list[1], (MICRO, IMAGES, SEQ, D), 1.0, 6.0, ((1, 16),), (1, 3, 16, 2.0)),
        "routes": draw_routes(jax.random.fold_in(key_list[13], 71), 0),
        "positions": draw_positions(jax.random.fold_in(key_list[13], 71), 0),
        "norm1_gain": jnp.clip(1.0 + 0.18 * jax.random.normal(key_list[4], (2, D), jnp.float32), 0.1, 1.9),
        "norm1_bias": normal_values(key_list[5], (2, D), 0.5, 3.0, ((0, 2),), jnp.float32),
        "qkv_weight": normal_values(key_list[6], (2, 3, D, D), D ** -0.5, 0.21875, ((0, 2), (3, 4))),
        "proj_weight": normal_values(key_list[7], (2, D, D), (D // 64) ** -0.5, 1.75, ((0, 2), (1, 4))),
        "norm2_gain": jnp.clip(1.0 + 0.18 * jax.random.normal(key_list[8], (2, D), jnp.float32), 0.1, 1.9),
        "norm2_bias": normal_values(key_list[9], (2, D), 0.5, 3.0, ((0, 2),), jnp.float32),
        "router_weight": normal_values(key_list[10], (2, D, E), (2 * D) ** -0.5, 0.15625, ((0, 2),), jnp.float32),
        "expert_in": normal_values(key_list[11], (2, E, D, FF), D ** -0.5, 0.21875, ((0, 2), (3, 4))),
        "expert_out": normal_values(key_list[12], (2, E, FF, D), (FF // 64) ** -0.5, 0.875, ((0, 2), (2, 4))),
    }


highest = lax.Precision.HIGHEST
eps = 1e-06

@jax.custom_vjp
def low(v):
    return lax.optimization_barrier(v.astype(jnp.bfloat16)).astype(jnp.float32)

@jax.custom_vjp
def low_back(v):
    return v

def low_keep(v):
    return (low(v), None)

def low_pass(kept, grad):
    return (grad,)

def back_keep(v):
    return (v, None)

def back_low(kept, grad):
    return (low(grad),)
low.defvjp(low_keep, low_pass)
low_back.defvjp(back_keep, back_low)

def layer_norm(source, gain, bias):
    average = lax.optimization_barrier(jnp.mean(source, axis=-1, keepdims=True))
    centred = source - average
    variance = lax.optimization_barrier(jnp.mean(centred * centred, axis=-1, keepdims=True))
    return centred * lax.rsqrt(variance + eps) * gain + bias

def section_forward(source, routes, positions, norm1_gain, norm1_bias, qkv_weight, proj_weight, norm2_gain, norm2_bias, router_weight, expert_in, expert_out):
    images = source.shape[0]
    blocks = images // IMG_MB
    scaling = 1.0 / math.sqrt(HD)
    normed1 = low(layer_norm(source, norm1_gain, norm1_bias))
    triple = jnp.einsum('isd,jdf->jisf', normed1, qkv_weight, precision=highest)
    triple = low_back(low(triple))
    by_head = triple.reshape(3, images, SEQ, HEADS, HD)
    scores = low_back(jnp.einsum('iqhc,ikhc->ihqk', by_head[0], by_head[1], precision=highest) * scaling)
    weights = low(jax.nn.softmax(scores, axis=-1))
    attended = jnp.einsum('ihqk,ikhc->iqhc', weights, by_head[2], precision=highest).reshape(images, SEQ, D)
    attended = low_back(low(attended))
    branch = low_back(jnp.einsum('isd,de->ise', attended, proj_weight, precision=highest))
    hidden = source + branch
    normed2 = layer_norm(hidden, norm2_gain, norm2_bias)
    router_probs = jax.nn.softmax(jnp.einsum('isd,de->ise', normed2, router_weight, precision=highest), axis=-1)
    flat_rows = low(normed2).reshape(blocks, TOK_MB, D)
    router_probs = router_probs.reshape(blocks, TOK_MB, E)
    route_rows = routes.reshape(blocks, TOK_MB, 2)
    slot_rows = positions.reshape(blocks, TOK_MB, 2)
    targets = (route_rows * CAP + slot_rows)[..., None]
    matches = (targets == jnp.arange(E * CAP, dtype=jnp.int32)).astype(jnp.float32)
    gate_values = jnp.take_along_axis(router_probs, route_rows, axis=-1)
    dispatch = lax.optimization_barrier(jnp.sum(matches, axis=2))
    combine = lax.optimization_barrier(jnp.sum(matches * gate_values[..., None], axis=2))
    buffer = jnp.einsum('btj,btd->bjd', dispatch, flat_rows, precision=highest).reshape(blocks, E, CAP, D)
    expert_pre = low_back(jnp.einsum('becd,edf->becf', buffer, expert_in, precision=highest))
    active = low(jax.nn.gelu(expert_pre))
    result = low_back(jnp.einsum('becf,efd->becd', active, expert_out, precision=highest)).reshape(blocks, E * CAP, D)
    mixture = jnp.einsum('btj,bjd->btd', combine, result, precision=highest).reshape(images, SEQ, D)
    return hidden + mixture

def section_layer(section_index, routes, positions):

    def micro_layers(source, *weights):
        return jnp.stack([section_forward(source[m], routes[section_index, m], positions[section_index, m], *weights) for m in range(MICRO)])
    return micro_layers

def reference(inputs, out_grad, routes, positions, norm1_gain, norm1_bias, qkv_weight, proj_weight, norm2_gain, norm2_bias, router_weight, expert_in, expert_out):
    parameters = [p.astype(jnp.float32) for p in (norm1_gain, norm1_bias, qkv_weight, proj_weight, norm2_gain, norm2_bias, router_weight, expert_in, expert_out)]
    first_out, first_back = jax.vjp(section_layer(0, routes, positions), inputs.astype(jnp.float32), *[p[0] for p in parameters])
    middle = first_out.astype(jnp.bfloat16)
    second_out, second_back = jax.vjp(section_layer(1, routes, positions), middle.astype(jnp.float32), *[p[1] for p in parameters])
    second_grads = second_back(out_grad.astype(jnp.float32))
    passed = second_grads[0].astype(jnp.bfloat16)
    first_grads = first_back(passed.astype(jnp.float32))
    activations = jnp.stack([middle, second_out.astype(jnp.bfloat16)])
    input_grads = jnp.stack([first_grads[0].astype(jnp.bfloat16), passed])
    stacked = [jnp.stack([first_grads[i + 1], second_grads[i + 1]]) for i in range(9)]
    return (activations, input_grads, stacked[0], stacked[1], stacked[2], stacked[3], stacked[4], stacked[5], stacked[6], stacked[7], stacked[8])
```

```python
import functools
import math

import jax
import jax.numpy as jnp
from jax import lax
from jax.experimental import pallas as pl
from jax.experimental.pallas import tpu as pltpu
from jax.sharding import PartitionSpec as P

HD = 64
E = 4
SEQ = 197
CAP = 111
ROWS = 208
SLOTS = 112
TABLE = E * SLOTS
BOTH = 2 * SLOTS
D = 768
LOCAL = 192
LANES = 128
WIDE = D + LANES
ROUTER_AT = 4

f32 = jnp.float32
bf16 = jnp.bfloat16
eps = 1e-06
VMEM = pl.BlockSpec(memory_space=pltpu.VMEM)
SMEM = pl.BlockSpec(memory_space=pltpu.SMEM)
ANY = pl.BlockSpec(memory_space=pl.ANY)
DMA = pltpu.SemaphoreType.DMA
LIMIT = 56 * 1024 * 1024


def dot(a, b):
    return lax.dot_general(a, b, (((1,), (0,)), ((), ())), preferred_element_type=f32)


def dot_nt(a, b):
    return lax.dot_general(a, b, (((1,), (1,)), ((), ())), preferred_element_type=f32)


def dot_tn(a, b):
    return lax.dot_general(a, b, (((0,), (0,)), ((), ())), preferred_element_type=f32)


def unit_norm(v):
    centred = v - jnp.mean(v, axis=-1, keepdims=True)
    inverse = lax.rsqrt(jnp.mean(centred * centred, axis=-1, keepdims=True) + eps)
    return centred * inverse, inverse


def norm_back(upstream, normed, inverse, gain):
    scaled = upstream * gain
    inner = jnp.mean(scaled * normed, axis=-1, keepdims=True)
    return inverse * (scaled - jnp.mean(scaled, axis=-1, keepdims=True) - normed * inner)


def head_mask(head):
    lane = lax.broadcasted_iota(jnp.int32, (1, LOCAL), 1)
    inside = (lane >= head * HD) & (lane < (head + 1) * HD)
    return jnp.where(inside, 1.0, 0.0).astype(bf16)


def slot_rows(row_ids):
    ids = lax.broadcasted_iota(jnp.int32, (TABLE, ROWS), 0)
    return jnp.where(ids == row_ids, 1.0, 0.0)


def slot_columns(column_ids):
    ids = lax.broadcasted_iota(jnp.int32, (ROWS, TABLE), 1)
    return jnp.where(ids == column_ids, 1.0, 0.0)


def expert_lanes(route):
    lane = lax.broadcasted_iota(jnp.int32, (ROWS, LANES), 1)
    return lane == route + ROUTER_AT


def attention_forward(summed, *refs):
    if summed:
        hidden, p0, p1, p2, p3, *refs = refs
    else:
        x_ref, *refs = refs
    gain, bias, w_qkv, w_proj, part, n1_ref, qkv_ref, p_ref, o_ref, *more = refs
    if summed:
        total = hidden[...] + (
            (p0[...].astype(f32) + p1[...].astype(f32))
            + (p2[...].astype(f32) + p3[...].astype(f32))
        )
        source = total.astype(bf16)
        more[0][...] = source
    else:
        source = x_ref[...]
    normed, _ = unit_norm(source.astype(f32))
    n1 = (normed * gain[...] + bias[...]).astype(bf16)
    n1_ref[...] = n1
    query, key, value = (dot(n1, w_qkv[j]).astype(bf16) for j in range(3))
    qkv_ref[0] = query
    qkv_ref[1] = key
    qkv_ref[2] = value
    real = lax.broadcasted_iota(jnp.int32, (1, ROWS), 1) < SEQ
    attended = jnp.zeros((ROWS, LOCAL), f32)
    for head in range(LOCAL // HD):
        mask = head_mask(head)
        scores = dot_nt(query * mask, key) * (1.0 / math.sqrt(HD))
        scores = jnp.where(real, scores, -1e30)
        shifted = jnp.exp(scores - jnp.max(scores, axis=-1, keepdims=True))
        weights = (shifted / jnp.sum(shifted, axis=-1, keepdims=True)).astype(bf16)
        p_ref[head] = weights
        attended = attended + dot(weights, value * mask)
    attended = attended.astype(bf16)
    o_ref[...] = attended
    part[...] = dot(attended, w_proj[...]).astype(bf16)


def run_attention_forward(source, gain, bias, w_qkv, w_proj):
    summed = isinstance(source, (tuple, list))
    sources = list(source) if summed else [source]
    outs = [
        jax.ShapeDtypeStruct((ROWS, D), bf16),
        jax.ShapeDtypeStruct((ROWS, D), bf16),
        jax.ShapeDtypeStruct((3, ROWS, LOCAL), bf16),
        jax.ShapeDtypeStruct((3, ROWS, ROWS), bf16),
        jax.ShapeDtypeStruct((ROWS, LOCAL), bf16),
    ]
    if summed:
        outs.append(jax.ShapeDtypeStruct((ROWS, D), bf16))
    return pl.pallas_call(
        functools.partial(attention_forward, summed),
        out_shape=outs,
        in_specs=[VMEM] * (len(sources) + 4),
        out_specs=[VMEM] * len(outs),
        compiler_params=pltpu.CompilerParams(vmem_limit_bytes=LIMIT),
        cost_estimate=pl.CostEstimate(
            flops=600_000_000, bytes_accessed=4_000_000, transcendentals=130_000
        ),
        name="attention_fwd",
    )(*sources, gain, bias, w_qkv, w_proj)


def experts_forward(*refs):
    xs, refs = refs[:2], refs[2:]
    parts, refs = (refs[:4], refs[4:8]), refs[8:]
    gain, bias, router, columns, lines, w_in, w_out, *refs = refs
    mixes, hiddens, n2s, probs, y0s, y1s = (refs[2 * j : 2 * j + 2] for j in range(6))
    buffer_out, active_out, slope_out, *refs = refs[12:]
    in_scr, out_scr, b_scr, u_scr, s_scr, y_scr, in_sem, out_sem, save_sem = refs
    loads_in = [pltpu.make_async_copy(w_in.at[e], in_scr.at[e], in_sem.at[e]) for e in range(E)]
    loads_out = [
        pltpu.make_async_copy(w_out.at[e], out_scr.at[e], out_sem.at[e]) for e in range(E)
    ]
    for e in range(E):
        loads_in[e].start()
        loads_out[e].start()
    router_wide = router[...]
    router_high = router_wide.astype(bf16)
    router_low = (router_wide - router_high.astype(f32)).astype(bf16)
    lane = lax.broadcasted_iota(jnp.int32, (1, LANES), 1)
    expert_lane = (lane >= ROUTER_AT) & (lane < ROUTER_AT + E)
    gates = []
    for i in range(2):
        hidden = xs[i][...].astype(f32) + (
            (parts[i][0][...].astype(f32) + parts[i][1][...].astype(f32))
            + (parts[i][2][...].astype(f32) + parts[i][3][...].astype(f32))
        )
        hiddens[i][...] = hidden
        normed, _ = unit_norm(hidden)
        n2 = normed * gain[...] + bias[...]
        high = n2.astype(bf16)
        low = (n2 - high.astype(f32)).astype(bf16)
        n2s[i][...] = high
        logits = dot(high, router_high) + (dot(low, router_high) + dot(high, router_low))
        logits = jnp.where(expert_lane, logits, -1e30)
        raised = jnp.exp(logits - jnp.max(logits, axis=-1, keepdims=True))
        prob = raised / jnp.sum(raised, axis=-1, keepdims=True)
        probs[i][...] = prob
        routes = columns[i]
        gates.append(
            [
                jnp.sum(
                    jnp.where(expert_lanes(routes[:, k : k + 1]), prob, 0.0),
                    axis=-1,
                    keepdims=True,
                )
                for k in range(2)
            ]
        )
        slots = lines[i]
        spread = (slot_rows(slots[0:1]) + slot_rows(slots[1:2])).astype(bf16)
        rows = dot(spread, high).astype(bf16)
        for e in range(E):
            b_scr[e, i * SLOTS : (i + 1) * SLOTS] = rows[e * SLOTS : (e + 1) * SLOTS]
    saves = [pltpu.make_async_copy(b_scr, buffer_out, save_sem.at[2 * E])]
    saves[0].start()
    curve = math.sqrt(2.0 / math.pi)
    for e in range(E):
        loads_in[e].wait()
        z = dot(b_scr[e], in_scr[e])
        square = z * z
        bend = jnp.tanh(curve * z * (1.0 + 0.044715 * square))
        half = 0.5 * (1.0 + bend)
        active = (z * half).astype(bf16)
        u_scr[e] = active
        slope = half + (0.5 * curve) * z * (1.0 - bend * bend) * (1.0 + 0.134145 * square)
        s_scr[e] = slope.astype(bf16)
        for held, kept, sem in ((u_scr, active_out, 2 * e), (s_scr, slope_out, 2 * e + 1)):
            copy = pltpu.make_async_copy(held.at[e], kept.at[e], save_sem.at[sem])
            copy.start()
            saves.append(copy)
        loads_out[e].wait()
        y = dot(active, out_scr[e]).astype(bf16)
        for i in range(2):
            y_scr[i, e * SLOTS : (e + 1) * SLOTS] = y[i * SLOTS : (i + 1) * SLOTS]
    for i in range(2):
        routes = columns[i]
        table = y_scr[i]
        mix = jnp.zeros((ROWS, D), f32)
        for k, kept in enumerate((y0s[i], y1s[i])):
            picked = dot(slot_columns(routes[:, 2 + k : 3 + k]).astype(bf16), table)
            kept[...] = picked.astype(bf16)
            mix = mix + gates[i][k] * picked
        mixes[i][...] = mix.astype(bf16)
    for copy in saves:
        copy.wait()


def run_experts_forward(xs, parts, gain, bias, router, columns, lines, w_in, w_out):
    narrow = jax.ShapeDtypeStruct((ROWS, D), bf16)
    table = jax.ShapeDtypeStruct((E, BOTH, D), bf16)
    outs = (
        [narrow] * 2
        + [jax.ShapeDtypeStruct((ROWS, D), f32)] * 2
        + [narrow] * 2
        + [jax.ShapeDtypeStruct((ROWS, LANES), f32)] * 2
        + [narrow] * 4
        + [table] * 3
    )
    result = pl.pallas_call(
        experts_forward,
        out_shape=outs,
        in_specs=[VMEM] * 15 + [ANY] * 2,
        out_specs=[VMEM] * 12 + [ANY] * 3,
        scratch_shapes=[
            pltpu.VMEM((E, D, D), bf16),
            pltpu.VMEM((E, D, D), bf16),
            pltpu.VMEM((E, BOTH, D), bf16),
            pltpu.VMEM((E, BOTH, D), bf16),
            pltpu.VMEM((E, BOTH, D), bf16),
            pltpu.VMEM((2, TABLE, D), bf16),
            DMA((E,)),
            DMA((E,)),
            DMA((2 * E + 1,)),
        ],
        compiler_params=pltpu.CompilerParams(vmem_limit_bytes=LIMIT),
        cost_estimate=pl.CostEstimate(
            flops=4_000_000_000, bytes_accessed=24_000_000, transcendentals=700_000
        ),
        name="experts_fwd",
    )(*xs, *parts[0], *parts[1], gain, bias, router, columns, lines, w_in, w_out)
    mixes, hiddens, n2s, probs, y0s, y1s = (result[2 * j : 2 * j + 2] for j in range(6))
    return mixes, hiddens, n2s, probs, y0s, y1s, tuple(result[12:])


def experts_backward(*refs):
    grads, probs, y0s, y1s = (refs[2 * j : 2 * j + 2] for j in range(4))
    columns, lines, slope_in, w_in, w_out, *refs = refs[8:]
    partials, refs = refs[:2], refs[2:]
    slot_out, pre_out, *refs = refs
    in_scr, out_scr, s_scr, dy_scr, dz_scr, db_scr, in_sem, out_sem, s_sem, save_sem = refs
    loads = []
    for e in range(E):
        loads.append(
            (
                pltpu.make_async_copy(w_out.at[e], out_scr.at[e], out_sem.at[e]),
                pltpu.make_async_copy(slope_in.at[e], s_scr.at[e], s_sem.at[e]),
                pltpu.make_async_copy(w_in.at[e], in_scr.at[e], in_sem.at[e]),
            )
        )
        for copy in loads[e]:
            copy.start()
    lane = lax.broadcasted_iota(jnp.int32, (ROWS, LANES), 1)
    for i in range(2):
        upstream = grads[i][...].astype(f32)
        routes = columns[i]
        slots = lines[i]
        rows = jnp.zeros((TABLE, D), f32)
        packed = jnp.zeros((ROWS, LANES), f32)
        for k, picked in enumerate((y0s[i], y1s[i])):
            gate = jnp.sum(
                jnp.where(expert_lanes(routes[:, k : k + 1]), probs[i][...], 0.0),
                axis=-1,
                keepdims=True,
            )
            rows = rows + dot(
                slot_rows(slots[k : k + 1]).astype(bf16), (gate * upstream).astype(bf16)
            )
            inner = jnp.sum(upstream * picked[...].astype(f32), axis=-1, keepdims=True)
            high = inner.astype(bf16).astype(f32)
            packed = packed + jnp.where(lane == k, high, 0.0)
            packed = packed + jnp.where(lane == 2 + k, inner - high, 0.0)
        partials[i][:, D:] = packed.astype(bf16)
        rows = rows.astype(bf16)
        for e in range(E):
            dy_scr[e, i * SLOTS : (i + 1) * SLOTS] = rows[e * SLOTS : (e + 1) * SLOTS]
    saves = [pltpu.make_async_copy(dy_scr, slot_out, save_sem.at[E])]
    saves[0].start()
    for e in range(E):
        loads[e][0].wait()
        grad_active = dot_nt(dy_scr[e], out_scr[e])
        loads[e][1].wait()
        grad_pre = (grad_active * s_scr[e].astype(f32)).astype(bf16)
        dz_scr[e] = grad_pre
        copy = pltpu.make_async_copy(dz_scr.at[e], pre_out.at[e], save_sem.at[e])
        copy.start()
        saves.append(copy)
        loads[e][2].wait()
        grad_rows = dot_nt(grad_pre, in_scr[e]).astype(bf16)
        for i in range(2):
            db_scr[i, e * SLOTS : (e + 1) * SLOTS] = grad_rows[i * SLOTS : (i + 1) * SLOTS]
    for i in range(2):
        routes = columns[i]
        gather = slot_columns(routes[:, 2:3]) + slot_columns(routes[:, 3:4])
        partials[i][:, :D] = dot(gather.astype(bf16), db_scr[i]).astype(bf16)
    for copy in saves:
        copy.wait()


def run_experts_backward(grads, probs, y0s, y1s, columns, lines, slope, w_in, w_out):
    table = jax.ShapeDtypeStruct((E, BOTH, D), bf16)
    outs = [jax.ShapeDtypeStruct((ROWS, WIDE), bf16)] * 2 + [table] * 2
    result = pl.pallas_call(
        experts_backward,
        out_shape=outs,
        in_specs=[VMEM] * 10 + [ANY] * 3,
        out_specs=[VMEM] * 2 + [ANY] * 2,
        scratch_shapes=[
            pltpu.VMEM((E, D, D), bf16),
            pltpu.VMEM((E, D, D), bf16),
            pltpu.VMEM((E, BOTH, D), bf16),
            pltpu.VMEM((E, BOTH, D), bf16),
            pltpu.VMEM((E, BOTH, D), bf16),
            pltpu.VMEM((2, TABLE, D), bf16),
            DMA((E,)),
            DMA((E,)),
            DMA((E,)),
            DMA((E + 1,)),
        ],
        compiler_params=pltpu.CompilerParams(vmem_limit_bytes=LIMIT),
        cost_estimate=pl.CostEstimate(
            flops=4_000_000_000, bytes_accessed=20_000_000, transcendentals=0
        ),
        name="experts_bwd",
    )(*grads, *probs, *y0s, *y1s, columns, lines, slope, w_in, w_out)
    return result[:2], result[2], result[3]


def attention_backward(
    grad_ref,
    p0,
    p1,
    p2,
    p3,
    hidden,
    prob_ref,
    column,
    router,
    gain2,
    weights_ref,
    qkv_ref,
    w_proj,
    w_qkv,
    x_ref,
    part,
    grad_hidden_ref,
    branch_ref,
    triple_ref,
    logit_ref,
    rows_ref,
):
    def total(columns):
        return (p0[:, columns].astype(f32) + p1[:, columns].astype(f32)) + (
            p2[:, columns].astype(f32) + p3[:, columns].astype(f32)
        )

    upstream = grad_ref[...].astype(f32)
    lane = lax.broadcasted_iota(jnp.int32, (ROWS, LANES), 1)
    inner = total(slice(D, WIDE))
    prob = prob_ref[...]
    grad_prob = jnp.zeros((ROWS, LANES), f32)
    for k in range(2):
        mine = (lane == k) | (lane == 2 + k)
        value = jnp.sum(jnp.where(mine, inner, 0.0), axis=-1, keepdims=True)
        grad_prob = grad_prob + jnp.where(expert_lanes(column[:, k : k + 1]), value, 0.0)
    grad_logit = prob * (grad_prob - jnp.sum(prob * grad_prob, axis=-1, keepdims=True))
    grad_logit = grad_logit.astype(bf16)
    logit_ref[...] = grad_logit
    grad_n2 = total(slice(0, D)) + dot_nt(grad_logit, router[...].astype(bf16))
    unit2, inverse2 = unit_norm(hidden[...])
    grad_hidden = upstream + norm_back(grad_n2, unit2, inverse2, gain2[...])
    grad_hidden_ref[...] = grad_hidden
    rows_ref[...] = jnp.zeros_like(rows_ref)
    rows_ref[2:3] = jnp.sum(grad_n2 * unit2, axis=0, keepdims=True)
    rows_ref[3:4] = jnp.sum(grad_n2, axis=0, keepdims=True)
    branch = grad_hidden.astype(bf16)
    branch_ref[...] = branch
    grad_attended = dot_nt(branch, w_proj[...]).astype(bf16)
    query, key, value = (qkv_ref[j] for j in range(3))
    grad_query = jnp.zeros((ROWS, LOCAL), f32)
    grad_key = jnp.zeros((ROWS, LOCAL), f32)
    grad_value = jnp.zeros((ROWS, LOCAL), f32)
    for head in range(LOCAL // HD):
        mask = head_mask(head)
        weights = weights_ref[head]
        wide = weights.astype(f32)
        arriving = grad_attended * mask
        grad_weights = dot_nt(arriving, value)
        grad_scores = wide * (
            grad_weights - jnp.sum(wide * grad_weights, axis=-1, keepdims=True)
        )
        grad_scores = grad_scores.astype(bf16)
        grad_value = grad_value + dot_tn(weights, arriving)
        grad_query = grad_query + dot(grad_scores, key * mask)
        grad_key = grad_key + dot_tn(grad_scores, query * mask)
    scaling = 1.0 / math.sqrt(HD)
    grad_n1 = jnp.zeros((ROWS, D), f32)
    for j, grad in enumerate((grad_query * scaling, grad_key * scaling, grad_value)):
        narrow = grad.astype(bf16)
        triple_ref[j] = narrow
        grad_n1 = grad_n1 + dot_nt(narrow, w_qkv[j])
    part[...] = grad_n1.astype(bf16)
    unit1, _ = unit_norm(x_ref[...].astype(f32))
    rows_ref[0:1] = jnp.sum(grad_n1 * unit1, axis=0, keepdims=True)
    rows_ref[1:2] = jnp.sum(grad_n1, axis=0, keepdims=True)


def run_attention_backward(*operands):
    return pl.pallas_call(
        attention_backward,
        out_shape=[
            jax.ShapeDtypeStruct((ROWS, D), bf16),
            jax.ShapeDtypeStruct((ROWS, D), f32),
            jax.ShapeDtypeStruct((ROWS, D), bf16),
            jax.ShapeDtypeStruct((3, ROWS, LOCAL), bf16),
            jax.ShapeDtypeStruct((ROWS, LANES), bf16),
            jax.ShapeDtypeStruct((16, D), f32),
        ],
        in_specs=[VMEM] * 15,
        out_specs=[VMEM] * 6,
        compiler_params=pltpu.CompilerParams(vmem_limit_bytes=LIMIT),
        cost_estimate=pl.CostEstimate(
            flops=1_000_000_000, bytes_accessed=6_000_000, transcendentals=0
        ),
        name="attention_bwd",
    )(*operands)


def source_backward(p0, p1, p2, p3, grad_hidden, x_ref, gain, out):
    upstream = (p0[...].astype(f32) + p1[...].astype(f32)) + (
        p2[...].astype(f32) + p3[...].astype(f32)
    )
    unit, inverse = unit_norm(x_ref[...].astype(f32))
    out[...] = (grad_hidden[...] + norm_back(upstream, unit, inverse, gain[...])).astype(bf16)


def run_source_backward(parts, grad_hidden, x, gain):
    return pl.pallas_call(
        source_backward,
        out_shape=jax.ShapeDtypeStruct((ROWS, D), bf16),
        in_specs=[VMEM] * 7,
        out_specs=VMEM,
        compiler_params=pltpu.CompilerParams(vmem_limit_bytes=LIMIT),
        cost_estimate=pl.CostEstimate(
            flops=6_000_000, bytes_accessed=3_000_000, transcendentals=0
        ),
        name="source_bwd",
    )(*parts, grad_hidden, x, gain)


def expert_grads(place, buffer, grad_pre, slot_grad, active, *refs):
    outs_in, outs_out, (scr_in, scr_out) = refs[:4], refs[4:8], refs[8:]
    at_z, at_x = place[0], place[1]
    grad_in = dot_tn(buffer[0], grad_pre[0]).astype(bf16)
    grad_out = dot_tn(slot_grad[0], active[0]).astype(bf16)
    for z in range(4):
        for x in range(4):
            at = (4 * z + x) * 48
            scr_in[z, x] = grad_in[at : at + 48]
            scr_out[z, x] = grad_out[at : at + 48]
    for k in range(4):
        to_x = lax.rem(at_x + k, 4)
        to_z = lax.rem(at_z + k, 4)
        for other in range(4):
            outs_in[k][0, other] = scr_in[other, to_x]
            outs_out[k][0, other] = scr_out[to_z, other]


def run_expert_grads(place, buffer, grad_pre, slot_grad, active):
    table = pl.BlockSpec((1, BOTH, D), lambda e: (e, 0, 0))
    block = pl.BlockSpec((1, 4, 48, D), lambda e: (e, 0, 0, 0))
    result = pl.pallas_call(
        expert_grads,
        grid=(E,),
        out_shape=[jax.ShapeDtypeStruct((E, 4, 48, D), bf16)] * 8,
        in_specs=[SMEM] + [table] * 4,
        out_specs=[block] * 8,
        scratch_shapes=[pltpu.VMEM((4, 4, 48, D), bf16)] * 2,
        compiler_params=pltpu.CompilerParams(vmem_limit_bytes=LIMIT),
        cost_estimate=pl.CostEstimate(
            flops=2_200_000_000, bytes_accessed=16_000_000, transcendentals=0
        ),
        name="expert_grads",
    )(place, buffer, grad_pre, slot_grad, active)
    return result[:4], result[4:]


def attention_grads(place, *refs):
    images, outs, scr = (refs[:7], refs[7:14]), refs[14:18], refs[18]
    at_z = place[0]

    def both(first, second):
        return sum(dot_tn(first(image), second(image)) for image in images)

    pieces = [both(lambda m: m[0][...], lambda m, j=j: m[1][j]) for j in range(3)]
    pieces.append(both(lambda m: m[2][...], lambda m: m[3][...]))
    pick = lax.broadcasted_iota(jnp.int32, (16, LANES), 0) == lax.broadcasted_iota(
        jnp.int32, (16, LANES), 1
    )
    pick = jnp.where(pick, 1.0, 0.0).astype(bf16)
    rows = (images[0][6][...] + images[1][6][...]).astype(bf16)
    small = both(lambda m: m[4][...], lambda m: m[5][...]) + dot_tn(rows, pick)
    wide = jnp.concatenate(pieces + [small], axis=1).astype(bf16)
    for z in range(4):
        scr[z] = wide[z * 192 : (z + 1) * 192]
    for k in range(4):
        outs[k][...] = scr[lax.rem(at_z + k, 4)]


def run_attention_grads(place, first, second):
    return pl.pallas_call(
        attention_grads,
        out_shape=[jax.ShapeDtypeStruct((192, WIDE), bf16)] * 4,
        in_specs=[SMEM] + [VMEM] * 14,
        out_specs=[VMEM] * 4,
        scratch_shapes=[pltpu.VMEM((4, 192, WIDE), bf16)],
        compiler_params=pltpu.CompilerParams(vmem_limit_bytes=LIMIT),
        cost_estimate=pl.CostEstimate(
            flops=600_000_000, bytes_accessed=6_000_000, transcendentals=0
        ),
        name="attention_grads",
    )(place, *first, *second)


def expert_middle(place, *refs):
    ins, outs, scr = refs[:8], refs[8:16], refs[16]
    for group, at in ((0, place[0]), (1, place[1])):
        a, b, c, d = (ref[0].astype(f32) for ref in ins[4 * group : 4 * group + 4])
        scr[...] = ((a + b) + (c + d)).astype(bf16)
        for k in range(4):
            outs[4 * group + k][0] = scr[lax.rem(at + k, 4)]


def run_expert_middle(place, by_x, by_z):
    block = pl.BlockSpec((1, 4, 48, D), lambda e: (e, 0, 0, 0))
    piece = pl.BlockSpec((1, 48, D), lambda e: (e, 0, 0))
    result = pl.pallas_call(
        expert_middle,
        grid=(E,),
        out_shape=[jax.ShapeDtypeStruct((E, 48, D), bf16)] * 8,
        in_specs=[SMEM] + [block] * 8,
        out_specs=[piece] * 8,
        scratch_shapes=[pltpu.VMEM((4, 48, D), bf16)],
        compiler_params=pltpu.CompilerParams(vmem_limit_bytes=LIMIT),
        cost_estimate=pl.CostEstimate(
            flops=6_000_000, bytes_accessed=12_000_000, transcendentals=0
        ),
        name="expert_middle",
    )(place, *by_x, *by_z)
    return result[:4], result[4:]


def attention_middle(place, a, b, c, d, *refs):
    outs, scr = refs[:4], refs[4]
    total = (a[...].astype(f32) + b[...].astype(f32)) + (c[...].astype(f32) + d[...].astype(f32))
    total = total.astype(bf16)
    for x in range(4):
        scr[x] = total[x * 48 : (x + 1) * 48]
    for k in range(4):
        outs[k][...] = scr[lax.rem(place[1] + k, 4)]


def run_attention_middle(place, by_z):
    return pl.pallas_call(
        attention_middle,
        out_shape=[jax.ShapeDtypeStruct((48, WIDE), bf16)] * 4,
        in_specs=[SMEM] + [VMEM] * 4,
        out_specs=[VMEM] * 4,
        scratch_shapes=[pltpu.VMEM((4, 48, WIDE), bf16)],
        compiler_params=pltpu.CompilerParams(vmem_limit_bytes=LIMIT),
        cost_estimate=pl.CostEstimate(
            flops=1_000_000, bytes_accessed=2_000_000, transcendentals=0
        ),
        name="attention_middle",
    )(place, *by_z)


def between_heads(x, pipe):
    received = [
        lax.ppermute(
            x, ("pipe", "tensor"), [(4 * pipe + i, 4 * pipe + (i + k) % 4) for i in range(4)]
        )
        for k in range(1, 4)
    ]
    return [x] + received


def onward(x):
    return [
        lax.ppermute(x, ("pipe", "tensor"), [(i, 4 + (i + k) % 4) for i in range(4)])
        for k in range(4)
    ]


def across(x, pipe):
    return lax.ppermute(x, "pipe", [(pipe, 1 - pipe)])


def scattered(xs, pipe, along_z):
    sides = lax.axis_size("dp") // 4
    received = []
    for k in range(1, 4):
        pairs = []
        for z in range(sides):
            for x in range(4):
                if along_z:
                    target = ((z + k) % 4) * 4 + x
                else:
                    target = z * 4 + (x + k) % 4
                pairs.append((16 * pipe + z * 4 + x, 16 * pipe + target))
        received.append(lax.ppermute(xs[k], ("pipe", "dp"), pairs))
    return [xs[0]] + received


def add_up(xs):
    a, b, c, d = (x.astype(f32) for x in xs)
    return (a + b) + (c + d)


def on_device(
    inputs,
    out_grad,
    routes,
    positions,
    norm1_gain,
    norm1_bias,
    qkv_weight,
    proj_weight,
    norm2_gain,
    norm2_bias,
    router_weight,
    expert_in,
    expert_out,
):
    leading = lax.axis_index("pipe") == 0
    at = lax.axis_index("dp")
    place = jnp.stack([at // 4, at % 4]).astype(jnp.int32)
    pad = ((0, 0), (0, ROWS - SEQ), (0, 0))
    sources = jnp.pad(inputs.reshape(2, SEQ, D), pad)
    targets = jnp.pad(out_grad.reshape(2, SEQ, D), pad)
    sources = [sources[i] for i in range(2)]
    targets = [targets[i] for i in range(2)]
    route = routes[0].reshape(2, SEQ, 2)
    slot = route * SLOTS + positions[0].reshape(2, SEQ, 2)
    columns = jnp.pad(jnp.concatenate([route, slot], axis=-1), pad, constant_values=-64)
    lines = columns[:, :, 2:].transpose(0, 2, 1)
    router = jnp.pad(router_weight[0], ((0, 0), (ROUTER_AT, LANES - ROUTER_AT - E)))
    w_qkv, w_proj, w_in, w_out = qkv_weight[0], proj_weight[0], expert_in[0], expert_out[0]

    def forward(entering, pipe):
        firsts = []
        for entry in entering:
            firsts.append(run_attention_forward(entry, norm1_gain, norm1_bias, w_qkv, w_proj))
        if isinstance(entering[0], (tuple, list)):
            xs = [first[5] for first in firsts]
        else:
            xs = entering
        parts = [between_heads(first[0], pipe) for first in firsts]
        mixes, hiddens, n2s, probs, y0s, y1s, saved = run_experts_forward(
            xs, parts, norm2_gain, norm2_bias, router, columns, lines, w_in, w_out
        )
        return mixes, hiddens, (xs, firsts, hiddens, n2s, probs, y0s, y1s, saved)

    def backward(grads, kept, pipe):
        xs, firsts, hiddens, n2s, probs, y0s, y1s, (buffer, active, slope) = kept
        partials, slot_grad, grad_pre = run_experts_backward(
            grads, probs, y0s, y1s, columns, lines, slope, w_in, w_out
        )
        parts = [between_heads(partial, pipe) for partial in partials]
        by_x, by_z = run_expert_grads(place, buffer, grad_pre, slot_grad, active)
        by_x = scattered(by_x, pipe, False)
        by_z = scattered(by_z, pipe, True)
        results = []
        seconds = []
        for i in range(2):
            part, grad_hidden, branch, triple, logit, rows = run_attention_backward(
                grads[i],
                *parts[i],
                hiddens[i],
                probs[i],
                columns[i],
                router,
                norm2_gain,
                firsts[i][3],
                firsts[i][2],
                w_proj,
                w_qkv,
                xs[i],
            )
            results.append((between_heads(part, pipe), grad_hidden))
            seconds.append((firsts[i][1], triple, branch, firsts[i][4], n2s[i], logit, rows))
        passed = [
            run_source_backward(results[i][0], results[i][1], xs[i], norm1_gain)
            for i in range(2)
        ]
        narrow = run_attention_grads(place, *seconds)
        narrow = scattered(narrow, pipe, True)
        return passed, by_x, by_z, narrow

    def reduced(by_x, by_z, narrow, pipe):
        by_x, by_z = run_expert_middle(place, by_x, by_z)
        grad_in = add_up(scattered(by_x, pipe, True))
        grad_out = add_up(scattered(by_z, pipe, False))
        small = add_up(scattered(run_attention_middle(place, narrow), pipe, False))
        return grad_in, grad_out, small

    mixes, hiddens, kept_first = forward(sources, 0)
    entering = [[across(hiddens[i], 0)] + onward(mixes[i]) for i in range(2)]
    mixes, hiddens, kept_second = forward(entering, 1)
    middle = kept_second[0]
    passed, *sums = backward(targets, kept_second, 1)
    arriving = [across(grad, 1) for grad in passed]
    grads_second = reduced(*sums, 1)
    last, *sums = backward(arriving, kept_first, 0)
    grads_first = reduced(*sums, 0)

    first_out = [across(x, 1) for x in middle]
    finals = []
    for i in range(2):
        final = hiddens[i] + add_up(between_heads(mixes[i], 1))
        finals.append(final.astype(bf16))
    activations = jnp.stack([jnp.where(leading, first_out[i], finals[i]) for i in range(2)])
    input_grads = jnp.stack([jnp.where(leading, last[i], passed[i]) for i in range(2)])
    grad_in, grad_out, small = (
        jnp.where(leading, a, b) for a, b in zip(grads_first, grads_second)
    )
    ends = small[:, D : D + 2].astype(bf16)
    norm1 = add_up(
        [ends]
        + [
            lax.ppermute(ends, "tensor", [(i, (i + k) % 4) for i in range(4)])
            for k in range(1, 4)
        ]
    )
    shape_out = (1, 2, 1, SEQ, D)
    return (
        activations[:, :SEQ].reshape(shape_out),
        input_grads[:, :SEQ].reshape(shape_out),
        norm1[:, 0][None],
        norm1[:, 1][None],
        small[:, : 3 * LOCAL].reshape(48, 3, LOCAL).transpose(1, 0, 2)[None],
        small[:, 3 * LOCAL : D].T[None],
        small[:, D + 2][None],
        small[:, D + 3][None],
        small[:, D + ROUTER_AT : D + ROUTER_AT + E][None],
        grad_in[None],
        grad_out.transpose(0, 2, 1)[None],
    )


def solution(mesh):
    in_specs = (
        P(None, "dp", None, None),
        P(None, "dp", None, None),
        P("pipe", None, "dp", None, None),
        P("pipe", None, "dp", None, None),
        P("pipe", None),
        P("pipe", None),
        P("pipe", None, None, "tensor"),
        P("pipe", "tensor", None),
        P("pipe", None),
        P("pipe", None),
        P("pipe", None, None),
        P("pipe", None, None, "tensor"),
        P("pipe", None, "tensor", None),
    )
    out_specs = (
        P("pipe", None, "dp", None, None),
        P("pipe", None, "dp", None, None),
        P("pipe", "dp"),
        P("pipe", "dp"),
        P("pipe", None, "dp", "tensor"),
        P("pipe", "tensor", "dp"),
        P("pipe", "dp"),
        P("pipe", "dp"),
        P("pipe", "dp", None),
        P("pipe", None, "dp", "tensor"),
        P("pipe", None, "tensor", "dp"),
    )
    return jax.shard_map(
        on_device, mesh=mesh, in_specs=in_specs, out_specs=out_specs, check_vma=False
    )
```

```python
import functools
import math

import jax
import jax.numpy as jnp
from jax import lax
from jax.experimental import pallas as pl
from jax.experimental.pallas import tpu as pltpu
from jax.sharding import PartitionSpec as P

HD = 64
E = 4
SEQ = 197
CAP = 111
ROWS = 208
SLOTS = 112
TABLE = E * SLOTS
D = 768
LOCAL = 192
LANES = 128
WIDE = D + LANES
SPARE = 200
ROUTER_AT = 4
ROUTES_AT = 8
SLOTS_AT = 10

f32 = jnp.float32
bf16 = jnp.bfloat16
eps = 1e-06
VMEM = pl.BlockSpec(memory_space=pltpu.VMEM)
SMEM = pl.BlockSpec(memory_space=pltpu.SMEM)
HBM = pl.BlockSpec(memory_space=pl.ANY)
DMA = pltpu.SemaphoreType.DMA
LIMIT = 60 * 1024 * 1024
SHORT = 28 * 1024 * 1024


def dot(a, b):
    return lax.dot_general(a, b, (((1,), (0,)), ((), ())), preferred_element_type=f32)


def dot_nt(a, b):
    return lax.dot_general(a, b, (((1,), (1,)), ((), ())), preferred_element_type=f32)


def dot_tn(a, b):
    return lax.dot_general(a, b, (((0,), (0,)), ((), ())), preferred_element_type=f32)


def unit_norm(v):
    centred = v - jnp.mean(v, axis=-1, keepdims=True)
    inverse = lax.rsqrt(jnp.mean(centred * centred, axis=-1, keepdims=True) + eps)
    return centred * inverse, inverse


def norm_back(upstream, normed, inverse, gain):
    scaled = upstream * gain
    inner = jnp.mean(scaled * normed, axis=-1, keepdims=True)
    return inverse * (scaled - jnp.mean(scaled, axis=-1, keepdims=True) - normed * inner)


def head_mask(head):
    lane = lax.broadcasted_iota(jnp.int32, (1, LOCAL), 1)
    inside = (lane >= head * HD) & (lane < (head + 1) * HD)
    return jnp.where(inside, 1.0, 0.0).astype(bf16)


def slot_rows(row_ids):
    ids = lax.broadcasted_iota(jnp.int32, (TABLE, ROWS), 0)
    return jnp.where(ids == row_ids, 1.0, 0.0)


def slot_columns(column_ids):
    ids = lax.broadcasted_iota(jnp.int32, (ROWS, TABLE), 1)
    return jnp.where(ids == column_ids, 1.0, 0.0)


def expert_lanes(route):
    lane = lax.broadcasted_iota(jnp.int32, (ROWS, LANES), 1)
    return lane == route + ROUTER_AT


def gate_of(prob, route):
    return jnp.sum(jnp.where(expert_lanes(route), prob, 0.0), axis=-1, keepdims=True)


class Picked:
    def __init__(self, own, other, use_own, held, sem):
        self.copies = [pltpu.make_async_copy(ref, held, sem) for ref in (own, other)]
        self.use_own = use_own

    def start(self):
        pl.when(self.use_own)(self.copies[0].start)
        pl.when(jnp.logical_not(self.use_own))(self.copies[1].start)

    def wait(self):
        self.copies[0].wait()


class Halves:
    def __init__(self, core, held, stay_out, send_out, sems):
        self.core, self.held, self.sems = core, held, sems
        self.outs = (stay_out, send_out)
        self.copies = []

    def put(self, j, e, value):
        self.held[j, e] = value
        stay, send = (
            pltpu.make_async_copy(self.held.at[j, e], out.at[j, e % 2], self.sems.at[j, e])
            for out in self.outs
        )
        mine = self.core == e // 2
        pl.when(mine)(stay.start)
        pl.when(jnp.logical_not(mine))(send.start)
        self.copies.append(stay)

    def wait(self):
        for copy in self.copies:
            copy.wait()


class Kept:
    def __init__(self, outs, held, sems):
        self.outs, self.held, self.sems = outs, held, sems
        self.copies = []

    def put(self, at, value, index=None):
        held, out = self.held[at], self.outs[at]
        if index is not None:
            held, out = held.at[index], out.at[index]
        held[...] = value
        copy = pltpu.make_async_copy(held, out, self.sems.at[len(self.copies)])
        copy.start()
        self.copies.append(copy)

    def wait(self):
        for copy in self.copies:
            copy.wait()


def unit_rows():
    row = lax.broadcasted_iota(jnp.int32, (16, LANES), 0)
    lane = lax.broadcasted_iota(jnp.int32, (16, LANES), 1)
    return jnp.where(row == lane, 1.0, 0.0).astype(bf16)


def add_four(refs):
    a, b, c, d = (ref[...].astype(f32) for ref in refs)
    return (a + b) + (c + d)


def attention_forward(section, place, *refs):
    summed = section == 1
    if summed:
        hidden, *refs = refs
        parts, refs = refs[:4], refs[4:]
    else:
        x_ref, *refs = refs
    params, qkv_own, qkv_other, proj_own, proj_other, *refs = refs
    part, refs = refs[0], refs[1:]
    saved, refs = refs[:4], refs[4:]
    *more, w_qkv, w_proj, sems, held_n1, held_qkv, held_p, held_o, save_sems = refs
    kept = Kept(saved, (held_n1, held_qkv, held_p, held_o), save_sems)
    use_own = place[2] == section
    load_qkv = Picked(qkv_own, qkv_other, use_own, w_qkv, sems.at[0])
    load_proj = Picked(proj_own, proj_other, use_own, w_proj, sems.at[1])
    load_qkv.start()
    load_proj.start()
    if summed:
        source = (hidden[...] + add_four(parts)).astype(bf16)
        more[0][...] = source
    else:
        source = x_ref[...]
    normed, _ = unit_norm(source.astype(f32))
    n1 = (normed * params[0:1] + params[1:2]).astype(bf16)
    kept.put(0, n1)
    load_qkv.wait()
    query, key, value = (dot_nt(n1, w_qkv[j]).astype(bf16) for j in range(3))
    for j, piece in enumerate((query, key, value)):
        kept.put(1, piece, j)
    real = lax.broadcasted_iota(jnp.int32, (1, ROWS), 1) < SEQ
    attended = jnp.zeros((ROWS, LOCAL), f32)
    for head in range(LOCAL // HD):
        mask = head_mask(head)
        scores = dot_nt(query * mask, key) * (1.0 / math.sqrt(HD))
        scores = jnp.where(real, scores, -1e30)
        shifted = jnp.exp(scores - jnp.max(scores, axis=-1, keepdims=True))
        weights = (shifted / jnp.sum(shifted, axis=-1, keepdims=True)).astype(bf16)
        kept.put(2, weights, head)
        attended = attended + dot(weights, value * mask)
    attended = attended.astype(bf16)
    kept.put(3, attended)
    load_proj.wait()
    part[...] = dot(attended, w_proj[...]).astype(bf16)
    kept.wait()


def run_attention_forward(section, place, source, params, w_qkv, w_proj):
    saved = [(ROWS, D), (3, ROWS, LOCAL), (3, ROWS, ROWS), (ROWS, LOCAL)]
    outs = [jax.ShapeDtypeStruct((ROWS, D), bf16)]
    outs += [jax.ShapeDtypeStruct(shape, bf16) for shape in saved]
    if section == 1:
        outs.append(jax.ShapeDtypeStruct((ROWS, D), bf16))
    return pl.pallas_call(
        functools.partial(attention_forward, section),
        out_shape=outs,
        in_specs=[SMEM] + [VMEM] * (len(source) + 1) + [HBM] * 4,
        out_specs=[VMEM] + [HBM] * 4 + [VMEM] * (len(outs) - 5),
        scratch_shapes=[
            pltpu.VMEM((3, LOCAL, D), bf16),
            pltpu.VMEM((LOCAL, D), bf16),
            DMA((2,)),
        ]
        + [pltpu.VMEM(shape, bf16) for shape in saved]
        + [DMA((8,))],
        compiler_params=pltpu.CompilerParams(vmem_limit_bytes=LIMIT),
        cost_estimate=pl.CostEstimate(
            flops=600_000_000, bytes_accessed=4_000_000, transcendentals=130_000
        ),
        name="attention_fwd",
    )(place, *source, params, *w_qkv, *w_proj)


def experts_forward(section, place, *refs):
    x_ref, *refs = refs
    parts, refs = refs[:4], refs[4:]
    params, columns, in_own, in_other, out_own, out_other, *refs = refs
    mix_ref, *refs = refs
    saved, (stay_out, send_out), refs = refs[:6], refs[6:8], refs[8:]
    held, refs = refs[:6], refs[6:]
    w_in, w_out, kept, table, in_sem, out_sem, save_sems, keep_sem = refs
    saver = Kept(saved, held, save_sems)
    halves = Halves(place[2], kept, stay_out, send_out, keep_sem)
    use_own = place[2] == section
    loads_in = []
    loads_out = []
    for e in range(E):
        loads_in.append(
            Picked(in_own.at[e], in_other.at[e], use_own, w_in.at[e], in_sem.at[e])
        )
        loads_out.append(
            Picked(out_own.at[e], out_other.at[e], use_own, w_out.at[e], out_sem.at[e])
        )
    for e in range(E):
        loads_in[e].start()
        loads_out[e].start()
    router = jnp.concatenate([params[...], jnp.zeros((LANES - 16, D), f32)], axis=0)
    router_high = router.astype(bf16)
    router_low = (router - router_high.astype(f32)).astype(bf16)
    lane = lax.broadcasted_iota(jnp.int32, (1, LANES), 1)
    expert_lane = (lane >= ROUTER_AT) & (lane < ROUTER_AT + E)
    hidden = x_ref[...].astype(f32) + add_four(parts)
    saver.put(0, hidden)
    normed, _ = unit_norm(hidden)
    n2 = normed * params[2:3] + params[3:4]
    high = n2.astype(bf16)
    low = (n2 - high.astype(f32)).astype(bf16)
    saver.put(1, high)
    slots = params[SLOTS_AT : SLOTS_AT + 2, :ROWS].astype(jnp.int32)
    spread = (slot_rows(slots[0:1]) + slot_rows(slots[1:2])).astype(bf16)
    rows = dot(spread, high).astype(bf16)
    for e in range(E):
        halves.put(0, e, rows[e * SLOTS : (e + 1) * SLOTS])
    logits = dot_nt(high, router_high) + (dot_nt(low, router_high) + dot_nt(high, router_low))
    logits = jnp.where(expert_lane, logits, -1e30)
    raised = jnp.exp(logits - jnp.max(logits, axis=-1, keepdims=True))
    prob = raised / jnp.sum(raised, axis=-1, keepdims=True)
    saver.put(2, prob)
    curve = math.sqrt(2.0 / math.pi)
    for e in range(E):
        loads_in[e].wait()
        z = dot(kept[0, e], w_in[e])
        square = z * z
        bend = jnp.tanh(curve * z * (1.0 + 0.044715 * square))
        half = 0.5 * (1.0 + bend)
        active = (z * half).astype(bf16)
        halves.put(1, e, active)
        slope = half + (0.5 * curve) * z * (1.0 - bend * bend) * (1.0 + 0.134145 * square)
        saver.put(5, slope.astype(bf16), e)
        loads_out[e].wait()
        table[e * SLOTS : (e + 1) * SLOTS] = dot(active, w_out[e]).astype(bf16)
    mix = jnp.zeros((ROWS, D), f32)
    for k in range(2):
        gate = gate_of(prob, columns[:, k : k + 1])
        picked = dot(slot_columns(columns[:, 2 + k : 3 + k]).astype(bf16), table[...])
        saver.put(3 + k, picked.astype(bf16))
        mix = mix + gate * picked
    mix_ref[...] = mix.astype(bf16)
    saver.wait()
    halves.wait()


def run_experts_forward(section, place, x, parts, params, columns, w_in, w_out):
    saved = [
        ((ROWS, D), f32),
        ((ROWS, D), bf16),
        ((ROWS, LANES), f32),
        ((ROWS, D), bf16),
        ((ROWS, D), bf16),
        ((E, SLOTS, D), bf16),
    ]
    return pl.pallas_call(
        functools.partial(experts_forward, section),
        out_shape=[jax.ShapeDtypeStruct((ROWS, D), bf16)]
        + [jax.ShapeDtypeStruct(*kind) for kind in saved]
        + [jax.ShapeDtypeStruct((2, E // 2, SLOTS, D), bf16)] * 2,
        in_specs=[SMEM] + [VMEM] * 7 + [HBM] * 4,
        out_specs=[VMEM] + [HBM] * 8,
        scratch_shapes=[pltpu.VMEM(*kind) for kind in saved]
        + [
            pltpu.VMEM((E, D, D), bf16),
            pltpu.VMEM((E, D, D), bf16),
            pltpu.VMEM((2, E, SLOTS, D), bf16),
            pltpu.VMEM((TABLE, D), bf16),
            DMA((E,)),
            DMA((E,)),
            DMA((5 + E,)),
            DMA((2, E)),
        ],
        compiler_params=pltpu.CompilerParams(vmem_limit_bytes=LIMIT),
        cost_estimate=pl.CostEstimate(
            flops=4_000_000_000, bytes_accessed=16_000_000, transcendentals=400_000
        ),
        name="experts_fwd",
    )(place, x, *parts, params, columns, *w_in, *w_out)


def experts_backward(section, place, *refs):
    if section == 0:
        parts, refs = refs[:4], refs[4:]
        grad_hidden, x_ref, later, *refs = refs
    else:
        grad_ref, *refs = refs
    prob_ref, y0_ref, y1_ref, params, columns, slope_in, *refs = refs
    in_own, in_other, out_own, out_other, partial_ref, stay_out, send_out, *refs = refs
    if section == 0:
        passed_ref, *refs = refs
    w_in, w_out, slopes, kept, table, in_sem, out_sem, slope_sem, keep_sem = refs
    halves = Halves(place[2], kept, stay_out, send_out, keep_sem)
    use_own = place[2] == section
    loads = []
    for e in range(E):
        loads.append(
            (
                Picked(out_own.at[e], out_other.at[e], use_own, w_out.at[e], out_sem.at[e]),
                pltpu.make_async_copy(slope_in.at[e], slopes.at[e], slope_sem.at[e]),
                Picked(in_own.at[e], in_other.at[e], use_own, w_in.at[e], in_sem.at[e]),
            )
        )
        for copy in loads[e]:
            copy.start()
    if section == 0:
        unit, inverse = unit_norm(x_ref[...].astype(f32))
        passed = norm_back(add_four(parts), unit, inverse, later[0:1])
        passed = (grad_hidden[...] + passed).astype(bf16)
        passed_ref[...] = passed
        upstream = passed.astype(f32)
    else:
        upstream = grad_ref[...].astype(f32)
    lane = lax.broadcasted_iota(jnp.int32, (ROWS, LANES), 1)
    slots = params[SLOTS_AT : SLOTS_AT + 2, :ROWS].astype(jnp.int32)
    prob = prob_ref[...]
    rows = jnp.zeros((TABLE, D), f32)
    for k in range(2):
        gate = gate_of(prob, columns[:, k : k + 1])
        weighted = (gate * upstream).astype(bf16)
        rows = rows + dot(slot_rows(slots[k : k + 1]).astype(bf16), weighted)
    rows = rows.astype(bf16)
    for e in range(E):
        halves.put(0, e, rows[e * SLOTS : (e + 1) * SLOTS])
    for e in range(E):
        loads[e][0].wait()
        grad_active = dot_nt(kept[0, e], w_out[e])
        loads[e][1].wait()
        grad_pre = (grad_active * slopes[e].astype(f32)).astype(bf16)
        halves.put(1, e, grad_pre)
        loads[e][2].wait()
        table[e * SLOTS : (e + 1) * SLOTS] = dot_nt(grad_pre, w_in[e]).astype(bf16)
    packed = jnp.zeros((ROWS, LANES), f32)
    for k, picked in enumerate((y0_ref, y1_ref)):
        inner = jnp.sum(upstream * picked[...].astype(f32), axis=-1, keepdims=True)
        high = inner.astype(bf16).astype(f32)
        packed = packed + jnp.where(lane == k, high, 0.0)
        packed = packed + jnp.where(lane == 2 + k, inner - high, 0.0)
    longer = jnp.concatenate([packed, jnp.zeros((D - ROWS, LANES), f32)], axis=0).astype(bf16)
    tail = dot_nt(unit_rows(), longer)[: ROWS - SPARE]
    gather = slot_columns(columns[:, 2:3]) + slot_columns(columns[:, 3:4])
    spread = dot(gather.astype(bf16), table[...])
    partial_ref[...] = jnp.concatenate([spread[:SPARE], tail], axis=0).astype(bf16)
    halves.wait()


def run_experts_backward(
    section, place, grad, prob, y0, y1, params, columns, slope, w_in, w_out
):
    outs = [
        jax.ShapeDtypeStruct((ROWS, D), bf16),
        jax.ShapeDtypeStruct((2, E // 2, SLOTS, D), bf16),
        jax.ShapeDtypeStruct((2, E // 2, SLOTS, D), bf16),
    ]
    if section == 0:
        outs.append(jax.ShapeDtypeStruct((ROWS, D), bf16))
    return pl.pallas_call(
        functools.partial(experts_backward, section),
        out_shape=outs,
        in_specs=[SMEM] + [VMEM] * (len(grad) + 5) + [HBM] * 5,
        out_specs=[VMEM, HBM, HBM] + [VMEM] * (len(outs) - 3),
        scratch_shapes=[
            pltpu.VMEM((E, D, D), bf16),
            pltpu.VMEM((E, D, D), bf16),
            pltpu.VMEM((E, SLOTS, D), bf16),
            pltpu.VMEM((2, E, SLOTS, D), bf16),
            pltpu.VMEM((TABLE, D), bf16),
            DMA((E,)),
            DMA((E,)),
            DMA((E,)),
            DMA((2, E)),
        ],
        compiler_params=pltpu.CompilerParams(vmem_limit_bytes=LIMIT),
        cost_estimate=pl.CostEstimate(
            flops=4_000_000_000, bytes_accessed=16_000_000, transcendentals=0
        ),
        name="experts_bwd",
    )(place, *grad, prob, y0, y1, params, columns, slope, *w_in, *w_out)


def attention_backward(
    section,
    place,
    grad_ref,
    p0,
    p1,
    p2,
    p3,
    hidden,
    prob_ref,
    params,
    column,
    weights_ref,
    qkv_ref,
    x_ref,
    qkv_own,
    qkv_other,
    proj_own,
    proj_other,
    part,
    grad_hidden_ref,
    branch_ref,
    triple_ref,
    logit_ref,
    rows_ref,
    w_qkv,
    w_proj,
    sems,
):
    use_own = place[2] == section
    load_qkv = Picked(qkv_own, qkv_other, use_own, w_qkv, sems.at[0])
    load_proj = Picked(proj_own, proj_other, use_own, w_proj, sems.at[1])
    load_proj.start()
    load_qkv.start()
    parts = (p0, p1, p2, p3)
    router = jnp.concatenate([params[...], jnp.zeros((LANES - 16, D), f32)], axis=0)
    upstream = grad_ref[...].astype(f32)
    lane = lax.broadcasted_iota(jnp.int32, (ROWS, LANES), 1)
    arrived = add_four(parts)
    tail = arrived[SPARE:]
    tail_high = tail.astype(bf16)
    tail_low = (tail - tail_high.astype(f32)).astype(bf16)
    tails = jnp.concatenate([tail_high.astype(f32), tail_low.astype(f32)], axis=0).astype(bf16)
    pick = lax.broadcasted_iota(jnp.int32, (16, LANES), 0) % (ROWS - SPARE) == (
        lax.broadcasted_iota(jnp.int32, (16, LANES), 1)
    )
    inner = dot_tn(tails, jnp.where(pick, 1.0, 0.0).astype(bf16))[:ROWS]
    token = lax.broadcasted_iota(jnp.int32, (ROWS, 1), 0)
    arrived = jnp.where(token < SPARE, arrived, 0.0)
    prob = prob_ref[...]
    grad_prob = jnp.zeros((ROWS, LANES), f32)
    for k in range(2):
        mine = (lane == k) | (lane == 2 + k)
        value = jnp.sum(jnp.where(mine, inner, 0.0), axis=-1, keepdims=True)
        grad_prob = grad_prob + jnp.where(expert_lanes(column[:, k : k + 1]), value, 0.0)
    grad_logit = prob * (grad_prob - jnp.sum(prob * grad_prob, axis=-1, keepdims=True))
    grad_logit = grad_logit.astype(bf16)
    logit_ref[...] = grad_logit
    grad_n2 = arrived + dot(grad_logit, router.astype(bf16))
    unit2, inverse2 = unit_norm(hidden[...])
    grad_hidden = upstream + norm_back(grad_n2, unit2, inverse2, params[2:3])
    grad_hidden_ref[...] = grad_hidden
    gain_row = jnp.sum(grad_n2 * unit2, axis=0, keepdims=True)
    bias_row = jnp.sum(grad_n2, axis=0, keepdims=True)
    branch = grad_hidden.astype(bf16)
    branch_ref[...] = branch
    load_proj.wait()
    grad_attended = dot_nt(branch, w_proj[...]).astype(bf16)
    query, key, value = (qkv_ref[j] for j in range(3))
    grad_query = jnp.zeros((ROWS, LOCAL), f32)
    grad_key = jnp.zeros((ROWS, LOCAL), f32)
    grad_value = jnp.zeros((ROWS, LOCAL), f32)
    for head in range(LOCAL // HD):
        mask = head_mask(head)
        weights = weights_ref[head]
        wide = weights.astype(f32)
        arriving = grad_attended * mask
        grad_weights = dot_nt(arriving, value)
        grad_scores = wide * (
            grad_weights - jnp.sum(wide * grad_weights, axis=-1, keepdims=True)
        )
        grad_scores = grad_scores.astype(bf16)
        grad_value = grad_value + dot_tn(weights, arriving)
        grad_query = grad_query + dot(grad_scores, key * mask)
        grad_key = grad_key + dot_tn(grad_scores, query * mask)
    scaling = 1.0 / math.sqrt(HD)
    load_qkv.wait()
    grad_n1 = jnp.zeros((ROWS, D), f32)
    for j, grad in enumerate((grad_query * scaling, grad_key * scaling, grad_value)):
        narrow = grad.astype(bf16)
        triple_ref[j] = narrow
        grad_n1 = grad_n1 + dot(narrow, w_qkv[j])
    part[...] = grad_n1.astype(bf16)
    unit1, _ = unit_norm(x_ref[...].astype(f32))
    first_gain = jnp.sum(grad_n1 * unit1, axis=0, keepdims=True)
    first_bias = jnp.sum(grad_n1, axis=0, keepdims=True)
    ends = [first_gain, first_bias, gain_row, bias_row, jnp.zeros((12, D), f32)]
    rows_ref[...] = jnp.concatenate(ends, axis=0).astype(bf16)


def run_attention_backward(section, place, *operands):
    saved = [(ROWS, D), (3, ROWS, LOCAL), (ROWS, LANES), (16, D)]
    return pl.pallas_call(
        functools.partial(attention_backward, section),
        out_shape=[
            jax.ShapeDtypeStruct((ROWS, D), bf16),
            jax.ShapeDtypeStruct((ROWS, D), f32),
        ]
        + [jax.ShapeDtypeStruct(shape, bf16) for shape in saved],
        in_specs=[SMEM] + [VMEM] * 12 + [HBM] * 4,
        out_specs=[VMEM] * 6,
        scratch_shapes=[
            pltpu.VMEM((3, LOCAL, D), bf16),
            pltpu.VMEM((LOCAL, D), bf16),
            DMA((2,)),
        ],
        compiler_params=pltpu.CompilerParams(vmem_limit_bytes=SHORT),
        cost_estimate=pl.CostEstimate(
            flops=1_000_000_000, bytes_accessed=6_000_000, transcendentals=0
        ),
        name="attention_bwd",
    )(place, *operands)


def source_backward(p0, p1, p2, p3, grad_hidden, x_ref, params, out):
    unit, inverse = unit_norm(x_ref[...].astype(f32))
    passed = norm_back(add_four((p0, p1, p2, p3)), unit, inverse, params[0:1])
    out[...] = (grad_hidden[...] + passed).astype(bf16)


def run_source_backward(parts, grad_hidden, x, params):
    return pl.pallas_call(
        source_backward,
        out_shape=jax.ShapeDtypeStruct((ROWS, D), bf16),
        in_specs=[VMEM] * 7,
        out_specs=VMEM,
        compiler_params=pltpu.CompilerParams(vmem_limit_bytes=SHORT),
        cost_estimate=pl.CostEstimate(
            flops=6_000_000, bytes_accessed=3_000_000, transcendentals=0
        ),
        name="source_bwd",
    )(*parts, grad_hidden, x, params)


def expert_pair(stay, arrived, stay_later, arrived_later, e):
    def both(mine, other, j):
        return jnp.concatenate([mine[j, e], other[j, e]], axis=0)

    buffer, active = (both(stay, arrived, j) for j in range(2))
    slot_grad, grad_pre = (both(stay_later, arrived_later, j) for j in range(2))
    return dot_tn(buffer, grad_pre).astype(bf16), dot_tn(slot_grad, active).astype(bf16)


def attention_pieces(n1, triple, branch, attended):
    pieces = [dot_tn(n1[...], triple[j]) for j in range(3)]
    pieces.append(dot_tn(branch[...], attended[...]))
    return jnp.concatenate(pieces, axis=1).astype(bf16)


def small_grads(n2, logit, rows):
    return (dot_tn(n2[...], logit[...]) + dot_tn(rows[...], unit_rows())).astype(bf16)


def second_expert_grads(*refs):
    experts, out = refs[:4], refs[4]
    for e in range(E // 2):
        for m, grad in enumerate(expert_pair(*experts, e)):
            for j in range(16):
                out[j, 2 * e + m] = grad[j * 48 : (j + 1) * 48]


def run_second_expert_grads(*operands):
    return pl.pallas_call(
        second_expert_grads,
        out_shape=jax.ShapeDtypeStruct((16, E, 48, D), bf16),
        in_specs=[VMEM] * 4,
        out_specs=VMEM,
        compiler_params=pltpu.CompilerParams(vmem_limit_bytes=SHORT),
        cost_estimate=pl.CostEstimate(
            flops=1_100_000_000, bytes_accessed=8_000_000, transcendentals=0
        ),
        name="second_expert_grads",
    )(*operands)


def first_expert_grads(place, *refs):
    experts, (by_x, by_z), (scr_x, scr_z) = refs[:4], (refs[4:8], refs[8:12]), refs[12:]
    for e in range(E // 2):
        grad_in, grad_out = expert_pair(*experts, e)
        for z in range(4):
            for x in range(4):
                at = (4 * z + x) * 48
                scr_x[x, e, z] = grad_in[at : at + 48]
                scr_z[z, e, x] = grad_out[at : at + 48]
    for k in range(4):
        by_x[k][...] = scr_x[lax.rem(place[1] + k, 4)]
        by_z[k][...] = scr_z[lax.rem(place[0] + k, 4)]


def run_first_expert_grads(place, *operands):
    result = pl.pallas_call(
        first_expert_grads,
        out_shape=[jax.ShapeDtypeStruct((E // 2, 4, 48, D), bf16)] * 8,
        in_specs=[SMEM] + [VMEM] * 4,
        out_specs=[VMEM] * 8,
        scratch_shapes=[pltpu.VMEM((4, E // 2, 4, 48, D), bf16)] * 2,
        compiler_params=pltpu.CompilerParams(vmem_limit_bytes=SHORT),
        cost_estimate=pl.CostEstimate(
            flops=1_100_000_000, bytes_accessed=8_000_000, transcendentals=0
        ),
        name="first_expert_grads",
    )(place, *operands)
    return result[:4], result[4:]


def expert_middle(place, *refs):
    ins, outs, scr = (refs[:4], refs[4:8]), (refs[8:12], refs[12:16]), refs[16]
    for group in range(2):
        a, b, c, d = (ref[...].astype(f32) for ref in ins[group])
        scr[...] = ((a + b) + (c + d)).astype(bf16)
        for k in range(4):
            for e in range(E // 2):
                outs[group][k][e] = scr[e, lax.rem(place[group] + k, 4)]


def run_expert_middle(place, by_x, by_z):
    result = pl.pallas_call(
        expert_middle,
        out_shape=[jax.ShapeDtypeStruct((E // 2, 48, D), bf16)] * 8,
        in_specs=[SMEM] + [VMEM] * 8,
        out_specs=[VMEM] * 8,
        scratch_shapes=[pltpu.VMEM((E // 2, 4, 48, D), bf16)],
        compiler_params=pltpu.CompilerParams(vmem_limit_bytes=SHORT),
        cost_estimate=pl.CostEstimate(
            flops=6_000_000, bytes_accessed=7_000_000, transcendentals=0
        ),
        name="expert_middle",
    )(place, *by_x, *by_z)
    return result[:4], result[4:]


def attention_grads(section, place, *refs):
    attention, small, refs = refs[:4], refs[4:7], refs[7:]
    wide = jnp.concatenate([attention_pieces(*attention), small_grads(*small)], axis=1)
    if section == 1:
        refs[0][...] = wide
    else:
        other, mine, send = refs
        leading = place[2] == 0
        mine[...] = jnp.where(leading, wide, other[...])
        send[...] = jnp.where(leading, other[...], wide)


def run_attention_grads(section, place, *operands):
    outs = 1 if section == 1 else 2
    return pl.pallas_call(
        functools.partial(attention_grads, section),
        out_shape=[jax.ShapeDtypeStruct((D, WIDE), bf16)] * outs,
        in_specs=[SMEM] + [VMEM] * len(operands),
        out_specs=[VMEM] * outs,
        compiler_params=pltpu.CompilerParams(vmem_limit_bytes=SHORT),
        cost_estimate=pl.CostEstimate(
            flops=400_000_000, bytes_accessed=4_000_000, transcendentals=0
        ),
        name="attention_grads",
    )(place, *operands)


def between_heads(x):
    received = [
        lax.ppermute(x, "tensor", [(i, (i + k) % 4) for i in range(4)]) for k in range(1, 4)
    ]
    return [x] + received


def swapped(x):
    return lax.ppermute(x, "pipe", [(0, 1), (1, 0)])


def scattered(xs, along_z):
    received = []
    for k in range(1, 4):
        pairs = []
        for z in range(4):
            for x in range(4):
                if along_z:
                    target = ((z + k) % 4) * 4 + x
                else:
                    target = z * 4 + (x + k) % 4
                pairs.append((z * 4 + x, target))
        received.append(lax.ppermute(xs[k], "dp", pairs))
    return [xs[0]] + received


def add_up(xs):
    a, b, c, d = (x.astype(f32) for x in xs)
    return (a + b) + (c + d)


def on_device(
    inputs,
    out_grad,
    routes,
    positions,
    norm1_gain,
    norm1_bias,
    qkv_weight,
    proj_weight,
    norm2_gain,
    norm2_bias,
    router_weight,
    expert_in,
    expert_out,
):
    core = lax.axis_index("pipe")
    leading = core == 0
    at = lax.axis_index("dp")
    place = jnp.stack([at // 4, at % 4, core]).astype(jnp.int32)

    def own_image(x):
        x = lax.dynamic_index_in_dim(x, core, 0, keepdims=False)
        return jnp.pad(x.reshape(SEQ, D), ((0, ROWS - SEQ), (0, 0)))

    own_qkv = qkv_weight[0].transpose(0, 2, 1)
    w_qkv = (own_qkv, swapped(own_qkv))
    w_proj = (proj_weight[0], swapped(proj_weight[0]))
    route = routes[0].reshape(2, SEQ, 2)
    slot = route * SLOTS + positions[0].reshape(2, SEQ, 2)
    lines = jnp.concatenate([route, slot], axis=-1).transpose(0, 2, 1)
    lines = jnp.pad(lines, ((0, 0), (0, 0), (0, ROWS - SEQ)), constant_values=-64)
    lines = jnp.pad(lines.astype(f32), ((0, 0), (0, 0), (0, D - ROWS)))
    vectors = [norm1_gain, norm1_bias, norm2_gain, norm2_bias, router_weight[0].T]
    rest = jnp.zeros((4, D), f32)

    def packed(image):
        return jnp.concatenate(vectors + [lines[image], rest])

    own = jnp.where(leading, packed(0), packed(1))
    other = swapped(jnp.where(leading, packed(1), packed(0)))
    params = [jnp.where(leading, own, other), jnp.where(leading, other, own)]
    columns = [p[ROUTES_AT : ROUTES_AT + 4, :ROWS].T.astype(jnp.int32) for p in params]
    wait_for = (w_qkv[1], w_proj[1], other)
    own_in, own_out, *_ = lax.optimization_barrier((expert_in[0], expert_out[0], *wait_for))
    w_in = (expert_in[0], swapped(own_in))
    w_out = (expert_out[0], swapped(own_out))

    def forward(section, source, x):
        part, n1, triple, weights, attended, *more = run_attention_forward(
            section, place, source, params[section], w_qkv, w_proj
        )
        x = more[0] if more else x
        mix, hidden, n2, prob, y0, y1, slope, stay, send = run_experts_forward(
            section, place, x, between_heads(part), params[section], columns[section], w_in, w_out
        )
        stored = (x, n1, triple, weights, attended, hidden, n2, prob, y0, y1, slope)
        return hidden, between_heads(mix), [stay, swapped(send)], stored

    def backward(section, upstream, stored, expert_operands, later_narrow):
        x, n1, triple, weights, attended, hidden, n2, prob, y0, y1, slope = stored
        partial, stay, send, *more = run_experts_backward(
            section,
            place,
            upstream,
            prob,
            y0,
            y1,
            params[section],
            columns[section],
            slope,
            w_in,
            w_out,
        )
        grad = more[0] if more else upstream[0]
        parts = between_heads(partial)
        expert_operands = expert_operands + [stay, swapped(send)]
        expert_operands[0], parts[1] = lax.optimization_barrier((expert_operands[0], parts[1]))
        if section == 0:
            grads = run_first_expert_grads(place, *expert_operands)
        else:
            grads = run_second_expert_grads(*expert_operands)
        grad, grads = lax.optimization_barrier((grad, grads))
        part, grad_hidden, branch, grad_triple, logit, rows = run_attention_backward(
            section,
            place,
            grad,
            *parts,
            hidden,
            prob,
            params[section],
            columns[section],
            weights,
            triple,
            x,
            *w_qkv,
            *w_proj,
        )
        narrow = run_attention_grads(
            section, place, n1, grad_triple, branch, attended, n2, logit, rows, *later_narrow
        )
        return grad, between_heads(part), grad_hidden, grads, narrow

    source = own_image(inputs)
    hidden, mixes, first_operands, stored_first = forward(0, [source], source)
    hidden, mixes, second_operands, stored_second = forward(1, [hidden] + mixes, None)
    middle = stored_second[0]
    last = (hidden + add_up(mixes)).astype(bf16)
    _, parts, grad_hidden, second, narrow = backward(
        1, [own_image(out_grad)], stored_second, second_operands, []
    )
    second = lax.psum_scatter(second, "dp", scatter_dimension=0, tiled=True)[0]
    second = lax.optimization_barrier(second)
    passed, parts, grad_hidden, (by_x, by_z), (mine, send) = backward(
        0, parts + [grad_hidden, middle, params[1]], stored_first, first_operands, narrow
    )
    narrow = (mine.astype(f32) + swapped(send).astype(f32)).astype(bf16)
    narrow = lax.all_to_all(narrow.reshape(16, 48, WIDE), "dp", 0, 0, tiled=True)
    small = jnp.sum(narrow.astype(f32), axis=0)
    norm1 = add_up(between_heads(small[:, D : D + 2].astype(bf16)))
    by_x, by_z = run_expert_middle(place, scattered(by_x, False), scattered(by_z, True))
    first_in = add_up(scattered(by_x, True))
    first_out = add_up(scattered(by_z, False))
    entering = run_source_backward(parts, grad_hidden, source, params[0])

    def exchange(first, second):
        mine = jnp.where(leading, first, second)
        return mine, swapped(jnp.where(leading, second, first))

    mine, arrived = exchange(
        jnp.stack([first_in, first_out], axis=1).astype(bf16),
        second.reshape(E // 2, 2, 48, D),
    )
    experts = jnp.where(
        leading, jnp.concatenate([mine, arrived]), jnp.concatenate([arrived, mine])
    ).astype(f32)
    def both_images(first, second):
        mine = jnp.where(leading, first, second)[:SEQ]
        arrived = swapped(jnp.where(leading, second, first))[:SEQ]
        images = jnp.where(leading, jnp.stack([mine, arrived]), jnp.stack([arrived, mine]))
        return images.reshape(1, 2, 1, SEQ, D)

    return (
        both_images(middle, last),
        both_images(entering, passed),
        norm1[:, 0][None],
        norm1[:, 1][None],
        small[:, : 3 * LOCAL].reshape(48, 3, LOCAL).transpose(1, 0, 2)[None],
        small[:, 3 * LOCAL : D].T[None],
        small[:, D + 2][None],
        small[:, D + 3][None],
        small[:, D + ROUTER_AT : D + ROUTER_AT + E][None],
        experts[:, 0][None],
        experts[:, 1].transpose(0, 2, 1)[None],
    )


def solution(mesh):
    in_specs = (
        P(None, "dp", None, None),
        P(None, "dp", None, None),
        P("pipe", None, "dp", None, None),
        P("pipe", None, "dp", None, None),
        P("pipe", None),
        P("pipe", None),
        P("pipe", None, None, "tensor"),
        P("pipe", "tensor", None),
        P("pipe", None),
        P("pipe", None),
        P("pipe", None, None),
        P("pipe", None, None, "tensor"),
        P("pipe", None, "tensor", None),
    )
    out_specs = (
        P("pipe", None, "dp", None, None),
        P("pipe", None, "dp", None, None),
        P("pipe", "dp"),
        P("pipe", "dp"),
        P("pipe", None, "dp", "tensor"),
        P("pipe", "tensor", "dp"),
        P("pipe", "dp"),
        P("pipe", "dp"),
        P("pipe", "dp", None),
        P("pipe", None, "dp", "tensor"),
        P("pipe", None, "tensor", "dp"),
    )
    return jax.shard_map(
        on_device, mesh=mesh, in_specs=in_specs, out_specs=out_specs, check_vma=False
    )
```

```python
import functools
import math

import jax
import jax.numpy as jnp
from jax import lax
from jax.experimental import pallas as pl
from jax.experimental.pallas import tpu as pltpu
from jax.sharding import PartitionSpec as P

HD = 64
E = 4
SEQ = 197
CAP = 111
ROWS = 208
SLOTS = 112
TABLE = E * SLOTS
D = 768
LOCAL = 192
LANES = 128
WIDE = D + LANES
SPARE = 200
ROUTER_AT = 4
ROUTES_AT = 8
SLOTS_AT = 10

f32 = jnp.float32
bf16 = jnp.bfloat16
eps = 1e-06
VMEM = pl.BlockSpec(memory_space=pltpu.VMEM)
SMEM = pl.BlockSpec(memory_space=pltpu.SMEM)
HBM = pl.BlockSpec(memory_space=pl.ANY)
DMA = pltpu.SemaphoreType.DMA
LIMIT = 60 * 1024 * 1024
SHORT = 28 * 1024 * 1024


def dot(a, b):
    return lax.dot_general(a, b, (((1,), (0,)), ((), ())), preferred_element_type=f32)


def dot_nt(a, b):
    return lax.dot_general(a, b, (((1,), (1,)), ((), ())), preferred_element_type=f32)


def dot_tn(a, b):
    return lax.dot_general(a, b, (((0,), (0,)), ((), ())), preferred_element_type=f32)


def unit_norm(v):
    centred = v - jnp.mean(v, axis=-1, keepdims=True)
    inverse = lax.rsqrt(jnp.mean(centred * centred, axis=-1, keepdims=True) + eps)
    return centred * inverse, inverse


def norm_back(upstream, normed, inverse, gain):
    scaled = upstream * gain
    inner = jnp.mean(scaled * normed, axis=-1, keepdims=True)
    return inverse * (scaled - jnp.mean(scaled, axis=-1, keepdims=True) - normed * inner)


def head_mask(head):
    lane = lax.broadcasted_iota(jnp.int32, (1, LOCAL), 1)
    inside = (lane >= head * HD) & (lane < (head + 1) * HD)
    return jnp.where(inside, 1.0, 0.0).astype(bf16)


def slot_rows(row_ids):
    ids = lax.broadcasted_iota(jnp.int32, (TABLE, ROWS), 0)
    return jnp.where(ids == row_ids, 1.0, 0.0)


def slot_columns(column_ids):
    ids = lax.broadcasted_iota(jnp.int32, (ROWS, TABLE), 1)
    return jnp.where(ids == column_ids, 1.0, 0.0)


def expert_lanes(route):
    lane = lax.broadcasted_iota(jnp.int32, (ROWS, LANES), 1)
    return lane == route + ROUTER_AT


def gate_of(prob, route):
    return jnp.sum(jnp.where(expert_lanes(route), prob, 0.0), axis=-1, keepdims=True)


class Picked:
    def __init__(self, own, other, use_own, held, sem):
        self.copies = [pltpu.make_async_copy(ref, held, sem) for ref in (own, other)]
        self.use_own = use_own

    def start(self):
        pl.when(self.use_own)(self.copies[0].start)
        pl.when(jnp.logical_not(self.use_own))(self.copies[1].start)

    def wait(self):
        self.copies[0].wait()


class Operands:
    def __init__(self, held, out, sems):
        self.held, self.out, self.sems = held, out, sems
        self.copies = []

    def put(self, j, e, value):
        self.held[j, e] = value
        copy = pltpu.make_async_copy(self.held.at[j, e], self.out.at[j, e], self.sems.at[j, e])
        copy.start()
        self.copies.append(copy)

    def wait(self):
        for copy in self.copies:
            copy.wait()


class Kept:
    def __init__(self, outs, held, sems):
        self.outs, self.held, self.sems = outs, held, sems
        self.copies = []

    def put(self, at, value, index=None):
        held, out = self.held[at], self.outs[at]
        if index is not None:
            held, out = held.at[index], out.at[index]
        held[...] = value
        copy = pltpu.make_async_copy(held, out, self.sems.at[len(self.copies)])
        copy.start()
        self.copies.append(copy)

    def wait(self):
        for copy in self.copies:
            copy.wait()


def unit_rows():
    row = lax.broadcasted_iota(jnp.int32, (16, LANES), 0)
    lane = lax.broadcasted_iota(jnp.int32, (16, LANES), 1)
    return jnp.where(row == lane, 1.0, 0.0).astype(bf16)


def add_four(refs):
    a, b, c, d = (ref[...].astype(f32) for ref in refs)
    return (a + b) + (c + d)


def attention_forward(section, place, *refs):
    summed = section == 1
    if summed:
        hidden, *refs = refs
        parts, refs = refs[:4], refs[4:]
    else:
        x_ref, *refs = refs
    params, qkv_own, qkv_other, proj_own, proj_other, *refs = refs
    part, refs = refs[0], refs[1:]
    saved, refs = refs[:4], refs[4:]
    *more, w_qkv, w_proj, sems, held_n1, held_qkv, held_p, held_o, save_sems = refs
    kept = Kept(saved, (held_n1, held_qkv, held_p, held_o), save_sems)
    use_own = place[2] == section
    load_qkv = Picked(qkv_own, qkv_other, use_own, w_qkv, sems.at[0])
    load_proj = Picked(proj_own, proj_other, use_own, w_proj, sems.at[1])
    load_qkv.start()
    load_proj.start()
    if summed:
        source = (hidden[...] + add_four(parts)).astype(bf16)
        more[0][...] = source
    else:
        source = x_ref[...]
    normed, _ = unit_norm(source.astype(f32))
    n1 = (normed * params[0:1] + params[1:2]).astype(bf16)
    kept.put(0, n1)
    load_qkv.wait()
    query, key, value = (dot_nt(n1, w_qkv[j]).astype(bf16) for j in range(3))
    for j, piece in enumerate((query, key, value)):
        kept.put(1, piece, j)
    real = lax.broadcasted_iota(jnp.int32, (1, ROWS), 1) < SEQ
    attended = jnp.zeros((ROWS, LOCAL), f32)
    for head in range(LOCAL // HD):
        mask = head_mask(head)
        scores = dot_nt(query * mask, key) * (1.0 / math.sqrt(HD))
        scores = jnp.where(real, scores, -1e30)
        shifted = jnp.exp(scores - jnp.max(scores, axis=-1, keepdims=True))
        weights = (shifted / jnp.sum(shifted, axis=-1, keepdims=True)).astype(bf16)
        kept.put(2, weights, head)
        attended = attended + dot(weights, value * mask)
    attended = attended.astype(bf16)
    kept.put(3, attended)
    load_proj.wait()
    part[...] = dot(attended, w_proj[...]).astype(bf16)
    kept.wait()


def run_attention_forward(section, place, source, params, w_qkv, w_proj):
    saved = [(ROWS, D), (3, ROWS, LOCAL), (3, ROWS, ROWS), (ROWS, LOCAL)]
    outs = [jax.ShapeDtypeStruct((ROWS, D), bf16)]
    outs += [jax.ShapeDtypeStruct(shape, bf16) for shape in saved]
    if section == 1:
        outs.append(jax.ShapeDtypeStruct((ROWS, D), bf16))
    return pl.pallas_call(
        functools.partial(attention_forward, section),
        out_shape=outs,
        in_specs=[SMEM] + [VMEM] * (len(source) + 1) + [HBM] * 4,
        out_specs=[VMEM] + [HBM] * 4 + [VMEM] * (len(outs) - 5),
        scratch_shapes=[
            pltpu.VMEM((3, LOCAL, D), bf16),
            pltpu.VMEM((LOCAL, D), bf16),
            DMA((2,)),
        ]
        + [pltpu.VMEM(shape, bf16) for shape in saved]
        + [DMA((8,))],
        compiler_params=pltpu.CompilerParams(vmem_limit_bytes=LIMIT),
        cost_estimate=pl.CostEstimate(
            flops=600_000_000, bytes_accessed=4_000_000, transcendentals=130_000
        ),
        name="attention_fwd",
    )(place, *source, params, *w_qkv, *w_proj)


def experts_forward(section, place, *refs):
    x_ref, *refs = refs
    parts, refs = refs[:4], refs[4:]
    params, columns, in_own, in_other, out_own, out_other, *refs = refs
    mix_ref, *refs = refs
    saved, kept_out, refs = refs[:6], refs[6], refs[7:]
    held, refs = refs[:6], refs[6:]
    w_in, w_out, kept, table, in_sem, out_sem, save_sems, keep_sem = refs
    saver = Kept(saved, held, save_sems)
    operands = Operands(kept, kept_out, keep_sem)
    use_own = place[2] == section
    loads_in = []
    loads_out = []
    for e in range(E):
        loads_in.append(
            Picked(in_own.at[e], in_other.at[e], use_own, w_in.at[e], in_sem.at[e])
        )
        loads_out.append(
            Picked(out_own.at[e], out_other.at[e], use_own, w_out.at[e], out_sem.at[e])
        )
    for e in range(E):
        loads_in[e].start()
        loads_out[e].start()
    router = jnp.concatenate([params[...], jnp.zeros((LANES - 16, D), f32)], axis=0)
    router_high = router.astype(bf16)
    router_low = (router - router_high.astype(f32)).astype(bf16)
    lane = lax.broadcasted_iota(jnp.int32, (1, LANES), 1)
    expert_lane = (lane >= ROUTER_AT) & (lane < ROUTER_AT + E)
    hidden = x_ref[...].astype(f32) + add_four(parts)
    saver.put(0, hidden)
    normed, _ = unit_norm(hidden)
    n2 = normed * params[2:3] + params[3:4]
    high = n2.astype(bf16)
    low = (n2 - high.astype(f32)).astype(bf16)
    saver.put(1, high)
    slots = params[SLOTS_AT : SLOTS_AT + 2, :ROWS].astype(jnp.int32)
    spread = (slot_rows(slots[0:1]) + slot_rows(slots[1:2])).astype(bf16)
    rows = dot(spread, high).astype(bf16)
    for e in range(E):
        operands.put(0, e, rows[e * SLOTS : (e + 1) * SLOTS])
    logits = dot_nt(high, router_high) + (dot_nt(low, router_high) + dot_nt(high, router_low))
    logits = jnp.where(expert_lane, logits, -1e30)
    raised = jnp.exp(logits - jnp.max(logits, axis=-1, keepdims=True))
    prob = raised / jnp.sum(raised, axis=-1, keepdims=True)
    saver.put(2, prob)
    curve = math.sqrt(2.0 / math.pi)
    for e in range(E):
        loads_in[e].wait()
        z = dot(kept[0, e], w_in[e])
        square = z * z
        bend = jnp.tanh(curve * z * (1.0 + 0.044715 * square))
        half = 0.5 * (1.0 + bend)
        active = (z * half).astype(bf16)
        operands.put(1, e, active)
        slope = half + (0.5 * curve) * z * (1.0 - bend * bend) * (1.0 + 0.134145 * square)
        saver.put(5, slope.astype(bf16), e)
        loads_out[e].wait()
        table[e * SLOTS : (e + 1) * SLOTS] = dot(active, w_out[e]).astype(bf16)
    mix = jnp.zeros((ROWS, D), f32)
    for k in range(2):
        gate = gate_of(prob, columns[:, k : k + 1])
        picked = dot(slot_columns(columns[:, 2 + k : 3 + k]).astype(bf16), table[...])
        saver.put(3 + k, picked.astype(bf16))
        mix = mix + gate * picked
    mix_ref[...] = mix.astype(bf16)
    saver.wait()
    operands.wait()


def run_experts_forward(section, place, x, parts, params, columns, w_in, w_out):
    saved = [
        ((ROWS, D), f32),
        ((ROWS, D), bf16),
        ((ROWS, LANES), f32),
        ((ROWS, D), bf16),
        ((ROWS, D), bf16),
        ((E, SLOTS, D), bf16),
    ]
    return pl.pallas_call(
        functools.partial(experts_forward, section),
        out_shape=[jax.ShapeDtypeStruct((ROWS, D), bf16)]
        + [jax.ShapeDtypeStruct(*kind) for kind in saved]
        + [jax.ShapeDtypeStruct((2, E, SLOTS, D), bf16)],
        in_specs=[SMEM] + [VMEM] * 7 + [HBM] * 4,
        out_specs=[VMEM] + [HBM] * 7,
        scratch_shapes=[pltpu.VMEM(*kind) for kind in saved]
        + [
            pltpu.VMEM((E, D, D), bf16),
            pltpu.VMEM((E, D, D), bf16),
            pltpu.VMEM((2, E, SLOTS, D), bf16),
            pltpu.VMEM((TABLE, D), bf16),
            DMA((E,)),
            DMA((E,)),
            DMA((5 + E,)),
            DMA((2, E)),
        ],
        compiler_params=pltpu.CompilerParams(vmem_limit_bytes=LIMIT),
        cost_estimate=pl.CostEstimate(
            flops=4_000_000_000, bytes_accessed=16_000_000, transcendentals=400_000
        ),
        name="experts_fwd",
    )(place, x, *parts, params, columns, *w_in, *w_out)


def experts_backward(section, place, *refs):
    if section == 0:
        parts, refs = refs[:4], refs[4:]
        grad_hidden, x_ref, later, *refs = refs
    else:
        grad_ref, *refs = refs
    prob_ref, y0_ref, y1_ref, params, columns, slope_in, *refs = refs
    in_own, in_other, out_own, out_other, partial_ref, kept_out, *refs = refs
    if section == 0:
        passed_ref, *refs = refs
    w_in, w_out, slopes, kept, table, in_sem, out_sem, slope_sem, keep_sem = refs
    operands = Operands(kept, kept_out, keep_sem)
    use_own = place[2] == section
    loads = []
    for e in range(E):
        loads.append(
            (
                Picked(out_own.at[e], out_other.at[e], use_own, w_out.at[e], out_sem.at[e]),
                pltpu.make_async_copy(slope_in.at[e], slopes.at[e], slope_sem.at[e]),
                Picked(in_own.at[e], in_other.at[e], use_own, w_in.at[e], in_sem.at[e]),
            )
        )
        for copy in loads[e]:
            copy.start()
    if section == 0:
        unit, inverse = unit_norm(x_ref[...].astype(f32))
        passed = norm_back(add_four(parts), unit, inverse, later[0:1])
        passed = (grad_hidden[...] + passed).astype(bf16)
        passed_ref[...] = passed
        upstream = passed.astype(f32)
    else:
        upstream = grad_ref[...].astype(f32)
    lane = lax.broadcasted_iota(jnp.int32, (ROWS, LANES), 1)
    slots = params[SLOTS_AT : SLOTS_AT + 2, :ROWS].astype(jnp.int32)
    prob = prob_ref[...]
    rows = jnp.zeros((TABLE, D), f32)
    for k in range(2):
        gate = gate_of(prob, columns[:, k : k + 1])
        weighted = (gate * upstream).astype(bf16)
        rows = rows + dot(slot_rows(slots[k : k + 1]).astype(bf16), weighted)
    rows = rows.astype(bf16)
    for e in range(E):
        operands.put(0, e, rows[e * SLOTS : (e + 1) * SLOTS])
    for e in range(E):
        loads[e][0].wait()
        grad_active = dot_nt(kept[0, e], w_out[e])
        loads[e][1].wait()
        grad_pre = (grad_active * slopes[e].astype(f32)).astype(bf16)
        operands.put(1, e, grad_pre)
        loads[e][2].wait()
        table[e * SLOTS : (e + 1) * SLOTS] = dot_nt(grad_pre, w_in[e]).astype(bf16)
    packed = jnp.zeros((ROWS, LANES), f32)
    for k, picked in enumerate((y0_ref, y1_ref)):
        inner = jnp.sum(upstream * picked[...].astype(f32), axis=-1, keepdims=True)
        high = inner.astype(bf16).astype(f32)
        packed = packed + jnp.where(lane == k, high, 0.0)
        packed = packed + jnp.where(lane == 2 + k, inner - high, 0.0)
    longer = jnp.concatenate([packed, jnp.zeros((D - ROWS, LANES), f32)], axis=0).astype(bf16)
    tail = dot_nt(unit_rows(), longer)[: ROWS - SPARE]
    gather = slot_columns(columns[:, 2:3]) + slot_columns(columns[:, 3:4])
    spread = dot(gather.astype(bf16), table[...])
    partial_ref[...] = jnp.concatenate([spread[:SPARE], tail], axis=0).astype(bf16)
    operands.wait()


def run_experts_backward(
    section, place, grad, prob, y0, y1, params, columns, slope, w_in, w_out
):
    outs = [
        jax.ShapeDtypeStruct((ROWS, D), bf16),
        jax.ShapeDtypeStruct((2, E, SLOTS, D), bf16),
    ]
    if section == 0:
        outs.append(jax.ShapeDtypeStruct((ROWS, D), bf16))
    return pl.pallas_call(
        functools.partial(experts_backward, section),
        out_shape=outs,
        in_specs=[SMEM] + [VMEM] * (len(grad) + 5) + [HBM] * 5,
        out_specs=[VMEM, HBM] + [VMEM] * (len(outs) - 2),
        scratch_shapes=[
            pltpu.VMEM((E, D, D), bf16),
            pltpu.VMEM((E, D, D), bf16),
            pltpu.VMEM((E, SLOTS, D), bf16),
            pltpu.VMEM((2, E, SLOTS, D), bf16),
            pltpu.VMEM((TABLE, D), bf16),
            DMA((E,)),
            DMA((E,)),
            DMA((E,)),
            DMA((2, E)),
        ],
        compiler_params=pltpu.CompilerParams(vmem_limit_bytes=LIMIT),
        cost_estimate=pl.CostEstimate(
            flops=4_000_000_000, bytes_accessed=16_000_000, transcendentals=0
        ),
        name="experts_bwd",
    )(place, *grad, prob, y0, y1, params, columns, slope, *w_in, *w_out)


def attention_backward(
    section,
    place,
    grad_ref,
    p0,
    p1,
    p2,
    p3,
    hidden,
    prob_ref,
    params,
    column,
    weights_ref,
    qkv_ref,
    x_ref,
    qkv_own,
    qkv_other,
    proj_own,
    proj_other,
    part,
    grad_hidden_ref,
    branch_ref,
    triple_ref,
    logit_ref,
    rows_ref,
    w_qkv,
    w_proj,
    sems,
):
    use_own = place[2] == section
    load_qkv = Picked(qkv_own, qkv_other, use_own, w_qkv, sems.at[0])
    load_proj = Picked(proj_own, proj_other, use_own, w_proj, sems.at[1])
    load_proj.start()
    load_qkv.start()
    parts = (p0, p1, p2, p3)
    router = jnp.concatenate([params[...], jnp.zeros((LANES - 16, D), f32)], axis=0)
    upstream = grad_ref[...].astype(f32)
    lane = lax.broadcasted_iota(jnp.int32, (ROWS, LANES), 1)
    arrived = add_four(parts)
    tail = arrived[SPARE:]
    tail_high = tail.astype(bf16)
    tail_low = (tail - tail_high.astype(f32)).astype(bf16)
    tails = jnp.concatenate([tail_high.astype(f32), tail_low.astype(f32)], axis=0).astype(bf16)
    pick = lax.broadcasted_iota(jnp.int32, (16, LANES), 0) % (ROWS - SPARE) == (
        lax.broadcasted_iota(jnp.int32, (16, LANES), 1)
    )
    inner = dot_tn(tails, jnp.where(pick, 1.0, 0.0).astype(bf16))[:ROWS]
    token = lax.broadcasted_iota(jnp.int32, (ROWS, 1), 0)
    arrived = jnp.where(token < SPARE, arrived, 0.0)
    prob = prob_ref[...]
    grad_prob = jnp.zeros((ROWS, LANES), f32)
    for k in range(2):
        mine = (lane == k) | (lane == 2 + k)
        value = jnp.sum(jnp.where(mine, inner, 0.0), axis=-1, keepdims=True)
        grad_prob = grad_prob + jnp.where(expert_lanes(column[:, k : k + 1]), value, 0.0)
    grad_logit = prob * (grad_prob - jnp.sum(prob * grad_prob, axis=-1, keepdims=True))
    grad_logit = grad_logit.astype(bf16)
    logit_ref[...] = grad_logit
    grad_n2 = arrived + dot(grad_logit, router.astype(bf16))
    unit2, inverse2 = unit_norm(hidden[...])
    grad_hidden = upstream + norm_back(grad_n2, unit2, inverse2, params[2:3])
    grad_hidden_ref[...] = grad_hidden
    gain_row = jnp.sum(grad_n2 * unit2, axis=0, keepdims=True)
    bias_row = jnp.sum(grad_n2, axis=0, keepdims=True)
    branch = grad_hidden.astype(bf16)
    branch_ref[...] = branch
    load_proj.wait()
    grad_attended = dot_nt(branch, w_proj[...]).astype(bf16)
    query, key, value = (qkv_ref[j] for j in range(3))
    grad_query = jnp.zeros((ROWS, LOCAL), f32)
    grad_key = jnp.zeros((ROWS, LOCAL), f32)
    grad_value = jnp.zeros((ROWS, LOCAL), f32)
    for head in range(LOCAL // HD):
        mask = head_mask(head)
        weights = weights_ref[head]
        wide = weights.astype(f32)
        arriving = grad_attended * mask
        grad_weights = dot_nt(arriving, value)
        grad_scores = wide * (
            grad_weights - jnp.sum(wide * grad_weights, axis=-1, keepdims=True)
        )
        grad_scores = grad_scores.astype(bf16)
        grad_value = grad_value + dot_tn(weights, arriving)
        grad_query = grad_query + dot(grad_scores, key * mask)
        grad_key = grad_key + dot_tn(grad_scores, query * mask)
    scaling = 1.0 / math.sqrt(HD)
    load_qkv.wait()
    grad_n1 = jnp.zeros((ROWS, D), f32)
    for j, grad in enumerate((grad_query * scaling, grad_key * scaling, grad_value)):
        narrow = grad.astype(bf16)
        triple_ref[j] = narrow
        grad_n1 = grad_n1 + dot(narrow, w_qkv[j])
    part[...] = grad_n1.astype(bf16)
    unit1, _ = unit_norm(x_ref[...].astype(f32))
    first_gain = jnp.sum(grad_n1 * unit1, axis=0, keepdims=True)
    first_bias = jnp.sum(grad_n1, axis=0, keepdims=True)
    ends = [first_gain, first_bias, gain_row, bias_row, jnp.zeros((12, D), f32)]
    rows_ref[...] = jnp.concatenate(ends, axis=0).astype(bf16)


def run_attention_backward(section, place, *operands):
    saved = [(ROWS, D), (3, ROWS, LOCAL), (ROWS, LANES), (16, D)]
    return pl.pallas_call(
        functools.partial(attention_backward, section),
        out_shape=[
            jax.ShapeDtypeStruct((ROWS, D), bf16),
            jax.ShapeDtypeStruct((ROWS, D), f32),
        ]
        + [jax.ShapeDtypeStruct(shape, bf16) for shape in saved],
        in_specs=[SMEM] + [VMEM] * 12 + [HBM] * 4,
        out_specs=[VMEM] * 6,
        scratch_shapes=[
            pltpu.VMEM((3, LOCAL, D), bf16),
            pltpu.VMEM((LOCAL, D), bf16),
            DMA((2,)),
        ],
        compiler_params=pltpu.CompilerParams(vmem_limit_bytes=LIMIT),
        cost_estimate=pl.CostEstimate(
            flops=1_000_000_000, bytes_accessed=6_000_000, transcendentals=0
        ),
        name="attention_bwd",
    )(place, *operands)


def source_backward(p0, p1, p2, p3, grad_hidden, x_ref, params, out):
    unit, inverse = unit_norm(x_ref[...].astype(f32))
    passed = norm_back(add_four((p0, p1, p2, p3)), unit, inverse, params[0:1])
    out[...] = (grad_hidden[...] + passed).astype(bf16)


def run_source_backward(parts, grad_hidden, x, params):
    return pl.pallas_call(
        source_backward,
        out_shape=jax.ShapeDtypeStruct((ROWS, D), bf16),
        in_specs=[VMEM] * 7,
        out_specs=VMEM,
        compiler_params=pltpu.CompilerParams(vmem_limit_bytes=SHORT),
        cost_estimate=pl.CostEstimate(
            flops=6_000_000, bytes_accessed=3_000_000, transcendentals=0
        ),
        name="source_bwd",
    )(*parts, grad_hidden, x, params)


def attention_pieces(n1, triple, branch, attended):
    pieces = [dot_tn(n1[...], triple[j]) for j in range(3)]
    pieces.append(dot_tn(branch[...], attended[...]))
    return jnp.concatenate(pieces, axis=1).astype(bf16)


def small_grads(n2, logit, rows):
    return (dot_tn(n2[...], logit[...]) + dot_tn(rows[...], unit_rows())).astype(bf16)


def expert_grads(place, *refs):
    sets, out, (scr, done, in_sem, out_sem) = (refs[:4], refs[4:8]), refs[8], refs[9:]

    def loads(group, e):
        return [
            pltpu.make_async_copy(
                ref.at[j, e],
                scr.at[2 * (at // 2) + j, e, pl.ds((at % 2) * SLOTS, SLOTS)],
                in_sem.at[e],
            )
            for at, ref in enumerate(group)
            for j in range(2)
        ]

    for section, group in enumerate(sets):

        @pl.when(place[2] == section)
        def _():
            for e in range(E):
                for copy in loads(group, e):
                    copy.start()

    saves = []
    for e in range(E):
        for copy in loads(sets[0], e):
            copy.wait()
        buffer, active, slot_grad, grad_pre = (scr[j, e] for j in range(4))
        for m, grad in enumerate((dot_tn(buffer, grad_pre), dot_tn(slot_grad, active))):
            grad = grad.astype(bf16)
            for j in range(16):
                done[j, 2 * e + m] = grad[j * 48 : (j + 1) * 48]
            saves.append(
                pltpu.make_async_copy(
                    done.at[:, 2 * e + m], out.at[:, 2 * e + m], out_sem.at[2 * e + m]
                )
            )
            saves[-1].start()
    for copy in saves:
        copy.wait()


def run_expert_grads(place, first, second):
    return pl.pallas_call(
        expert_grads,
        out_shape=jax.ShapeDtypeStruct((16, 2 * E, 48, D), bf16),
        in_specs=[SMEM] + [HBM] * 8,
        out_specs=HBM,
        scratch_shapes=[
            pltpu.VMEM((4, E, 2 * SLOTS, D), bf16),
            pltpu.VMEM((16, 2 * E, 48, D), bf16),
            DMA((E,)),
            DMA((2 * E,)),
        ],
        compiler_params=pltpu.CompilerParams(vmem_limit_bytes=LIMIT),
        cost_estimate=pl.CostEstimate(
            flops=2_200_000_000, bytes_accessed=16_000_000, transcendentals=0
        ),
        name="expert_grads",
    )(place, *first, *second)


def attention_grads(section, place, *refs):
    attention, small, refs = refs[:4], refs[4:7], refs[7:]
    wide = jnp.concatenate([attention_pieces(*attention), small_grads(*small)], axis=1)
    if section == 1:
        refs[0][...] = wide
    else:
        other, mine, send = refs
        leading = place[2] == 0
        mine[...] = jnp.where(leading, wide, other[...])
        send[...] = jnp.where(leading, other[...], wide)


def run_attention_grads(section, place, *operands):
    outs = 1 if section == 1 else 2
    return pl.pallas_call(
        functools.partial(attention_grads, section),
        out_shape=[jax.ShapeDtypeStruct((D, WIDE), bf16)] * outs,
        in_specs=[SMEM] + [VMEM] * len(operands),
        out_specs=[VMEM] * outs,
        compiler_params=pltpu.CompilerParams(vmem_limit_bytes=SHORT),
        cost_estimate=pl.CostEstimate(
            flops=400_000_000, bytes_accessed=4_000_000, transcendentals=0
        ),
        name="attention_grads",
    )(place, *operands)


def between_heads(x):
    received = [
        lax.ppermute(x, "tensor", [(i, (i + k) % 4) for i in range(4)]) for k in range(1, 4)
    ]
    return [x] + received


def swapped(x):
    return lax.ppermute(x, "pipe", [(0, 1), (1, 0)])


def add_up(xs):
    a, b, c, d = (x.astype(f32) for x in xs)
    return (a + b) + (c + d)


def on_device(
    inputs,
    out_grad,
    routes,
    positions,
    norm1_gain,
    norm1_bias,
    qkv_weight,
    proj_weight,
    norm2_gain,
    norm2_bias,
    router_weight,
    expert_in,
    expert_out,
):
    core = lax.axis_index("pipe")
    leading = core == 0
    at = lax.axis_index("dp")
    place = jnp.stack([at // 4, at % 4, core]).astype(jnp.int32)

    def own_image(x):
        x = lax.dynamic_index_in_dim(x, core, 0, keepdims=False)
        return jnp.pad(x.reshape(SEQ, D), ((0, ROWS - SEQ), (0, 0)))

    own_qkv = qkv_weight[0].transpose(0, 2, 1)
    w_qkv = (own_qkv, swapped(own_qkv))
    w_proj = (proj_weight[0], swapped(proj_weight[0]))
    route = routes[0].reshape(2, SEQ, 2)
    slot = route * SLOTS + positions[0].reshape(2, SEQ, 2)
    lines = jnp.concatenate([route, slot], axis=-1).transpose(0, 2, 1)
    lines = jnp.pad(lines, ((0, 0), (0, 0), (0, ROWS - SEQ)), constant_values=-64)
    lines = jnp.pad(lines.astype(f32), ((0, 0), (0, 0), (0, D - ROWS)))
    vectors = [norm1_gain, norm1_bias, norm2_gain, norm2_bias, router_weight[0].T]
    rest = jnp.zeros((4, D), f32)

    def packed(image):
        return jnp.concatenate(vectors + [lines[image], rest])

    own = jnp.where(leading, packed(0), packed(1))
    other = swapped(jnp.where(leading, packed(1), packed(0)))
    params = [jnp.where(leading, own, other), jnp.where(leading, other, own)]
    columns = [p[ROUTES_AT : ROUTES_AT + 4, :ROWS].T.astype(jnp.int32) for p in params]
    wait_for = (w_qkv[1], w_proj[1], other)
    own_in, own_out, *_ = lax.optimization_barrier((expert_in[0], expert_out[0], *wait_for))
    w_in = (expert_in[0], swapped(own_in))
    w_out = (expert_out[0], swapped(own_out))

    def forward(section, source, x):
        part, n1, triple, weights, attended, *more = run_attention_forward(
            section, place, source, params[section], w_qkv, w_proj
        )
        x = more[0] if more else x
        mix, hidden, n2, prob, y0, y1, slope, kept = run_experts_forward(
            section, place, x, between_heads(part), params[section], columns[section], w_in, w_out
        )
        stored = (x, n1, triple, weights, attended, hidden, n2, prob, y0, y1, slope)
        return hidden, between_heads(mix), [kept, swapped(kept)], stored

    def backward(section, upstream, stored, later_operands, later_narrow):
        x, n1, triple, weights, attended, hidden, n2, prob, y0, y1, slope = stored
        partial, kept, *more = run_experts_backward(
            section,
            place,
            upstream,
            prob,
            y0,
            y1,
            params[section],
            columns[section],
            slope,
            w_in,
            w_out,
        )
        grad = more[0] if more else upstream[0]
        parts = between_heads(partial)
        operands = [kept, swapped(kept)]
        wide = None
        if section == 0:
            wide = run_expert_grads(
                place, first_operands + operands, second_operands + later_operands
            )
            grad, wide = lax.optimization_barrier((grad, wide))
        part, grad_hidden, branch, grad_triple, logit, rows = run_attention_backward(
            section,
            place,
            grad,
            *parts,
            hidden,
            prob,
            params[section],
            columns[section],
            weights,
            triple,
            x,
            *w_qkv,
            *w_proj,
        )
        narrow = run_attention_grads(
            section, place, n1, grad_triple, branch, attended, n2, logit, rows, *later_narrow
        )
        return grad, between_heads(part), grad_hidden, operands, wide, narrow

    def both_images(first, second):
        mine = jnp.where(leading, first, second)[:SEQ]
        arrived = swapped(jnp.where(leading, second, first))[:SEQ]
        images = jnp.where(leading, jnp.stack([mine, arrived]), jnp.stack([arrived, mine]))
        return images.reshape(1, 2, 1, SEQ, D)

    source = own_image(inputs)
    hidden, mixes, first_operands, stored_first = forward(0, [source], source)
    hidden, mixes, second_operands, stored_second = forward(1, [hidden] + mixes, None)
    middle = stored_second[0]
    last = (hidden + add_up(mixes)).astype(bf16)
    _, parts, grad_hidden, operands, _, narrow = backward(
        1, [own_image(out_grad)], stored_second, None, []
    )
    passed, parts, grad_hidden, _, wide, (mine, send) = backward(
        0, parts + [grad_hidden, middle, params[1]], stored_first, operands, narrow
    )
    wide = lax.psum_scatter(wide, "dp", scatter_dimension=0, tiled=True)
    wide = lax.optimization_barrier(wide).reshape(E, 2, 48, D).astype(f32)
    narrow = (mine.astype(f32) + swapped(send).astype(f32)).astype(bf16)
    narrow = lax.all_to_all(narrow.reshape(16, 48, WIDE), "dp", 0, 0, tiled=True)
    small = jnp.sum(narrow.astype(f32), axis=0)
    norm1 = add_up(between_heads(small[:, D : D + 2].astype(bf16)))
    entering = run_source_backward(parts, grad_hidden, source, params[0])
    activations = both_images(middle, last)
    input_grads = both_images(entering, passed)
    return (
        activations,
        input_grads,
        norm1[:, 0][None],
        norm1[:, 1][None],
        small[:, : 3 * LOCAL].reshape(48, 3, LOCAL).transpose(1, 0, 2)[None],
        small[:, 3 * LOCAL : D].T[None],
        small[:, D + 2][None],
        small[:, D + 3][None],
        small[:, D + ROUTER_AT : D + ROUTER_AT + E][None],
        wide[:, 0][None],
        wide[:, 1].transpose(0, 2, 1)[None],
    )


def solution(mesh):
    in_specs = (
        P(None, "dp", None, None),
        P(None, "dp", None, None),
        P("pipe", None, "dp", None, None),
        P("pipe", None, "dp", None, None),
        P("pipe", None),
        P("pipe", None),
        P("pipe", None, None, "tensor"),
        P("pipe", "tensor", None),
        P("pipe", None),
        P("pipe", None),
        P("pipe", None, None),
        P("pipe", None, None, "tensor"),
        P("pipe", None, "tensor", None),
    )
    out_specs = (
        P("pipe", None, "dp", None, None),
        P("pipe", None, "dp", None, None),
        P("pipe", "dp"),
        P("pipe", "dp"),
        P("pipe", None, "dp", "tensor"),
        P("pipe", "tensor", "dp"),
        P("pipe", "dp"),
        P("pipe", "dp"),
        P("pipe", "dp", None),
        P("pipe", None, "dp", "tensor"),
        P("pipe", None, "tensor", "dp"),
    )
    return jax.shard_map(
        on_device, mesh=mesh, in_specs=in_specs, out_specs=out_specs, check_vma=False
    )
```

```python
import functools
import math

import jax
import jax.numpy as jnp
from jax import lax
from jax.experimental import pallas as pl
from jax.experimental.pallas import tpu as pltpu
from jax.sharding import PartitionSpec as P

HD = 64
E = 4
SEQ = 197
CAP = 111
ROWS = 208
SLOTS = 112
TABLE = E * SLOTS
D = 768
LOCAL = 192
LANES = 128
WIDE = D + LANES
SPARE = 200
ROUTER_AT = 4
ROUTES_AT = 8
SLOTS_AT = 10

f32 = jnp.float32
bf16 = jnp.bfloat16
eps = 1e-06
VMEM = pl.BlockSpec(memory_space=pltpu.VMEM)
SMEM = pl.BlockSpec(memory_space=pltpu.SMEM)
HBM = pl.BlockSpec(memory_space=pl.ANY)
DMA = pltpu.SemaphoreType.DMA
LIMIT = 60 * 1024 * 1024
SHORT = 28 * 1024 * 1024


def dot(a, b):
    return lax.dot_general(a, b, (((1,), (0,)), ((), ())), preferred_element_type=f32)


def dot_nt(a, b):
    return lax.dot_general(a, b, (((1,), (1,)), ((), ())), preferred_element_type=f32)


def dot_tn(a, b):
    return lax.dot_general(a, b, (((0,), (0,)), ((), ())), preferred_element_type=f32)


def unit_norm(v):
    centred = v - jnp.mean(v, axis=-1, keepdims=True)
    inverse = lax.rsqrt(jnp.mean(centred * centred, axis=-1, keepdims=True) + eps)
    return centred * inverse, inverse


def norm_back(upstream, normed, inverse, gain):
    scaled = upstream * gain
    inner = jnp.mean(scaled * normed, axis=-1, keepdims=True)
    return inverse * (scaled - jnp.mean(scaled, axis=-1, keepdims=True) - normed * inner)


def head_mask(head):
    lane = lax.broadcasted_iota(jnp.int32, (1, LOCAL), 1)
    inside = (lane >= head * HD) & (lane < (head + 1) * HD)
    return jnp.where(inside, 1.0, 0.0).astype(bf16)


def slot_rows(row_ids):
    ids = lax.broadcasted_iota(jnp.int32, (TABLE, ROWS), 0)
    return jnp.where(ids == row_ids, 1.0, 0.0)


def slot_columns(column_ids):
    ids = lax.broadcasted_iota(jnp.int32, (ROWS, TABLE), 1)
    return jnp.where(ids == column_ids, 1.0, 0.0)


def expert_lanes(route):
    lane = lax.broadcasted_iota(jnp.int32, (ROWS, LANES), 1)
    return lane == route + ROUTER_AT


def gate_of(prob, route):
    return jnp.sum(jnp.where(expert_lanes(route), prob, 0.0), axis=-1, keepdims=True)


class Picked:
    def __init__(self, own, other, use_own, held, sem):
        self.copies = [pltpu.make_async_copy(ref, held, sem) for ref in (own, other)]
        self.use_own = use_own

    def start(self):
        pl.when(self.use_own)(self.copies[0].start)
        pl.when(jnp.logical_not(self.use_own))(self.copies[1].start)

    def wait(self):
        self.copies[0].wait()


class Operands:
    def __init__(self, held, out, sems):
        self.held, self.out, self.sems = held, out, sems
        self.copies = []

    def put(self, j, e, value):
        self.held[j, e] = value
        copy = pltpu.make_async_copy(self.held.at[j, e], self.out.at[j, e], self.sems.at[j, e])
        copy.start()
        self.copies.append(copy)

    def wait(self):
        for copy in self.copies:
            copy.wait()


class Kept:
    def __init__(self, outs, held, sems):
        self.outs, self.held, self.sems = outs, held, sems
        self.copies = []

    def put(self, at, value, index=None):
        held, out = self.held[at], self.outs[at]
        if index is not None:
            held, out = held.at[index], out.at[index]
        held[...] = value
        copy = pltpu.make_async_copy(held, out, self.sems.at[len(self.copies)])
        copy.start()
        self.copies.append(copy)

    def wait(self):
        for copy in self.copies:
            copy.wait()


def unit_rows():
    row = lax.broadcasted_iota(jnp.int32, (16, LANES), 0)
    lane = lax.broadcasted_iota(jnp.int32, (16, LANES), 1)
    return jnp.where(row == lane, 1.0, 0.0).astype(bf16)


def add_four(refs):
    a, b, c, d = (ref[...].astype(f32) for ref in refs)
    return (a + b) + (c + d)


def attention_forward(section, place, *refs):
    summed = section == 1
    if summed:
        hidden, *refs = refs
        parts, refs = refs[:4], refs[4:]
    else:
        x_ref, *refs = refs
    params, qkv_own, qkv_other, proj_own, proj_other, *refs = refs
    part, refs = refs[0], refs[1:]
    saved, refs = refs[:4], refs[4:]
    *more, w_qkv, w_proj, sems, held_n1, held_qkv, held_p, held_o, save_sems = refs
    kept = Kept(saved, (held_n1, held_qkv, held_p, held_o), save_sems)
    use_own = place[2] == section
    load_qkv = Picked(qkv_own, qkv_other, use_own, w_qkv, sems.at[0])
    load_proj = Picked(proj_own, proj_other, use_own, w_proj, sems.at[1])
    load_qkv.start()
    load_proj.start()
    if summed:
        source = (hidden[...] + add_four(parts)).astype(bf16)
        more[0][...] = source
    else:
        source = x_ref[...]
    normed, _ = unit_norm(source.astype(f32))
    n1 = (normed * params[0:1] + params[1:2]).astype(bf16)
    kept.put(0, n1)
    load_qkv.wait()
    query, key, value = (dot_nt(n1, w_qkv[j]).astype(bf16) for j in range(3))
    for j, piece in enumerate((query, key, value)):
        kept.put(1, piece, j)
    real = lax.broadcasted_iota(jnp.int32, (1, ROWS), 1) < SEQ
    attended = jnp.zeros((ROWS, LOCAL), f32)
    for head in range(LOCAL // HD):
        mask = head_mask(head)
        scores = dot_nt(query * mask, key) * (1.0 / math.sqrt(HD))
        scores = jnp.where(real, scores, -1e30)
        shifted = jnp.exp(scores - jnp.max(scores, axis=-1, keepdims=True))
        weights = (shifted / jnp.sum(shifted, axis=-1, keepdims=True)).astype(bf16)
        kept.put(2, weights, head)
        attended = attended + dot(weights, value * mask)
    attended = attended.astype(bf16)
    kept.put(3, attended)
    load_proj.wait()
    part[...] = dot(attended, w_proj[...]).astype(bf16)
    kept.wait()


def run_attention_forward(section, place, source, params, w_qkv, w_proj):
    saved = [(ROWS, D), (3, ROWS, LOCAL), (3, ROWS, ROWS), (ROWS, LOCAL)]
    outs = [jax.ShapeDtypeStruct((ROWS, D), bf16)]
    outs += [jax.ShapeDtypeStruct(shape, bf16) for shape in saved]
    if section == 1:
        outs.append(jax.ShapeDtypeStruct((ROWS, D), bf16))
    return pl.pallas_call(
        functools.partial(attention_forward, section),
        out_shape=outs,
        in_specs=[SMEM] + [VMEM] * (len(source) + 1) + [HBM] * 4,
        out_specs=[VMEM] + [HBM] * 4 + [VMEM] * (len(outs) - 5),
        scratch_shapes=[
            pltpu.VMEM((3, LOCAL, D), bf16),
            pltpu.VMEM((LOCAL, D), bf16),
            DMA((2,)),
        ]
        + [pltpu.VMEM(shape, bf16) for shape in saved]
        + [DMA((8,))],
        compiler_params=pltpu.CompilerParams(vmem_limit_bytes=LIMIT),
        cost_estimate=pl.CostEstimate(
            flops=600_000_000, bytes_accessed=4_000_000, transcendentals=130_000
        ),
        name="attention_fwd",
    )(place, *source, params, *w_qkv, *w_proj)


def experts_forward(section, place, *refs):
    x_ref, *refs = refs
    parts, refs = refs[:4], refs[4:]
    params, columns, in_own, in_other, out_own, out_other, *refs = refs
    mix_ref, *refs = refs
    saved, kept_out, refs = refs[:6], refs[6], refs[7:]
    held, refs = refs[:6], refs[6:]
    w_in, w_out, kept, table, in_sem, out_sem, save_sems, keep_sem = refs
    saver = Kept(saved, held, save_sems)
    operands = Operands(kept, kept_out, keep_sem)
    use_own = place[2] == section
    loads_in = []
    loads_out = []
    for e in range(E):
        loads_in.append(
            Picked(in_own.at[e], in_other.at[e], use_own, w_in.at[e], in_sem.at[e])
        )
        loads_out.append(
            Picked(out_own.at[e], out_other.at[e], use_own, w_out.at[e], out_sem.at[e])
        )
    for e in range(E):
        loads_in[e].start()
        loads_out[e].start()
    router = jnp.concatenate([params[...], jnp.zeros((LANES - 16, D), f32)], axis=0)
    router_high = router.astype(bf16)
    router_low = (router - router_high.astype(f32)).astype(bf16)
    lane = lax.broadcasted_iota(jnp.int32, (1, LANES), 1)
    expert_lane = (lane >= ROUTER_AT) & (lane < ROUTER_AT + E)
    hidden = x_ref[...].astype(f32) + add_four(parts)
    saver.put(0, hidden)
    normed, _ = unit_norm(hidden)
    n2 = normed * params[2:3] + params[3:4]
    high = n2.astype(bf16)
    low = (n2 - high.astype(f32)).astype(bf16)
    saver.put(1, high)
    slots = params[SLOTS_AT : SLOTS_AT + 2, :ROWS].astype(jnp.int32)
    spread = (slot_rows(slots[0:1]) + slot_rows(slots[1:2])).astype(bf16)
    rows = dot(spread, high).astype(bf16)
    for e in range(E):
        operands.put(0, e, rows[e * SLOTS : (e + 1) * SLOTS])
    logits = dot_nt(high, router_high) + (dot_nt(low, router_high) + dot_nt(high, router_low))
    logits = jnp.where(expert_lane, logits, -1e30)
    raised = jnp.exp(logits - jnp.max(logits, axis=-1, keepdims=True))
    prob = raised / jnp.sum(raised, axis=-1, keepdims=True)
    saver.put(2, prob)
    curve = math.sqrt(2.0 / math.pi)
    for e in range(E):
        loads_in[e].wait()
        z = dot(kept[0, e], w_in[e])
        square = z * z
        bend = jnp.tanh(curve * z * (1.0 + 0.044715 * square))
        half = 0.5 * (1.0 + bend)
        active = (z * half).astype(bf16)
        operands.put(1, e, active)
        slope = half + (0.5 * curve) * z * (1.0 - bend * bend) * (1.0 + 0.134145 * square)
        saver.put(5, slope.astype(bf16), e)
        loads_out[e].wait()
        table[e * SLOTS : (e + 1) * SLOTS] = dot(active, w_out[e]).astype(bf16)
    mix = jnp.zeros((ROWS, D), f32)
    for k in range(2):
        gate = gate_of(prob, columns[:, k : k + 1])
        picked = dot(slot_columns(columns[:, 2 + k : 3 + k]).astype(bf16), table[...])
        saver.put(3 + k, picked.astype(bf16))
        mix = mix + gate * picked
    mix_ref[...] = mix.astype(bf16)
    saver.wait()
    operands.wait()


def run_experts_forward(section, place, x, parts, params, columns, w_in, w_out):
    saved = [
        ((ROWS, D), f32),
        ((ROWS, D), bf16),
        ((ROWS, LANES), f32),
        ((ROWS, D), bf16),
        ((ROWS, D), bf16),
        ((E, SLOTS, D), bf16),
    ]
    return pl.pallas_call(
        functools.partial(experts_forward, section),
        out_shape=[jax.ShapeDtypeStruct((ROWS, D), bf16)]
        + [jax.ShapeDtypeStruct(*kind) for kind in saved]
        + [jax.ShapeDtypeStruct((2, E, SLOTS, D), bf16)],
        in_specs=[SMEM] + [VMEM] * 7 + [HBM] * 4,
        out_specs=[VMEM] + [HBM] * 7,
        scratch_shapes=[pltpu.VMEM(*kind) for kind in saved]
        + [
            pltpu.VMEM((E, D, D), bf16),
            pltpu.VMEM((E, D, D), bf16),
            pltpu.VMEM((2, E, SLOTS, D), bf16),
            pltpu.VMEM((TABLE, D), bf16),
            DMA((E,)),
            DMA((E,)),
            DMA((5 + E,)),
            DMA((2, E)),
        ],
        compiler_params=pltpu.CompilerParams(vmem_limit_bytes=LIMIT),
        cost_estimate=pl.CostEstimate(
            flops=4_000_000_000, bytes_accessed=16_000_000, transcendentals=400_000
        ),
        name="experts_fwd",
    )(place, x, *parts, params, columns, *w_in, *w_out)


def experts_backward(section, place, *refs):
    if section == 0:
        parts, refs = refs[:4], refs[4:]
        grad_hidden, x_ref, later, *refs = refs
    else:
        grad_ref, *refs = refs
    prob_ref, y0_ref, y1_ref, params, columns, slope_in, *refs = refs
    in_own, in_other, out_own, out_other, partial_ref, kept_out, *refs = refs
    if section == 0:
        passed_ref, *refs = refs
    w_in, w_out, slopes, kept, table, in_sem, out_sem, slope_sem, keep_sem = refs
    operands = Operands(kept, kept_out, keep_sem)
    use_own = place[2] == section
    loads = []
    for e in range(E):
        loads.append(
            (
                Picked(out_own.at[e], out_other.at[e], use_own, w_out.at[e], out_sem.at[e]),
                pltpu.make_async_copy(slope_in.at[e], slopes.at[e], slope_sem.at[e]),
                Picked(in_own.at[e], in_other.at[e], use_own, w_in.at[e], in_sem.at[e]),
            )
        )
        for copy in loads[e]:
            copy.start()
    if section == 0:
        unit, inverse = unit_norm(x_ref[...].astype(f32))
        passed = norm_back(add_four(parts), unit, inverse, later[0:1])
        passed = (grad_hidden[...] + passed).astype(bf16)
        passed_ref[...] = passed
        upstream = passed.astype(f32)
    else:
        upstream = grad_ref[...].astype(f32)
    lane = lax.broadcasted_iota(jnp.int32, (ROWS, LANES), 1)
    slots = params[SLOTS_AT : SLOTS_AT + 2, :ROWS].astype(jnp.int32)
    prob = prob_ref[...]
    rows = jnp.zeros((TABLE, D), f32)
    for k in range(2):
        gate = gate_of(prob, columns[:, k : k + 1])
        weighted = (gate * upstream).astype(bf16)
        rows = rows + dot(slot_rows(slots[k : k + 1]).astype(bf16), weighted)
    rows = rows.astype(bf16)
    for e in range(E):
        operands.put(0, e, rows[e * SLOTS : (e + 1) * SLOTS])
    for e in range(E):
        loads[e][0].wait()
        grad_active = dot_nt(kept[0, e], w_out[e])
        loads[e][1].wait()
        grad_pre = (grad_active * slopes[e].astype(f32)).astype(bf16)
        operands.put(1, e, grad_pre)
        loads[e][2].wait()
        table[e * SLOTS : (e + 1) * SLOTS] = dot_nt(grad_pre, w_in[e]).astype(bf16)
    packed = jnp.zeros((ROWS, LANES), f32)
    for k, picked in enumerate((y0_ref, y1_ref)):
        inner = jnp.sum(upstream * picked[...].astype(f32), axis=-1, keepdims=True)
        high = inner.astype(bf16).astype(f32)
        packed = packed + jnp.where(lane == k, high, 0.0)
        packed = packed + jnp.where(lane == 2 + k, inner - high, 0.0)
    longer = jnp.concatenate([packed, jnp.zeros((D - ROWS, LANES), f32)], axis=0).astype(bf16)
    tail = dot_nt(unit_rows(), longer)[: ROWS - SPARE]
    gather = slot_columns(columns[:, 2:3]) + slot_columns(columns[:, 3:4])
    spread = dot(gather.astype(bf16), table[...])
    partial_ref[...] = jnp.concatenate([spread[:SPARE], tail], axis=0).astype(bf16)
    operands.wait()


def run_experts_backward(
    section, place, grad, prob, y0, y1, params, columns, slope, w_in, w_out
):
    outs = [
        jax.ShapeDtypeStruct((ROWS, D), bf16),
        jax.ShapeDtypeStruct((2, E, SLOTS, D), bf16),
    ]
    if section == 0:
        outs.append(jax.ShapeDtypeStruct((ROWS, D), bf16))
    return pl.pallas_call(
        functools.partial(experts_backward, section),
        out_shape=outs,
        in_specs=[SMEM] + [VMEM] * (len(grad) + 5) + [HBM] * 5,
        out_specs=[VMEM, HBM] + [VMEM] * (len(outs) - 2),
        scratch_shapes=[
            pltpu.VMEM((E, D, D), bf16),
            pltpu.VMEM((E, D, D), bf16),
            pltpu.VMEM((E, SLOTS, D), bf16),
            pltpu.VMEM((2, E, SLOTS, D), bf16),
            pltpu.VMEM((TABLE, D), bf16),
            DMA((E,)),
            DMA((E,)),
            DMA((E,)),
            DMA((2, E)),
        ],
        compiler_params=pltpu.CompilerParams(vmem_limit_bytes=LIMIT),
        cost_estimate=pl.CostEstimate(
            flops=4_000_000_000, bytes_accessed=16_000_000, transcendentals=0
        ),
        name="experts_bwd",
    )(place, *grad, prob, y0, y1, params, columns, slope, *w_in, *w_out)


def attention_backward(
    section,
    place,
    grad_ref,
    p0,
    p1,
    p2,
    p3,
    hidden,
    prob_ref,
    params,
    column,
    weights_ref,
    qkv_ref,
    x_ref,
    qkv_own,
    qkv_other,
    proj_own,
    proj_other,
    part,
    grad_hidden_ref,
    branch_ref,
    triple_ref,
    logit_ref,
    rows_ref,
    w_qkv,
    w_proj,
    sems,
):
    use_own = place[2] == section
    load_qkv = Picked(qkv_own, qkv_other, use_own, w_qkv, sems.at[0])
    load_proj = Picked(proj_own, proj_other, use_own, w_proj, sems.at[1])
    load_proj.start()
    load_qkv.start()
    parts = (p0, p1, p2, p3)
    router = jnp.concatenate([params[...], jnp.zeros((LANES - 16, D), f32)], axis=0)
    upstream = grad_ref[...].astype(f32)
    lane = lax.broadcasted_iota(jnp.int32, (ROWS, LANES), 1)
    arrived = add_four(parts)
    tail = arrived[SPARE:]
    tail_high = tail.astype(bf16)
    tail_low = (tail - tail_high.astype(f32)).astype(bf16)
    tails = jnp.concatenate([tail_high.astype(f32), tail_low.astype(f32)], axis=0).astype(bf16)
    pick = lax.broadcasted_iota(jnp.int32, (16, LANES), 0) % (ROWS - SPARE) == (
        lax.broadcasted_iota(jnp.int32, (16, LANES), 1)
    )
    inner = dot_tn(tails, jnp.where(pick, 1.0, 0.0).astype(bf16))[:ROWS]
    token = lax.broadcasted_iota(jnp.int32, (ROWS, 1), 0)
    arrived = jnp.where(token < SPARE, arrived, 0.0)
    prob = prob_ref[...]
    grad_prob = jnp.zeros((ROWS, LANES), f32)
    for k in range(2):
        mine = (lane == k) | (lane == 2 + k)
        value = jnp.sum(jnp.where(mine, inner, 0.0), axis=-1, keepdims=True)
        grad_prob = grad_prob + jnp.where(expert_lanes(column[:, k : k + 1]), value, 0.0)
    grad_logit = prob * (grad_prob - jnp.sum(prob * grad_prob, axis=-1, keepdims=True))
    grad_logit = grad_logit.astype(bf16)
    logit_ref[...] = grad_logit
    grad_n2 = arrived + dot(grad_logit, router.astype(bf16))
    unit2, inverse2 = unit_norm(hidden[...])
    grad_hidden = upstream + norm_back(grad_n2, unit2, inverse2, params[2:3])
    grad_hidden_ref[...] = grad_hidden
    gain_row = jnp.sum(grad_n2 * unit2, axis=0, keepdims=True)
    bias_row = jnp.sum(grad_n2, axis=0, keepdims=True)
    branch = grad_hidden.astype(bf16)
    branch_ref[...] = branch
    load_proj.wait()
    grad_attended = dot_nt(branch, w_proj[...]).astype(bf16)
    query, key, value = (qkv_ref[j] for j in range(3))
    grad_query = jnp.zeros((ROWS, LOCAL), f32)
    grad_key = jnp.zeros((ROWS, LOCAL), f32)
    grad_value = jnp.zeros((ROWS, LOCAL), f32)
    for head in range(LOCAL // HD):
        mask = head_mask(head)
        weights = weights_ref[head]
        wide = weights.astype(f32)
        arriving = grad_attended * mask
        grad_weights = dot_nt(arriving, value)
        grad_scores = wide * (
            grad_weights - jnp.sum(wide * grad_weights, axis=-1, keepdims=True)
        )
        grad_scores = grad_scores.astype(bf16)
        grad_value = grad_value + dot_tn(weights, arriving)
        grad_query = grad_query + dot(grad_scores, key * mask)
        grad_key = grad_key + dot_tn(grad_scores, query * mask)
    scaling = 1.0 / math.sqrt(HD)
    load_qkv.wait()
    grad_n1 = jnp.zeros((ROWS, D), f32)
    for j, grad in enumerate((grad_query * scaling, grad_key * scaling, grad_value)):
        narrow = grad.astype(bf16)
        triple_ref[j] = narrow
        grad_n1 = grad_n1 + dot(narrow, w_qkv[j])
    part[...] = grad_n1.astype(bf16)
    unit1, _ = unit_norm(x_ref[...].astype(f32))
    first_gain = jnp.sum(grad_n1 * unit1, axis=0, keepdims=True)
    first_bias = jnp.sum(grad_n1, axis=0, keepdims=True)
    ends = [first_gain, first_bias, gain_row, bias_row, jnp.zeros((12, D), f32)]
    rows_ref[...] = jnp.concatenate(ends, axis=0).astype(bf16)


def run_attention_backward(section, place, *operands):
    saved = [(ROWS, D), (3, ROWS, LOCAL), (ROWS, LANES), (16, D)]
    return pl.pallas_call(
        functools.partial(attention_backward, section),
        out_shape=[
            jax.ShapeDtypeStruct((ROWS, D), bf16),
            jax.ShapeDtypeStruct((ROWS, D), f32),
        ]
        + [jax.ShapeDtypeStruct(shape, bf16) for shape in saved],
        in_specs=[SMEM] + [VMEM] * 12 + [HBM] * 4,
        out_specs=[VMEM] * 6,
        scratch_shapes=[
            pltpu.VMEM((3, LOCAL, D), bf16),
            pltpu.VMEM((LOCAL, D), bf16),
            DMA((2,)),
        ],
        compiler_params=pltpu.CompilerParams(vmem_limit_bytes=LIMIT),
        cost_estimate=pl.CostEstimate(
            flops=1_000_000_000, bytes_accessed=6_000_000, transcendentals=0
        ),
        name="attention_bwd",
    )(place, *operands)


def source_backward(p0, p1, p2, p3, grad_hidden, x_ref, params, out):
    unit, inverse = unit_norm(x_ref[...].astype(f32))
    passed = norm_back(add_four((p0, p1, p2, p3)), unit, inverse, params[0:1])
    out[...] = (grad_hidden[...] + passed).astype(bf16)


def run_source_backward(parts, grad_hidden, x, params):
    return pl.pallas_call(
        source_backward,
        out_shape=jax.ShapeDtypeStruct((ROWS, D), bf16),
        in_specs=[VMEM] * 7,
        out_specs=VMEM,
        compiler_params=pltpu.CompilerParams(vmem_limit_bytes=SHORT),
        cost_estimate=pl.CostEstimate(
            flops=6_000_000, bytes_accessed=3_000_000, transcendentals=0
        ),
        name="source_bwd",
    )(*parts, grad_hidden, x, params)


def attention_pieces(n1, triple, branch, attended):
    pieces = [dot_tn(n1[...], triple[j]) for j in range(3)]
    pieces.append(dot_tn(branch[...], attended[...]))
    return jnp.concatenate(pieces, axis=1).astype(bf16)


def small_grads(n2, logit, rows):
    return (dot_tn(n2[...], logit[...]) + dot_tn(rows[...], unit_rows())).astype(bf16)


def expert_grads(place, *refs):
    sets, out, (scr, done, in_sem, out_sem) = (refs[:4], refs[4:8]), refs[8], refs[9:]

    def loads(group, e):
        return [
            pltpu.make_async_copy(
                ref.at[j, e],
                scr.at[2 * (at // 2) + j, e, pl.ds((at % 2) * SLOTS, SLOTS)],
                in_sem.at[e],
            )
            for at, ref in enumerate(group)
            for j in range(2)
        ]

    for section, group in enumerate(sets):

        @pl.when(place[2] == section)
        def _():
            for e in range(E):
                for copy in loads(group, e):
                    copy.start()

    saves = []
    for e in range(E):
        for copy in loads(sets[0], e):
            copy.wait()
        buffer, active, slot_grad, grad_pre = (scr[j, e] for j in range(4))
        for m, grad in enumerate((dot_tn(buffer, grad_pre), dot_tn(slot_grad, active))):
            grad = grad.astype(bf16)
            for j in range(16):
                done[j, 2 * e + m] = grad[j * 48 : (j + 1) * 48]
            saves.append(
                pltpu.make_async_copy(
                    done.at[:, 2 * e + m], out.at[:, 2 * e + m], out_sem.at[2 * e + m]
                )
            )
            saves[-1].start()
    for copy in saves:
        copy.wait()


def run_expert_grads(place, first, second):
    return pl.pallas_call(
        expert_grads,
        out_shape=jax.ShapeDtypeStruct((16, 2 * E, 48, D), bf16),
        in_specs=[SMEM] + [HBM] * 8,
        out_specs=HBM,
        scratch_shapes=[
            pltpu.VMEM((4, E, 2 * SLOTS, D), bf16),
            pltpu.VMEM((16, 2 * E, 48, D), bf16),
            DMA((E,)),
            DMA((2 * E,)),
        ],
        compiler_params=pltpu.CompilerParams(vmem_limit_bytes=LIMIT),
        cost_estimate=pl.CostEstimate(
            flops=2_200_000_000, bytes_accessed=16_000_000, transcendentals=0
        ),
        name="expert_grads",
    )(place, *first, *second)


def attention_grads(section, place, *refs):
    attention, small, refs = refs[:4], refs[4:7], refs[7:]
    wide = jnp.concatenate([attention_pieces(*attention), small_grads(*small)], axis=1)
    if section == 1:
        refs[0][...] = wide
    else:
        other, mine, send = refs
        leading = place[2] == 0
        mine[...] = jnp.where(leading, wide, other[...])
        send[...] = jnp.where(leading, other[...], wide)


def run_attention_grads(section, place, *operands):
    outs = 1 if section == 1 else 2
    return pl.pallas_call(
        functools.partial(attention_grads, section),
        out_shape=[jax.ShapeDtypeStruct((D, WIDE), bf16)] * outs,
        in_specs=[SMEM] + [VMEM] * len(operands),
        out_specs=[VMEM] * outs,
        compiler_params=pltpu.CompilerParams(vmem_limit_bytes=SHORT),
        cost_estimate=pl.CostEstimate(
            flops=400_000_000, bytes_accessed=4_000_000, transcendentals=0
        ),
        name="attention_grads",
    )(place, *operands)


def between_heads(x):
    received = [
        lax.ppermute(x, "tensor", [(i, (i + k) % 4) for i in range(4)]) for k in range(1, 4)
    ]
    return [x] + received


def swapped(x):
    return lax.ppermute(x, "pipe", [(0, 1), (1, 0)])


def add_up(xs):
    a, b, c, d = (x.astype(f32) for x in xs)
    return (a + b) + (c + d)


def on_device(
    inputs,
    out_grad,
    routes,
    positions,
    norm1_gain,
    norm1_bias,
    qkv_weight,
    proj_weight,
    norm2_gain,
    norm2_bias,
    router_weight,
    expert_in,
    expert_out,
):
    core = lax.axis_index("pipe")
    leading = core == 0
    at = lax.axis_index("dp")
    place = jnp.stack([at // 4, at % 4, core]).astype(jnp.int32)

    def own_image(x):
        x = lax.dynamic_index_in_dim(x, core, 0, keepdims=False)
        return jnp.pad(x.reshape(SEQ, D), ((0, ROWS - SEQ), (0, 0)))

    own_qkv = qkv_weight[0].transpose(0, 2, 1)
    w_qkv = (own_qkv, swapped(own_qkv))
    w_proj = (proj_weight[0], swapped(proj_weight[0]))
    route = routes[0].reshape(2, SEQ, 2)
    slot = route * SLOTS + positions[0].reshape(2, SEQ, 2)
    lines = jnp.concatenate([route, slot], axis=-1).transpose(0, 2, 1)
    lines = jnp.pad(lines, ((0, 0), (0, 0), (0, ROWS - SEQ)), constant_values=-64)
    lines = jnp.pad(lines.astype(f32), ((0, 0), (0, 0), (0, D - ROWS)))
    vectors = [norm1_gain, norm1_bias, norm2_gain, norm2_bias, router_weight[0].T]
    rest = jnp.zeros((4, D), f32)

    def packed(image):
        return jnp.concatenate(vectors + [lines[image], rest])

    own = jnp.where(leading, packed(0), packed(1))
    other = swapped(jnp.where(leading, packed(1), packed(0)))
    params = [jnp.where(leading, own, other), jnp.where(leading, other, own)]
    columns = [p[ROUTES_AT : ROUTES_AT + 4, :ROWS].T.astype(jnp.int32) for p in params]
    wait_for = (w_qkv[1], w_proj[1], other)
    own_in, own_out, *_ = lax.optimization_barrier((expert_in[0], expert_out[0], *wait_for))
    w_in = (expert_in[0], swapped(own_in))
    w_out = (expert_out[0], swapped(own_out))

    def forward(section, source, x):
        part, n1, triple, weights, attended, *more = run_attention_forward(
            section, place, source, params[section], w_qkv, w_proj
        )
        x = more[0] if more else x
        mix, hidden, n2, prob, y0, y1, slope, kept = run_experts_forward(
            section, place, x, between_heads(part), params[section], columns[section], w_in, w_out
        )
        stored = (x, n1, triple, weights, attended, hidden, n2, prob, y0, y1, slope)
        return hidden, between_heads(mix), [kept, swapped(kept)], stored

    def backward(section, upstream, stored, later_operands, later_narrow):
        x, n1, triple, weights, attended, hidden, n2, prob, y0, y1, slope = stored
        partial, kept, *more = run_experts_backward(
            section,
            place,
            upstream,
            prob,
            y0,
            y1,
            params[section],
            columns[section],
            slope,
            w_in,
            w_out,
        )
        grad = more[0] if more else upstream[0]
        parts = between_heads(partial)
        operands = [kept, swapped(kept)]
        wide = None
        if section == 0:
            wide = run_expert_grads(
                place, first_operands + operands, second_operands + later_operands
            )
            grad, wide = lax.optimization_barrier((grad, wide))
        part, grad_hidden, branch, grad_triple, logit, rows = run_attention_backward(
            section,
            place,
            grad,
            *parts,
            hidden,
            prob,
            params[section],
            columns[section],
            weights,
            triple,
            x,
            *w_qkv,
            *w_proj,
        )
        narrow = run_attention_grads(
            section, place, n1, grad_triple, branch, attended, n2, logit, rows, *later_narrow
        )
        return grad, between_heads(part), grad_hidden, operands, wide, narrow

    def both_images(first, second):
        mine = jnp.where(leading, first, second)[:SEQ]
        arrived = swapped(jnp.where(leading, second, first))[:SEQ]
        images = jnp.where(leading, jnp.stack([mine, arrived]), jnp.stack([arrived, mine]))
        return images.reshape(1, 2, 1, SEQ, D)

    source = own_image(inputs)
    hidden, mixes, first_operands, stored_first = forward(0, [source], source)
    hidden, mixes, second_operands, stored_second = forward(1, [hidden] + mixes, None)
    middle = stored_second[0]
    last = (hidden + add_up(mixes)).astype(bf16)
    _, parts, grad_hidden, operands, _, narrow = backward(
        1, [own_image(out_grad)], stored_second, None, []
    )
    passed, parts, grad_hidden, _, wide, (mine, send) = backward(
        0, parts + [grad_hidden, middle, params[1]], stored_first, operands, narrow
    )
    wide = lax.psum_scatter(wide, "dp", scatter_dimension=0, tiled=True)
    wide = lax.optimization_barrier(wide).reshape(E, 2, 48, D).astype(f32)
    narrow = (mine.astype(f32) + swapped(send).astype(f32)).astype(bf16)
    narrow, middle, last, passed, parts = lax.optimization_barrier(
        (narrow, middle, last, passed, parts)
    )
    narrow = lax.all_to_all(narrow.reshape(16, 48, WIDE), "dp", 0, 0, tiled=True)
    small = jnp.sum(narrow.astype(f32), axis=0)
    norm1 = add_up(between_heads(small[:, D : D + 2].astype(bf16)))
    entering = run_source_backward(parts, grad_hidden, source, params[0])
    activations = both_images(middle, last)
    input_grads = both_images(entering, passed)
    return (
        activations,
        input_grads,
        norm1[:, 0][None],
        norm1[:, 1][None],
        small[:, : 3 * LOCAL].reshape(48, 3, LOCAL).transpose(1, 0, 2)[None],
        small[:, 3 * LOCAL : D].T[None],
        small[:, D + 2][None],
        small[:, D + 3][None],
        small[:, D + ROUTER_AT : D + ROUTER_AT + E][None],
        wide[:, 0][None],
        wide[:, 1].transpose(0, 2, 1)[None],
    )


def solution(mesh):
    in_specs = (
        P(None, "dp", None, None),
        P(None, "dp", None, None),
        P("pipe", None, "dp", None, None),
        P("pipe", None, "dp", None, None),
        P("pipe", None),
        P("pipe", None),
        P("pipe", None, None, "tensor"),
        P("pipe", "tensor", None),
        P("pipe", None),
        P("pipe", None),
        P("pipe", None, None),
        P("pipe", None, None, "tensor"),
        P("pipe", None, "tensor", None),
    )
    out_specs = (
        P("pipe", None, "dp", None, None),
        P("pipe", None, "dp", None, None),
        P("pipe", "dp"),
        P("pipe", "dp"),
        P("pipe", None, "dp", "tensor"),
        P("pipe", "tensor", "dp"),
        P("pipe", "dp"),
        P("pipe", "dp"),
        P("pipe", "dp", None),
        P("pipe", None, "dp", "tensor"),
        P("pipe", None, "tensor", "dp"),
    )
    return jax.shard_map(
        on_device, mesh=mesh, in_specs=in_specs, out_specs=out_specs, check_vma=False
    )
```

```python
import functools
import math

import jax
import jax.numpy as jnp
from jax import lax
from jax.experimental import pallas as pl
from jax.experimental.pallas import tpu as pltpu
from jax.sharding import PartitionSpec as P

HD = 64
E = 4
SEQ = 197
CAP = 111
ROWS = 208
SLOTS = 112
TABLE = E * SLOTS
D = 768
LOCAL = 192
LANES = 128
WIDE = D + LANES
SPARE = 200
ROUTER_AT = 4
ROUTES_AT = 8
SLOTS_AT = 10

f32 = jnp.float32
bf16 = jnp.bfloat16
eps = 1e-06
VMEM = pl.BlockSpec(memory_space=pltpu.VMEM)
SMEM = pl.BlockSpec(memory_space=pltpu.SMEM)
HBM = pl.BlockSpec(memory_space=pl.ANY)
DMA = pltpu.SemaphoreType.DMA
LIMIT = 60 * 1024 * 1024
SHORT = 28 * 1024 * 1024


def dot(a, b):
    return lax.dot_general(a, b, (((1,), (0,)), ((), ())), preferred_element_type=f32)


def dot_nt(a, b):
    return lax.dot_general(a, b, (((1,), (1,)), ((), ())), preferred_element_type=f32)


def dot_tn(a, b):
    return lax.dot_general(a, b, (((0,), (0,)), ((), ())), preferred_element_type=f32)


def unit_norm(v):
    centred = v - jnp.mean(v, axis=-1, keepdims=True)
    inverse = lax.rsqrt(jnp.mean(centred * centred, axis=-1, keepdims=True) + eps)
    return centred * inverse, inverse


def norm_back(upstream, normed, inverse, gain):
    scaled = upstream * gain
    inner = jnp.mean(scaled * normed, axis=-1, keepdims=True)
    return inverse * (scaled - jnp.mean(scaled, axis=-1, keepdims=True) - normed * inner)


def head_mask(head):
    lane = lax.broadcasted_iota(jnp.int32, (1, LOCAL), 1)
    inside = (lane >= head * HD) & (lane < (head + 1) * HD)
    return jnp.where(inside, 1.0, 0.0).astype(bf16)


def slot_rows(row_ids):
    ids = lax.broadcasted_iota(jnp.int32, (TABLE, ROWS), 0)
    return jnp.where(ids == row_ids, 1.0, 0.0)


def slot_columns(column_ids):
    ids = lax.broadcasted_iota(jnp.int32, (ROWS, TABLE), 1)
    return jnp.where(ids == column_ids, 1.0, 0.0)


def expert_lanes(route):
    lane = lax.broadcasted_iota(jnp.int32, (ROWS, LANES), 1)
    return lane == route + ROUTER_AT


def gate_of(prob, route):
    return jnp.sum(jnp.where(expert_lanes(route), prob, 0.0), axis=-1, keepdims=True)


class Picked:
    def __init__(self, own, other, use_own, held, sem):
        self.copies = [pltpu.make_async_copy(ref, held, sem) for ref in (own, other)]
        self.use_own = use_own

    def start(self):
        pl.when(self.use_own)(self.copies[0].start)
        pl.when(jnp.logical_not(self.use_own))(self.copies[1].start)

    def wait(self):
        self.copies[0].wait()


class Operands:
    def __init__(self, held, out, sems):
        self.held, self.out, self.sems = held, out, sems
        self.copies = []

    def put(self, j, e, value):
        self.held[j, e] = value
        copy = pltpu.make_async_copy(self.held.at[j, e], self.out.at[j, e], self.sems.at[j, e])
        copy.start()
        self.copies.append(copy)

    def wait(self):
        for copy in self.copies:
            copy.wait()


class Kept:
    def __init__(self, outs, held, sems):
        self.outs, self.held, self.sems = outs, held, sems
        self.copies = []

    def put(self, at, value, index=None):
        held, out = self.held[at], self.outs[at]
        if index is not None:
            held, out = held.at[index], out.at[index]
        held[...] = value
        copy = pltpu.make_async_copy(held, out, self.sems.at[len(self.copies)])
        copy.start()
        self.copies.append(copy)

    def wait(self):
        for copy in self.copies:
            copy.wait()


def unit_rows():
    row = lax.broadcasted_iota(jnp.int32, (16, LANES), 0)
    lane = lax.broadcasted_iota(jnp.int32, (16, LANES), 1)
    return jnp.where(row == lane, 1.0, 0.0).astype(bf16)


def add_four(refs):
    a, b, c, d = (ref[...].astype(f32) for ref in refs)
    return (a + b) + (c + d)


def attention_forward(section, place, *refs):
    summed = section == 1
    if summed:
        hidden, *refs = refs
        parts, refs = refs[:4], refs[4:]
    else:
        x_ref, *refs = refs
    params, qkv_own, qkv_other, proj_own, proj_other, *refs = refs
    part, refs = refs[0], refs[1:]
    saved, refs = refs[:4], refs[4:]
    *more, w_qkv, w_proj, sems, held_n1, held_qkv, held_p, held_o, save_sems = refs
    kept = Kept(saved, (held_n1, held_qkv, held_p, held_o), save_sems)
    use_own = place[2] == section
    load_qkv = Picked(qkv_own, qkv_other, use_own, w_qkv, sems.at[0])
    load_proj = Picked(proj_own, proj_other, use_own, w_proj, sems.at[1])
    load_qkv.start()
    load_proj.start()
    if summed:
        source = (hidden[...] + add_four(parts)).astype(bf16)
        more[0][...] = source
    else:
        source = x_ref[...]
    normed, _ = unit_norm(source.astype(f32))
    n1 = (normed * params[0:1] + params[1:2]).astype(bf16)
    kept.put(0, n1)
    load_qkv.wait()
    query, key, value = (dot_nt(n1, w_qkv[j]).astype(bf16) for j in range(3))
    for j, piece in enumerate((query, key, value)):
        kept.put(1, piece, j)
    real = lax.broadcasted_iota(jnp.int32, (1, ROWS), 1) < SEQ
    attended = jnp.zeros((ROWS, LOCAL), f32)
    for head in range(LOCAL // HD):
        mask = head_mask(head)
        scores = dot_nt(query * mask, key) * (1.0 / math.sqrt(HD))
        scores = jnp.where(real, scores, -1e30)
        shifted = jnp.exp(scores - jnp.max(scores, axis=-1, keepdims=True))
        weights = (shifted / jnp.sum(shifted, axis=-1, keepdims=True)).astype(bf16)
        kept.put(2, weights, head)
        attended = attended + dot(weights, value * mask)
    attended = attended.astype(bf16)
    kept.put(3, attended)
    load_proj.wait()
    part[...] = dot(attended, w_proj[...]).astype(bf16)
    kept.wait()


def run_attention_forward(section, place, source, params, w_qkv, w_proj):
    saved = [(ROWS, D), (3, ROWS, LOCAL), (3, ROWS, ROWS), (ROWS, LOCAL)]
    outs = [jax.ShapeDtypeStruct((ROWS, D), bf16)]
    outs += [jax.ShapeDtypeStruct(shape, bf16) for shape in saved]
    if section == 1:
        outs.append(jax.ShapeDtypeStruct((ROWS, D), bf16))
    return pl.pallas_call(
        functools.partial(attention_forward, section),
        out_shape=outs,
        in_specs=[SMEM] + [VMEM] * (len(source) + 1) + [HBM] * 4,
        out_specs=[VMEM] + [HBM] * 4 + [VMEM] * (len(outs) - 5),
        scratch_shapes=[
            pltpu.VMEM((3, LOCAL, D), bf16),
            pltpu.VMEM((LOCAL, D), bf16),
            DMA((2,)),
        ]
        + [pltpu.VMEM(shape, bf16) for shape in saved]
        + [DMA((8,))],
        compiler_params=pltpu.CompilerParams(vmem_limit_bytes=LIMIT),
        cost_estimate=pl.CostEstimate(
            flops=600_000_000, bytes_accessed=4_000_000, transcendentals=130_000
        ),
        name="attention_fwd",
    )(place, *source, params, *w_qkv, *w_proj)


def experts_forward(section, place, *refs):
    x_ref, *refs = refs
    parts, refs = refs[:4], refs[4:]
    params, columns, in_own, in_other, out_own, out_other, *refs = refs
    mix_ref, *refs = refs
    saved, kept_out, refs = refs[:6], refs[6], refs[7:]
    held, refs = refs[:6], refs[6:]
    w_in, w_out, kept, table, in_sem, out_sem, save_sems, keep_sem = refs
    saver = Kept(saved, held, save_sems)
    operands = Operands(kept, kept_out, keep_sem)
    use_own = place[2] == section
    loads_in = []
    loads_out = []
    for e in range(E):
        loads_in.append(
            Picked(in_own.at[e], in_other.at[e], use_own, w_in.at[e], in_sem.at[e])
        )
        loads_out.append(
            Picked(out_own.at[e], out_other.at[e], use_own, w_out.at[e], out_sem.at[e])
        )
    for e in range(E):
        loads_in[e].start()
        loads_out[e].start()
    router = jnp.concatenate([params[...], jnp.zeros((LANES - 16, D), f32)], axis=0)
    router_high = router.astype(bf16)
    router_low = (router - router_high.astype(f32)).astype(bf16)
    lane = lax.broadcasted_iota(jnp.int32, (1, LANES), 1)
    expert_lane = (lane >= ROUTER_AT) & (lane < ROUTER_AT + E)
    hidden = x_ref[...].astype(f32) + add_four(parts)
    saver.put(0, hidden)
    normed, _ = unit_norm(hidden)
    n2 = normed * params[2:3] + params[3:4]
    high = n2.astype(bf16)
    low = (n2 - high.astype(f32)).astype(bf16)
    saver.put(1, high)
    slots = params[SLOTS_AT : SLOTS_AT + 2, :ROWS].astype(jnp.int32)
    spread = (slot_rows(slots[0:1]) + slot_rows(slots[1:2])).astype(bf16)
    rows = dot(spread, high).astype(bf16)
    for e in range(E):
        operands.put(0, e, rows[e * SLOTS : (e + 1) * SLOTS])
    logits = dot_nt(high, router_high) + (dot_nt(low, router_high) + dot_nt(high, router_low))
    logits = jnp.where(expert_lane, logits, -1e30)
    raised = jnp.exp(logits - jnp.max(logits, axis=-1, keepdims=True))
    prob = raised / jnp.sum(raised, axis=-1, keepdims=True)
    saver.put(2, prob)
    curve = math.sqrt(2.0 / math.pi)
    for e in range(E):
        loads_in[e].wait()
        z = dot(kept[0, e], w_in[e])
        square = z * z
        bend = jnp.tanh(curve * z * (1.0 + 0.044715 * square))
        half = 0.5 * (1.0 + bend)
        active = (z * half).astype(bf16)
        operands.put(1, e, active)
        slope = half + (0.5 * curve) * z * (1.0 - bend * bend) * (1.0 + 0.134145 * square)
        saver.put(5, slope.astype(bf16), e)
        loads_out[e].wait()
        table[e * SLOTS : (e + 1) * SLOTS] = dot(active, w_out[e]).astype(bf16)
    mix = jnp.zeros((ROWS, D), f32)
    for k in range(2):
        gate = gate_of(prob, columns[:, k : k + 1])
        picked = dot(slot_columns(columns[:, 2 + k : 3 + k]).astype(bf16), table[...])
        saver.put(3 + k, picked.astype(bf16))
        mix = mix + gate * picked
    mix_ref[...] = mix.astype(bf16)
    saver.wait()
    operands.wait()


def run_experts_forward(section, place, x, parts, params, columns, w_in, w_out):
    saved = [
        ((ROWS, D), f32),
        ((ROWS, D), bf16),
        ((ROWS, LANES), f32),
        ((ROWS, D), bf16),
        ((ROWS, D), bf16),
        ((E, SLOTS, D), bf16),
    ]
    return pl.pallas_call(
        functools.partial(experts_forward, section),
        out_shape=[jax.ShapeDtypeStruct((ROWS, D), bf16)]
        + [jax.ShapeDtypeStruct(*kind) for kind in saved]
        + [jax.ShapeDtypeStruct((2, E, SLOTS, D), bf16)],
        in_specs=[SMEM] + [VMEM] * 7 + [HBM] * 4,
        out_specs=[VMEM] + [HBM] * 7,
        scratch_shapes=[pltpu.VMEM(*kind) for kind in saved]
        + [
            pltpu.VMEM((E, D, D), bf16),
            pltpu.VMEM((E, D, D), bf16),
            pltpu.VMEM((2, E, SLOTS, D), bf16),
            pltpu.VMEM((TABLE, D), bf16),
            DMA((E,)),
            DMA((E,)),
            DMA((5 + E,)),
            DMA((2, E)),
        ],
        compiler_params=pltpu.CompilerParams(vmem_limit_bytes=LIMIT),
        cost_estimate=pl.CostEstimate(
            flops=4_000_000_000, bytes_accessed=16_000_000, transcendentals=400_000
        ),
        name="experts_fwd",
    )(place, x, *parts, params, columns, *w_in, *w_out)


def experts_backward(section, place, *refs):
    if section == 0:
        parts, refs = refs[:4], refs[4:]
        grad_hidden, x_ref, later, *refs = refs
    else:
        grad_ref, *refs = refs
    prob_ref, y0_ref, y1_ref, params, columns, slope_in, *refs = refs
    in_own, in_other, out_own, out_other, partial_ref, kept_out, *refs = refs
    if section == 0:
        passed_ref, *refs = refs
    w_in, w_out, slopes, kept, table, in_sem, out_sem, slope_sem, keep_sem = refs
    operands = Operands(kept, kept_out, keep_sem)
    use_own = place[2] == section
    loads = []
    for e in range(E):
        loads.append(
            (
                Picked(out_own.at[e], out_other.at[e], use_own, w_out.at[e], out_sem.at[e]),
                pltpu.make_async_copy(slope_in.at[e], slopes.at[e], slope_sem.at[e]),
                Picked(in_own.at[e], in_other.at[e], use_own, w_in.at[e], in_sem.at[e]),
            )
        )
        for copy in loads[e]:
            copy.start()
    if section == 0:
        unit, inverse = unit_norm(x_ref[...].astype(f32))
        passed = norm_back(add_four(parts), unit, inverse, later[0:1])
        passed = (grad_hidden[...] + passed).astype(bf16)
        passed_ref[...] = passed
        upstream = passed.astype(f32)
    else:
        upstream = grad_ref[...].astype(f32)
    lane = lax.broadcasted_iota(jnp.int32, (ROWS, LANES), 1)
    slots = params[SLOTS_AT : SLOTS_AT + 2, :ROWS].astype(jnp.int32)
    prob = prob_ref[...]
    rows = jnp.zeros((TABLE, D), f32)
    for k in range(2):
        gate = gate_of(prob, columns[:, k : k + 1])
        weighted = (gate * upstream).astype(bf16)
        rows = rows + dot(slot_rows(slots[k : k + 1]).astype(bf16), weighted)
    rows = rows.astype(bf16)
    for e in range(E):
        operands.put(0, e, rows[e * SLOTS : (e + 1) * SLOTS])
    for e in range(E):
        loads[e][0].wait()
        grad_active = dot_nt(kept[0, e], w_out[e])
        loads[e][1].wait()
        grad_pre = (grad_active * slopes[e].astype(f32)).astype(bf16)
        operands.put(1, e, grad_pre)
        loads[e][2].wait()
        table[e * SLOTS : (e + 1) * SLOTS] = dot_nt(grad_pre, w_in[e]).astype(bf16)
    packed = jnp.zeros((ROWS, LANES), f32)
    for k, picked in enumerate((y0_ref, y1_ref)):
        inner = jnp.sum(upstream * picked[...].astype(f32), axis=-1, keepdims=True)
        high = inner.astype(bf16).astype(f32)
        packed = packed + jnp.where(lane == k, high, 0.0)
        packed = packed + jnp.where(lane == 2 + k, inner - high, 0.0)
    longer = jnp.concatenate([packed, jnp.zeros((D - ROWS, LANES), f32)], axis=0).astype(bf16)
    tail = dot_nt(unit_rows(), longer)[: ROWS - SPARE]
    gather = slot_columns(columns[:, 2:3]) + slot_columns(columns[:, 3:4])
    spread = dot(gather.astype(bf16), table[...])
    partial_ref[...] = jnp.concatenate([spread[:SPARE], tail], axis=0).astype(bf16)
    operands.wait()


def run_experts_backward(
    section, place, grad, prob, y0, y1, params, columns, slope, w_in, w_out
):
    outs = [
        jax.ShapeDtypeStruct((ROWS, D), bf16),
        jax.ShapeDtypeStruct((2, E, SLOTS, D), bf16),
    ]
    if section == 0:
        outs.append(jax.ShapeDtypeStruct((ROWS, D), bf16))
    return pl.pallas_call(
        functools.partial(experts_backward, section),
        out_shape=outs,
        in_specs=[SMEM] + [VMEM] * (len(grad) + 5) + [HBM] * 5,
        out_specs=[VMEM, HBM] + [VMEM] * (len(outs) - 2),
        scratch_shapes=[
            pltpu.VMEM((E, D, D), bf16),
            pltpu.VMEM((E, D, D), bf16),
            pltpu.VMEM((E, SLOTS, D), bf16),
            pltpu.VMEM((2, E, SLOTS, D), bf16),
            pltpu.VMEM((TABLE, D), bf16),
            DMA((E,)),
            DMA((E,)),
            DMA((E,)),
            DMA((2, E)),
        ],
        compiler_params=pltpu.CompilerParams(vmem_limit_bytes=LIMIT),
        cost_estimate=pl.CostEstimate(
            flops=4_000_000_000, bytes_accessed=16_000_000, transcendentals=0
        ),
        name="experts_bwd",
    )(place, *grad, prob, y0, y1, params, columns, slope, *w_in, *w_out)


def attention_backward(
    section,
    place,
    grad_ref,
    p0,
    p1,
    p2,
    p3,
    hidden,
    prob_ref,
    params,
    column,
    weights_ref,
    qkv_ref,
    x_ref,
    qkv_own,
    qkv_other,
    proj_own,
    proj_other,
    part,
    grad_hidden_ref,
    branch_ref,
    triple_ref,
    logit_ref,
    rows_ref,
    w_qkv,
    w_proj,
    sems,
):
    use_own = place[2] == section
    load_qkv = Picked(qkv_own, qkv_other, use_own, w_qkv, sems.at[0])
    load_proj = Picked(proj_own, proj_other, use_own, w_proj, sems.at[1])
    load_proj.start()
    load_qkv.start()
    parts = (p0, p1, p2, p3)
    router = jnp.concatenate([params[...], jnp.zeros((LANES - 16, D), f32)], axis=0)
    upstream = grad_ref[...].astype(f32)
    lane = lax.broadcasted_iota(jnp.int32, (ROWS, LANES), 1)
    arrived = add_four(parts)
    tail = arrived[SPARE:]
    tail_high = tail.astype(bf16)
    tail_low = (tail - tail_high.astype(f32)).astype(bf16)
    tails = jnp.concatenate([tail_high.astype(f32), tail_low.astype(f32)], axis=0).astype(bf16)
    pick = lax.broadcasted_iota(jnp.int32, (16, LANES), 0) % (ROWS - SPARE) == (
        lax.broadcasted_iota(jnp.int32, (16, LANES), 1)
    )
    inner = dot_tn(tails, jnp.where(pick, 1.0, 0.0).astype(bf16))[:ROWS]
    token = lax.broadcasted_iota(jnp.int32, (ROWS, 1), 0)
    arrived = jnp.where(token < SPARE, arrived, 0.0)
    prob = prob_ref[...]
    grad_prob = jnp.zeros((ROWS, LANES), f32)
    for k in range(2):
        mine = (lane == k) | (lane == 2 + k)
        value = jnp.sum(jnp.where(mine, inner, 0.0), axis=-1, keepdims=True)
        grad_prob = grad_prob + jnp.where(expert_lanes(column[:, k : k + 1]), value, 0.0)
    grad_logit = prob * (grad_prob - jnp.sum(prob * grad_prob, axis=-1, keepdims=True))
    grad_logit = grad_logit.astype(bf16)
    logit_ref[...] = grad_logit
    grad_n2 = arrived + dot(grad_logit, router.astype(bf16))
    unit2, inverse2 = unit_norm(hidden[...])
    grad_hidden = upstream + norm_back(grad_n2, unit2, inverse2, params[2:3])
    grad_hidden_ref[...] = grad_hidden
    gain_row = jnp.sum(grad_n2 * unit2, axis=0, keepdims=True)
    bias_row = jnp.sum(grad_n2, axis=0, keepdims=True)
    branch = grad_hidden.astype(bf16)
    branch_ref[...] = branch
    load_proj.wait()
    grad_attended = dot_nt(branch, w_proj[...]).astype(bf16)
    query, key, value = (qkv_ref[j] for j in range(3))
    grad_query = jnp.zeros((ROWS, LOCAL), f32)
    grad_key = jnp.zeros((ROWS, LOCAL), f32)
    grad_value = jnp.zeros((ROWS, LOCAL), f32)
    for head in range(LOCAL // HD):
        mask = head_mask(head)
        weights = weights_ref[head]
        wide = weights.astype(f32)
        arriving = grad_attended * mask
        grad_weights = dot_nt(arriving, value)
        grad_scores = wide * (
            grad_weights - jnp.sum(wide * grad_weights, axis=-1, keepdims=True)
        )
        grad_scores = grad_scores.astype(bf16)
        grad_value = grad_value + dot_tn(weights, arriving)
        grad_query = grad_query + dot(grad_scores, key * mask)
        grad_key = grad_key + dot_tn(grad_scores, query * mask)
    scaling = 1.0 / math.sqrt(HD)
    load_qkv.wait()
    grad_n1 = jnp.zeros((ROWS, D), f32)
    for j, grad in enumerate((grad_query * scaling, grad_key * scaling, grad_value)):
        narrow = grad.astype(bf16)
        triple_ref[j] = narrow
        grad_n1 = grad_n1 + dot(narrow, w_qkv[j])
    part[...] = grad_n1.astype(bf16)
    unit1, _ = unit_norm(x_ref[...].astype(f32))
    first_gain = jnp.sum(grad_n1 * unit1, axis=0, keepdims=True)
    first_bias = jnp.sum(grad_n1, axis=0, keepdims=True)
    ends = [first_gain, first_bias, gain_row, bias_row, jnp.zeros((12, D), f32)]
    rows_ref[...] = jnp.concatenate(ends, axis=0).astype(bf16)


def run_attention_backward(section, place, *operands):
    saved = [(ROWS, D), (3, ROWS, LOCAL), (ROWS, LANES), (16, D)]
    return pl.pallas_call(
        functools.partial(attention_backward, section),
        out_shape=[
            jax.ShapeDtypeStruct((ROWS, D), bf16),
            jax.ShapeDtypeStruct((ROWS, D), f32),
        ]
        + [jax.ShapeDtypeStruct(shape, bf16) for shape in saved],
        in_specs=[SMEM] + [VMEM] * 12 + [HBM] * 4,
        out_specs=[VMEM] * 6,
        scratch_shapes=[
            pltpu.VMEM((3, LOCAL, D), bf16),
            pltpu.VMEM((LOCAL, D), bf16),
            DMA((2,)),
        ],
        compiler_params=pltpu.CompilerParams(vmem_limit_bytes=LIMIT),
        cost_estimate=pl.CostEstimate(
            flops=1_000_000_000, bytes_accessed=6_000_000, transcendentals=0
        ),
        name="attention_bwd",
    )(place, *operands)


def source_backward(p0, p1, p2, p3, grad_hidden, x_ref, params, out):
    unit, inverse = unit_norm(x_ref[...].astype(f32))
    passed = norm_back(add_four((p0, p1, p2, p3)), unit, inverse, params[0:1])
    out[...] = (grad_hidden[...] + passed).astype(bf16)


def run_source_backward(parts, grad_hidden, x, params):
    return pl.pallas_call(
        source_backward,
        out_shape=jax.ShapeDtypeStruct((ROWS, D), bf16),
        in_specs=[VMEM] * 7,
        out_specs=VMEM,
        compiler_params=pltpu.CompilerParams(vmem_limit_bytes=SHORT),
        cost_estimate=pl.CostEstimate(
            flops=6_000_000, bytes_accessed=3_000_000, transcendentals=0
        ),
        name="source_bwd",
    )(*parts, grad_hidden, x, params)


def attention_pieces(n1, triple, branch, attended):
    pieces = [dot_tn(n1[...], triple[j]) for j in range(3)]
    pieces.append(dot_tn(branch[...], attended[...]))
    return jnp.concatenate(pieces, axis=1).astype(bf16)


def small_grads(n2, logit, rows):
    return (dot_tn(n2[...], logit[...]) + dot_tn(rows[...], unit_rows())).astype(bf16)


def expert_grads(place, *refs):
    sets, out, (scr, done, in_sem, out_sem) = (refs[:4], refs[4:8]), refs[8], refs[9:]

    def loads(group, e):
        return [
            pltpu.make_async_copy(
                ref.at[j, e],
                scr.at[2 * (at // 2) + j, e, pl.ds((at % 2) * SLOTS, SLOTS)],
                in_sem.at[e],
            )
            for at, ref in enumerate(group)
            for j in range(2)
        ]

    for section, group in enumerate(sets):

        @pl.when(place[2] == section)
        def _():
            for e in range(E):
                for copy in loads(group, e):
                    copy.start()

    saves = []
    for e in range(E):
        for copy in loads(sets[0], e):
            copy.wait()
        buffer, active, slot_grad, grad_pre = (scr[j, e] for j in range(4))
        for m, grad in enumerate((dot_tn(buffer, grad_pre), dot_tn(slot_grad, active))):
            grad = grad.astype(bf16)
            for j in range(16):
                done[j, 2 * e + m] = grad[j * 48 : (j + 1) * 48]
            saves.append(
                pltpu.make_async_copy(
                    done.at[:, 2 * e + m], out.at[:, 2 * e + m], out_sem.at[2 * e + m]
                )
            )
            saves[-1].start()
    for copy in saves:
        copy.wait()


def run_expert_grads(place, first, second):
    return pl.pallas_call(
        expert_grads,
        out_shape=jax.ShapeDtypeStruct((16, 2 * E, 48, D), bf16),
        in_specs=[SMEM] + [HBM] * 8,
        out_specs=HBM,
        scratch_shapes=[
            pltpu.VMEM((4, E, 2 * SLOTS, D), bf16),
            pltpu.VMEM((16, 2 * E, 48, D), bf16),
            DMA((E,)),
            DMA((2 * E,)),
        ],
        compiler_params=pltpu.CompilerParams(vmem_limit_bytes=LIMIT),
        cost_estimate=pl.CostEstimate(
            flops=2_200_000_000, bytes_accessed=16_000_000, transcendentals=0
        ),
        name="expert_grads",
    )(place, *first, *second)


def attention_grads(section, place, *refs):
    attention, small, refs = refs[:4], refs[4:7], refs[7:]
    wide = jnp.concatenate([attention_pieces(*attention), small_grads(*small)], axis=1)
    if section == 1:
        refs[0][...] = wide
    else:
        other, mine, send = refs
        leading = place[2] == 0
        mine[...] = jnp.where(leading, wide, other[...])
        send[...] = jnp.where(leading, other[...], wide)


def run_attention_grads(section, place, *operands):
    outs = 1 if section == 1 else 2
    return pl.pallas_call(
        functools.partial(attention_grads, section),
        out_shape=[jax.ShapeDtypeStruct((D, WIDE), bf16)] * outs,
        in_specs=[SMEM] + [VMEM] * len(operands),
        out_specs=[VMEM] * outs,
        compiler_params=pltpu.CompilerParams(vmem_limit_bytes=SHORT),
        cost_estimate=pl.CostEstimate(
            flops=400_000_000, bytes_accessed=4_000_000, transcendentals=0
        ),
        name="attention_grads",
    )(place, *operands)


def between_heads(x):
    received = [
        lax.ppermute(x, "tensor", [(i, (i + k) % 4) for i in range(4)]) for k in range(1, 4)
    ]
    return [x] + received


def swapped(x):
    return lax.ppermute(x, "pipe", [(0, 1), (1, 0)])


def add_up(xs):
    a, b, c, d = (x.astype(f32) for x in xs)
    return (a + b) + (c + d)


def on_device(
    inputs,
    out_grad,
    routes,
    positions,
    norm1_gain,
    norm1_bias,
    qkv_weight,
    proj_weight,
    norm2_gain,
    norm2_bias,
    router_weight,
    expert_in,
    expert_out,
):
    core = lax.axis_index("pipe")
    leading = core == 0
    at = lax.axis_index("dp")
    place = jnp.stack([at // 4, at % 4, core]).astype(jnp.int32)

    def own_image(x):
        x = lax.dynamic_index_in_dim(x, core, 0, keepdims=False)
        return jnp.pad(x.reshape(SEQ, D), ((0, ROWS - SEQ), (0, 0)))

    own_qkv = qkv_weight[0].transpose(0, 2, 1)
    w_qkv = (own_qkv, swapped(own_qkv))
    w_proj = (proj_weight[0], swapped(proj_weight[0]))
    route = routes[0].reshape(2, SEQ, 2)
    slot = route * SLOTS + positions[0].reshape(2, SEQ, 2)
    lines = jnp.concatenate([route, slot], axis=-1).transpose(0, 2, 1)
    lines = jnp.pad(lines, ((0, 0), (0, 0), (0, ROWS - SEQ)), constant_values=-64)
    lines = jnp.pad(lines.astype(f32), ((0, 0), (0, 0), (0, D - ROWS)))
    vectors = [norm1_gain, norm1_bias, norm2_gain, norm2_bias, router_weight[0].T]
    rest = jnp.zeros((4, D), f32)

    def packed(image):
        return jnp.concatenate(vectors + [lines[image], rest])

    own = jnp.where(leading, packed(0), packed(1))
    other = swapped(jnp.where(leading, packed(1), packed(0)))
    params = [jnp.where(leading, own, other), jnp.where(leading, other, own)]
    columns = [p[ROUTES_AT : ROUTES_AT + 4, :ROWS].T.astype(jnp.int32) for p in params]
    wait_for = (w_qkv[1], w_proj[1], other)
    own_in, own_out, *_ = lax.optimization_barrier((expert_in[0], expert_out[0], *wait_for))
    w_in = (expert_in[0], swapped(own_in))
    w_out = (expert_out[0], swapped(own_out))

    def forward(section, source, x):
        part, n1, triple, weights, attended, *more = run_attention_forward(
            section, place, source, params[section], w_qkv, w_proj
        )
        x = more[0] if more else x
        mix, hidden, n2, prob, y0, y1, slope, kept = run_experts_forward(
            section, place, x, between_heads(part), params[section], columns[section], w_in, w_out
        )
        stored = (x, n1, triple, weights, attended, hidden, n2, prob, y0, y1, slope)
        return hidden, between_heads(mix), [kept, swapped(kept)], stored

    def backward(section, upstream, stored, later_operands, later_narrow):
        x, n1, triple, weights, attended, hidden, n2, prob, y0, y1, slope = stored
        partial, kept, *more = run_experts_backward(
            section,
            place,
            upstream,
            prob,
            y0,
            y1,
            params[section],
            columns[section],
            slope,
            w_in,
            w_out,
        )
        grad = more[0] if more else upstream[0]
        parts = between_heads(partial)
        operands = [kept, swapped(kept)]
        wide = None
        if section == 0:
            wide = run_expert_grads(
                place, first_operands + operands, second_operands + later_operands
            )
            grad, wide = lax.optimization_barrier((grad, wide))
        part, grad_hidden, branch, grad_triple, logit, rows = run_attention_backward(
            section,
            place,
            grad,
            *parts,
            hidden,
            prob,
            params[section],
            columns[section],
            weights,
            triple,
            x,
            *w_qkv,
            *w_proj,
        )
        narrow = run_attention_grads(
            section, place, n1, grad_triple, branch, attended, n2, logit, rows, *later_narrow
        )
        return grad, between_heads(part), grad_hidden, operands, wide, narrow

    def both_images(first, second):
        mine = jnp.where(leading, first, second)[:SEQ]
        arrived = swapped(jnp.where(leading, second, first))[:SEQ]
        images = jnp.where(leading, jnp.stack([mine, arrived]), jnp.stack([arrived, mine]))
        return images.reshape(1, 2, 1, SEQ, D)

    source = own_image(inputs)
    hidden, mixes, first_operands, stored_first = forward(0, [source], source)
    hidden, mixes, second_operands, stored_second = forward(1, [hidden] + mixes, None)
    middle = stored_second[0]
    last = (hidden + add_up(mixes)).astype(bf16)
    _, parts, grad_hidden, operands, _, narrow = backward(
        1, [own_image(out_grad)], stored_second, None, []
    )
    passed, parts, grad_hidden, _, wide, (mine, send) = backward(
        0, parts + [grad_hidden, middle, params[1]], stored_first, operands, narrow
    )
    wide = lax.psum_scatter(wide, "dp", scatter_dimension=0, tiled=True)
    wide = lax.optimization_barrier(wide).reshape(E, 2, 48, D).astype(f32)
    narrow = (mine.astype(f32) + swapped(send).astype(f32)).astype(bf16)
    narrow, middle, last = lax.optimization_barrier((narrow, middle, last))
    narrow = lax.all_to_all(narrow.reshape(16, 48, WIDE), "dp", 0, 0, tiled=True)
    small = jnp.sum(narrow.astype(f32), axis=0)
    norm1 = add_up(between_heads(small[:, D : D + 2].astype(bf16)))
    entering = run_source_backward(parts, grad_hidden, source, params[0])
    activations = both_images(middle, last)
    input_grads = both_images(entering, passed)
    return (
        activations,
        input_grads,
        norm1[:, 0][None],
        norm1[:, 1][None],
        small[:, : 3 * LOCAL].reshape(48, 3, LOCAL).transpose(1, 0, 2)[None],
        small[:, 3 * LOCAL : D].T[None],
        small[:, D + 2][None],
        small[:, D + 3][None],
        small[:, D + ROUTER_AT : D + ROUTER_AT + E][None],
        wide[:, 0][None],
        wide[:, 1].transpose(0, 2, 1)[None],
    )


def solution(mesh):
    in_specs = (
        P(None, "dp", None, None),
        P(None, "dp", None, None),
        P("pipe", None, "dp", None, None),
        P("pipe", None, "dp", None, None),
        P("pipe", None),
        P("pipe", None),
        P("pipe", None, None, "tensor"),
        P("pipe", "tensor", None),
        P("pipe", None),
        P("pipe", None),
        P("pipe", None, None),
        P("pipe", None, None, "tensor"),
        P("pipe", None, "tensor", None),
    )
    out_specs = (
        P("pipe", None, "dp", None, None),
        P("pipe", None, "dp", None, None),
        P("pipe", "dp"),
        P("pipe", "dp"),
        P("pipe", None, "dp", "tensor"),
        P("pipe", "tensor", "dp"),
        P("pipe", "dp"),
        P("pipe", "dp"),
        P("pipe", "dp", None),
        P("pipe", None, "dp", "tensor"),
        P("pipe", None, "tensor", "dp"),
    )
    return jax.shard_map(
        on_device, mesh=mesh, in_specs=in_specs, out_specs=out_specs, check_vma=False
    )
```

```python
import functools
import math

import jax
import jax.numpy as jnp
from jax import lax
from jax.experimental import pallas as pl
from jax.experimental.pallas import tpu as pltpu
from jax.sharding import PartitionSpec as P

HD = 64
E = 4
SEQ = 197
CAP = 111
ROWS = 208
SLOTS = 112
TABLE = E * SLOTS
D = 768
LOCAL = 192
LANES = 128
WIDE = D + LANES
SPARE = 200
ROUTER_AT = 4
ROUTES_AT = 8
SLOTS_AT = 10

f32 = jnp.float32
bf16 = jnp.bfloat16
eps = 1e-06
VMEM = pl.BlockSpec(memory_space=pltpu.VMEM)
SMEM = pl.BlockSpec(memory_space=pltpu.SMEM)
HBM = pl.BlockSpec(memory_space=pl.ANY)
DMA = pltpu.SemaphoreType.DMA
LIMIT = 60 * 1024 * 1024
SHORT = 28 * 1024 * 1024


def dot(a, b):
    return lax.dot_general(a, b, (((1,), (0,)), ((), ())), preferred_element_type=f32)


def dot_nt(a, b):
    return lax.dot_general(a, b, (((1,), (1,)), ((), ())), preferred_element_type=f32)


def dot_tn(a, b):
    return lax.dot_general(a, b, (((0,), (0,)), ((), ())), preferred_element_type=f32)


def unit_norm(v):
    centred = v - jnp.mean(v, axis=-1, keepdims=True)
    inverse = lax.rsqrt(jnp.mean(centred * centred, axis=-1, keepdims=True) + eps)
    return centred * inverse, inverse


def norm_back(upstream, normed, inverse, gain):
    scaled = upstream * gain
    inner = jnp.mean(scaled * normed, axis=-1, keepdims=True)
    return inverse * (scaled - jnp.mean(scaled, axis=-1, keepdims=True) - normed * inner)


def head_mask(head):
    lane = lax.broadcasted_iota(jnp.int32, (1, LOCAL), 1)
    inside = (lane >= head * HD) & (lane < (head + 1) * HD)
    return jnp.where(inside, 1.0, 0.0).astype(bf16)


def slot_rows(row_ids):
    ids = lax.broadcasted_iota(jnp.int32, (TABLE, ROWS), 0)
    return jnp.where(ids == row_ids, 1.0, 0.0)


def slot_columns(column_ids):
    ids = lax.broadcasted_iota(jnp.int32, (ROWS, TABLE), 1)
    return jnp.where(ids == column_ids, 1.0, 0.0)


def expert_lanes(route):
    lane = lax.broadcasted_iota(jnp.int32, (ROWS, LANES), 1)
    return lane == route + ROUTER_AT


def gate_of(prob, route):
    return jnp.sum(jnp.where(expert_lanes(route), prob, 0.0), axis=-1, keepdims=True)


class Picked:
    def __init__(self, own, other, use_own, held, sem):
        self.copies = [pltpu.make_async_copy(ref, held, sem) for ref in (own, other)]
        self.use_own = use_own

    def start(self):
        pl.when(self.use_own)(self.copies[0].start)
        pl.when(jnp.logical_not(self.use_own))(self.copies[1].start)

    def wait(self):
        self.copies[0].wait()


class Operands:
    def __init__(self, held, out, sems):
        self.held, self.out, self.sems = held, out, sems
        self.copies = []

    def put(self, j, e, value):
        self.held[j, e] = value
        copy = pltpu.make_async_copy(self.held.at[j, e], self.out.at[j, e], self.sems.at[j, e])
        copy.start()
        self.copies.append(copy)

    def wait(self):
        for copy in self.copies:
            copy.wait()


class Kept:
    def __init__(self, outs, held, sems):
        self.outs, self.held, self.sems = outs, held, sems
        self.copies = []

    def put(self, at, value, index=None):
        held, out = self.held[at], self.outs[at]
        if index is not None:
            held, out = held.at[index], out.at[index]
        held[...] = value
        copy = pltpu.make_async_copy(held, out, self.sems.at[len(self.copies)])
        copy.start()
        self.copies.append(copy)

    def wait(self):
        for copy in self.copies:
            copy.wait()


def unit_rows():
    row = lax.broadcasted_iota(jnp.int32, (16, LANES), 0)
    lane = lax.broadcasted_iota(jnp.int32, (16, LANES), 1)
    return jnp.where(row == lane, 1.0, 0.0).astype(bf16)


def add_four(refs):
    a, b, c, d = (ref[...].astype(f32) for ref in refs)
    return (a + b) + (c + d)


def attention_forward(section, place, *refs):
    summed = section == 1
    if summed:
        hidden, *refs = refs
        parts, refs = refs[:4], refs[4:]
    else:
        x_ref, *refs = refs
    params, qkv_own, qkv_other, proj_own, proj_other, *refs = refs
    part, refs = refs[0], refs[1:]
    saved, refs = refs[:4], refs[4:]
    *more, w_qkv, w_proj, sems, held_n1, held_qkv, held_p, held_o, save_sems = refs
    kept = Kept(saved, (held_n1, held_qkv, held_p, held_o), save_sems)
    use_own = place[2] == section
    load_qkv = Picked(qkv_own, qkv_other, use_own, w_qkv, sems.at[0])
    load_proj = Picked(proj_own, proj_other, use_own, w_proj, sems.at[1])
    load_qkv.start()
    load_proj.start()
    if summed:
        source = (hidden[...] + add_four(parts)).astype(bf16)
        more[0][...] = source
    else:
        source = x_ref[...]
    normed, _ = unit_norm(source.astype(f32))
    n1 = (normed * params[0:1] + params[1:2]).astype(bf16)
    kept.put(0, n1)
    load_qkv.wait()
    query, key, value = (dot_nt(n1, w_qkv[j]).astype(bf16) for j in range(3))
    for j, piece in enumerate((query, key, value)):
        kept.put(1, piece, j)
    real = lax.broadcasted_iota(jnp.int32, (1, ROWS), 1) < SEQ
    attended = jnp.zeros((ROWS, LOCAL), f32)
    for head in range(LOCAL // HD):
        mask = head_mask(head)
        scores = dot_nt(query * mask, key) * (1.0 / math.sqrt(HD))
        scores = jnp.where(real, scores, -1e30)
        shifted = jnp.exp(scores - jnp.max(scores, axis=-1, keepdims=True))
        weights = (shifted / jnp.sum(shifted, axis=-1, keepdims=True)).astype(bf16)
        kept.put(2, weights, head)
        attended = attended + dot(weights, value * mask)
    attended = attended.astype(bf16)
    kept.put(3, attended)
    load_proj.wait()
    part[...] = dot(attended, w_proj[...]).astype(bf16)
    kept.wait()


def run_attention_forward(section, place, source, params, w_qkv, w_proj):
    saved = [(ROWS, D), (3, ROWS, LOCAL), (3, ROWS, ROWS), (ROWS, LOCAL)]
    outs = [jax.ShapeDtypeStruct((ROWS, D), bf16)]
    outs += [jax.ShapeDtypeStruct(shape, bf16) for shape in saved]
    if section == 1:
        outs.append(jax.ShapeDtypeStruct((ROWS, D), bf16))
    return pl.pallas_call(
        functools.partial(attention_forward, section),
        out_shape=outs,
        in_specs=[SMEM] + [VMEM] * (len(source) + 1) + [HBM] * 4,
        out_specs=[VMEM] + [HBM] * 4 + [VMEM] * (len(outs) - 5),
        scratch_shapes=[
            pltpu.VMEM((3, LOCAL, D), bf16),
            pltpu.VMEM((LOCAL, D), bf16),
            DMA((2,)),
        ]
        + [pltpu.VMEM(shape, bf16) for shape in saved]
        + [DMA((8,))],
        compiler_params=pltpu.CompilerParams(vmem_limit_bytes=LIMIT),
        cost_estimate=pl.CostEstimate(
            flops=600_000_000, bytes_accessed=4_000_000, transcendentals=130_000
        ),
        name="attention_fwd",
    )(place, *source, params, *w_qkv, *w_proj)


def experts_forward(section, place, *refs):
    x_ref, *refs = refs
    parts, refs = refs[:4], refs[4:]
    params, columns, in_own, in_other, out_own, out_other, *refs = refs
    mix_ref, *refs = refs
    saved, kept_out, refs = refs[:6], refs[6], refs[7:]
    held, refs = refs[:6], refs[6:]
    w_in, w_out, kept, table, in_sem, out_sem, save_sems, keep_sem = refs
    saver = Kept(saved, held, save_sems)
    operands = Operands(kept, kept_out, keep_sem)
    use_own = place[2] == section
    loads_in = []
    loads_out = []
    for e in range(E):
        loads_in.append(
            Picked(in_own.at[e], in_other.at[e], use_own, w_in.at[e], in_sem.at[e])
        )
        loads_out.append(
            Picked(out_own.at[e], out_other.at[e], use_own, w_out.at[e], out_sem.at[e])
        )
    for e in range(E):
        loads_in[e].start()
        loads_out[e].start()
    router = jnp.concatenate([params[...], jnp.zeros((LANES - 16, D), f32)], axis=0)
    router_high = router.astype(bf16)
    router_low = (router - router_high.astype(f32)).astype(bf16)
    lane = lax.broadcasted_iota(jnp.int32, (1, LANES), 1)
    expert_lane = (lane >= ROUTER_AT) & (lane < ROUTER_AT + E)
    hidden = x_ref[...].astype(f32) + add_four(parts)
    saver.put(0, hidden)
    normed, _ = unit_norm(hidden)
    n2 = normed * params[2:3] + params[3:4]
    high = n2.astype(bf16)
    low = (n2 - high.astype(f32)).astype(bf16)
    saver.put(1, high)
    slots = params[SLOTS_AT : SLOTS_AT + 2, :ROWS].astype(jnp.int32)
    spread = (slot_rows(slots[0:1]) + slot_rows(slots[1:2])).astype(bf16)
    rows = dot(spread, high).astype(bf16)
    for e in range(E):
        operands.put(0, e, rows[e * SLOTS : (e + 1) * SLOTS])
    logits = dot_nt(high, router_high) + (dot_nt(low, router_high) + dot_nt(high, router_low))
    logits = jnp.where(expert_lane, logits, -1e30)
    raised = jnp.exp(logits - jnp.max(logits, axis=-1, keepdims=True))
    prob = raised / jnp.sum(raised, axis=-1, keepdims=True)
    saver.put(2, prob)
    curve = math.sqrt(2.0 / math.pi)
    for e in range(E):
        loads_in[e].wait()
        z = dot(kept[0, e], w_in[e])
        square = z * z
        bend = jnp.tanh(curve * z * (1.0 + 0.044715 * square))
        half = 0.5 * (1.0 + bend)
        active = (z * half).astype(bf16)
        operands.put(1, e, active)
        slope = half + (0.5 * curve) * z * (1.0 - bend * bend) * (1.0 + 0.134145 * square)
        saver.put(5, slope.astype(bf16), e)
        loads_out[e].wait()
        table[e * SLOTS : (e + 1) * SLOTS] = dot(active, w_out[e]).astype(bf16)
    mix = jnp.zeros((ROWS, D), f32)
    for k in range(2):
        gate = gate_of(prob, columns[:, k : k + 1])
        picked = dot(slot_columns(columns[:, 2 + k : 3 + k]).astype(bf16), table[...])
        saver.put(3 + k, picked.astype(bf16))
        mix = mix + gate * picked
    mix_ref[...] = mix.astype(bf16)
    saver.wait()
    operands.wait()


def run_experts_forward(section, place, x, parts, params, columns, w_in, w_out):
    saved = [
        ((ROWS, D), f32),
        ((ROWS, D), bf16),
        ((ROWS, LANES), f32),
        ((ROWS, D), bf16),
        ((ROWS, D), bf16),
        ((E, SLOTS, D), bf16),
    ]
    return pl.pallas_call(
        functools.partial(experts_forward, section),
        out_shape=[jax.ShapeDtypeStruct((ROWS, D), bf16)]
        + [jax.ShapeDtypeStruct(*kind) for kind in saved]
        + [jax.ShapeDtypeStruct((2, E, SLOTS, D), bf16)],
        in_specs=[SMEM] + [VMEM] * 7 + [HBM] * 4,
        out_specs=[VMEM] + [HBM] * 7,
        scratch_shapes=[pltpu.VMEM(*kind) for kind in saved]
        + [
            pltpu.VMEM((E, D, D), bf16),
            pltpu.VMEM((E, D, D), bf16),
            pltpu.VMEM((2, E, SLOTS, D), bf16),
            pltpu.VMEM((TABLE, D), bf16),
            DMA((E,)),
            DMA((E,)),
            DMA((5 + E,)),
            DMA((2, E)),
        ],
        compiler_params=pltpu.CompilerParams(vmem_limit_bytes=LIMIT),
        cost_estimate=pl.CostEstimate(
            flops=4_000_000_000, bytes_accessed=16_000_000, transcendentals=400_000
        ),
        name="experts_fwd",
    )(place, x, *parts, params, columns, *w_in, *w_out)


def experts_backward(section, place, *refs):
    if section == 0:
        parts, refs = refs[:4], refs[4:]
        grad_hidden, x_ref, later, *refs = refs
    else:
        grad_ref, *refs = refs
    prob_ref, y0_ref, y1_ref, params, columns, slope_in, *refs = refs
    in_own, in_other, out_own, out_other, partial_ref, kept_out, *refs = refs
    if section == 0:
        passed_ref, *refs = refs
    w_in, w_out, slopes, kept, table, in_sem, out_sem, slope_sem, keep_sem = refs
    operands = Operands(kept, kept_out, keep_sem)
    use_own = place[2] == section
    loads = []
    for e in range(E):
        loads.append(
            (
                Picked(out_own.at[e], out_other.at[e], use_own, w_out.at[e], out_sem.at[e]),
                pltpu.make_async_copy(slope_in.at[e], slopes.at[e], slope_sem.at[e]),
                Picked(in_own.at[e], in_other.at[e], use_own, w_in.at[e], in_sem.at[e]),
            )
        )
        for copy in loads[e]:
            copy.start()
    if section == 0:
        unit, inverse = unit_norm(x_ref[...].astype(f32))
        passed = norm_back(add_four(parts), unit, inverse, later[0:1])
        passed = (grad_hidden[...] + passed).astype(bf16)
        passed_ref[...] = passed
        upstream = passed.astype(f32)
    else:
        upstream = grad_ref[...].astype(f32)
    lane = lax.broadcasted_iota(jnp.int32, (ROWS, LANES), 1)
    slots = params[SLOTS_AT : SLOTS_AT + 2, :ROWS].astype(jnp.int32)
    prob = prob_ref[...]
    rows = jnp.zeros((TABLE, D), f32)
    for k in range(2):
        gate = gate_of(prob, columns[:, k : k + 1])
        weighted = (gate * upstream).astype(bf16)
        rows = rows + dot(slot_rows(slots[k : k + 1]).astype(bf16), weighted)
    rows = rows.astype(bf16)
    for e in range(E):
        operands.put(0, e, rows[e * SLOTS : (e + 1) * SLOTS])
    for e in range(E):
        loads[e][0].wait()
        grad_active = dot_nt(kept[0, e], w_out[e])
        loads[e][1].wait()
        grad_pre = (grad_active * slopes[e].astype(f32)).astype(bf16)
        operands.put(1, e, grad_pre)
        loads[e][2].wait()
        table[e * SLOTS : (e + 1) * SLOTS] = dot_nt(grad_pre, w_in[e]).astype(bf16)
    packed = jnp.zeros((ROWS, LANES), f32)
    for k, picked in enumerate((y0_ref, y1_ref)):
        inner = jnp.sum(upstream * picked[...].astype(f32), axis=-1, keepdims=True)
        high = inner.astype(bf16).astype(f32)
        packed = packed + jnp.where(lane == k, high, 0.0)
        packed = packed + jnp.where(lane == 2 + k, inner - high, 0.0)
    longer = jnp.concatenate([packed, jnp.zeros((D - ROWS, LANES), f32)], axis=0).astype(bf16)
    tail = dot_nt(unit_rows(), longer)[: ROWS - SPARE]
    gather = slot_columns(columns[:, 2:3]) + slot_columns(columns[:, 3:4])
    spread = dot(gather.astype(bf16), table[...])
    partial_ref[...] = jnp.concatenate([spread[:SPARE], tail], axis=0).astype(bf16)
    operands.wait()


def run_experts_backward(
    section, place, grad, prob, y0, y1, params, columns, slope, w_in, w_out
):
    outs = [
        jax.ShapeDtypeStruct((ROWS, D), bf16),
        jax.ShapeDtypeStruct((2, E, SLOTS, D), bf16),
    ]
    if section == 0:
        outs.append(jax.ShapeDtypeStruct((ROWS, D), bf16))
    return pl.pallas_call(
        functools.partial(experts_backward, section),
        out_shape=outs,
        in_specs=[SMEM] + [VMEM] * (len(grad) + 5) + [HBM] * 5,
        out_specs=[VMEM, HBM] + [VMEM] * (len(outs) - 2),
        scratch_shapes=[
            pltpu.VMEM((E, D, D), bf16),
            pltpu.VMEM((E, D, D), bf16),
            pltpu.VMEM((E, SLOTS, D), bf16),
            pltpu.VMEM((2, E, SLOTS, D), bf16),
            pltpu.VMEM((TABLE, D), bf16),
            DMA((E,)),
            DMA((E,)),
            DMA((E,)),
            DMA((2, E)),
        ],
        compiler_params=pltpu.CompilerParams(vmem_limit_bytes=LIMIT),
        cost_estimate=pl.CostEstimate(
            flops=4_000_000_000, bytes_accessed=16_000_000, transcendentals=0
        ),
        name="experts_bwd",
    )(place, *grad, prob, y0, y1, params, columns, slope, *w_in, *w_out)


def attention_backward(
    section,
    place,
    grad_ref,
    p0,
    p1,
    p2,
    p3,
    hidden,
    prob_ref,
    params,
    column,
    weights_ref,
    qkv_ref,
    x_ref,
    qkv_own,
    qkv_other,
    proj_own,
    proj_other,
    part,
    grad_hidden_ref,
    branch_ref,
    triple_ref,
    logit_ref,
    rows_ref,
    w_qkv,
    w_proj,
    sems,
):
    use_own = place[2] == section
    load_qkv = Picked(qkv_own, qkv_other, use_own, w_qkv, sems.at[0])
    load_proj = Picked(proj_own, proj_other, use_own, w_proj, sems.at[1])
    load_proj.start()
    load_qkv.start()
    parts = (p0, p1, p2, p3)
    router = jnp.concatenate([params[...], jnp.zeros((LANES - 16, D), f32)], axis=0)
    upstream = grad_ref[...].astype(f32)
    lane = lax.broadcasted_iota(jnp.int32, (ROWS, LANES), 1)
    arrived = add_four(parts)
    tail = arrived[SPARE:]
    tail_high = tail.astype(bf16)
    tail_low = (tail - tail_high.astype(f32)).astype(bf16)
    tails = jnp.concatenate([tail_high.astype(f32), tail_low.astype(f32)], axis=0).astype(bf16)
    pick = lax.broadcasted_iota(jnp.int32, (16, LANES), 0) % (ROWS - SPARE) == (
        lax.broadcasted_iota(jnp.int32, (16, LANES), 1)
    )
    inner = dot_tn(tails, jnp.where(pick, 1.0, 0.0).astype(bf16))[:ROWS]
    token = lax.broadcasted_iota(jnp.int32, (ROWS, 1), 0)
    arrived = jnp.where(token < SPARE, arrived, 0.0)
    prob = prob_ref[...]
    grad_prob = jnp.zeros((ROWS, LANES), f32)
    for k in range(2):
        mine = (lane == k) | (lane == 2 + k)
        value = jnp.sum(jnp.where(mine, inner, 0.0), axis=-1, keepdims=True)
        grad_prob = grad_prob + jnp.where(expert_lanes(column[:, k : k + 1]), value, 0.0)
    grad_logit = prob * (grad_prob - jnp.sum(prob * grad_prob, axis=-1, keepdims=True))
    grad_logit = grad_logit.astype(bf16)
    logit_ref[...] = grad_logit
    grad_n2 = arrived + dot(grad_logit, router.astype(bf16))
    unit2, inverse2 = unit_norm(hidden[...])
    grad_hidden = upstream + norm_back(grad_n2, unit2, inverse2, params[2:3])
    grad_hidden_ref[...] = grad_hidden
    gain_row = jnp.sum(grad_n2 * unit2, axis=0, keepdims=True)
    bias_row = jnp.sum(grad_n2, axis=0, keepdims=True)
    branch = grad_hidden.astype(bf16)
    branch_ref[...] = branch
    load_proj.wait()
    grad_attended = dot_nt(branch, w_proj[...]).astype(bf16)
    query, key, value = (qkv_ref[j] for j in range(3))
    grad_query = jnp.zeros((ROWS, LOCAL), f32)
    grad_key = jnp.zeros((ROWS, LOCAL), f32)
    grad_value = jnp.zeros((ROWS, LOCAL), f32)
    for head in range(LOCAL // HD):
        mask = head_mask(head)
        weights = weights_ref[head]
        wide = weights.astype(f32)
        arriving = grad_attended * mask
        grad_weights = dot_nt(arriving, value)
        grad_scores = wide * (
            grad_weights - jnp.sum(wide * grad_weights, axis=-1, keepdims=True)
        )
        grad_scores = grad_scores.astype(bf16)
        grad_value = grad_value + dot_tn(weights, arriving)
        grad_query = grad_query + dot(grad_scores, key * mask)
        grad_key = grad_key + dot_tn(grad_scores, query * mask)
    scaling = 1.0 / math.sqrt(HD)
    load_qkv.wait()
    grad_n1 = jnp.zeros((ROWS, D), f32)
    for j, grad in enumerate((grad_query * scaling, grad_key * scaling, grad_value)):
        narrow = grad.astype(bf16)
        triple_ref[j] = narrow
        grad_n1 = grad_n1 + dot(narrow, w_qkv[j])
    part[...] = grad_n1.astype(bf16)
    unit1, _ = unit_norm(x_ref[...].astype(f32))
    first_gain = jnp.sum(grad_n1 * unit1, axis=0, keepdims=True)
    first_bias = jnp.sum(grad_n1, axis=0, keepdims=True)
    ends = [first_gain, first_bias, gain_row, bias_row, jnp.zeros((12, D), f32)]
    rows_ref[...] = jnp.concatenate(ends, axis=0).astype(bf16)


def run_attention_backward(section, place, *operands):
    saved = [(ROWS, D), (3, ROWS, LOCAL), (ROWS, LANES), (16, D)]
    return pl.pallas_call(
        functools.partial(attention_backward, section),
        out_shape=[
            jax.ShapeDtypeStruct((ROWS, D), bf16),
            jax.ShapeDtypeStruct((ROWS, D), f32),
        ]
        + [jax.ShapeDtypeStruct(shape, bf16) for shape in saved],
        in_specs=[SMEM] + [VMEM] * 12 + [HBM] * 4,
        out_specs=[VMEM] * 6,
        scratch_shapes=[
            pltpu.VMEM((3, LOCAL, D), bf16),
            pltpu.VMEM((LOCAL, D), bf16),
            DMA((2,)),
        ],
        compiler_params=pltpu.CompilerParams(vmem_limit_bytes=LIMIT),
        cost_estimate=pl.CostEstimate(
            flops=1_000_000_000, bytes_accessed=6_000_000, transcendentals=0
        ),
        name="attention_bwd",
    )(place, *operands)


def source_backward(p0, p1, p2, p3, grad_hidden, x_ref, params, out):
    unit, inverse = unit_norm(x_ref[...].astype(f32))
    passed = norm_back(add_four((p0, p1, p2, p3)), unit, inverse, params[0:1])
    out[...] = (grad_hidden[...] + passed).astype(bf16)


def run_source_backward(parts, grad_hidden, x, params):
    return pl.pallas_call(
        source_backward,
        out_shape=jax.ShapeDtypeStruct((ROWS, D), bf16),
        in_specs=[VMEM] * 7,
        out_specs=VMEM,
        compiler_params=pltpu.CompilerParams(vmem_limit_bytes=SHORT),
        cost_estimate=pl.CostEstimate(
            flops=6_000_000, bytes_accessed=3_000_000, transcendentals=0
        ),
        name="source_bwd",
    )(*parts, grad_hidden, x, params)


def attention_pieces(n1, triple, branch, attended):
    pieces = [dot_tn(n1[...], triple[j]) for j in range(3)]
    pieces.append(dot_tn(branch[...], attended[...]))
    return jnp.concatenate(pieces, axis=1).astype(bf16)


def small_grads(n2, logit, rows):
    return (dot_tn(n2[...], logit[...]) + dot_tn(rows[...], unit_rows())).astype(bf16)


def expert_grads(place, *refs):
    sets, out, (scr, done, in_sem, out_sem) = (refs[:4], refs[4:8]), refs[8], refs[9:]

    def loads(group, e):
        return [
            pltpu.make_async_copy(
                ref.at[j, e],
                scr.at[2 * (at // 2) + j, e, pl.ds((at % 2) * SLOTS, SLOTS)],
                in_sem.at[e],
            )
            for at, ref in enumerate(group)
            for j in range(2)
        ]

    for section, group in enumerate(sets):

        @pl.when(place[2] == section)
        def _():
            for e in range(E):
                for copy in loads(group, e):
                    copy.start()

    saves = []
    for e in range(E):
        for copy in loads(sets[0], e):
            copy.wait()
        buffer, active, slot_grad, grad_pre = (scr[j, e] for j in range(4))
        for m, grad in enumerate((dot_tn(buffer, grad_pre), dot_tn(slot_grad, active))):
            grad = grad.astype(bf16)
            for j in range(16):
                done[j, 2 * e + m] = grad[j * 48 : (j + 1) * 48]
            saves.append(
                pltpu.make_async_copy(
                    done.at[:, 2 * e + m], out.at[:, 2 * e + m], out_sem.at[2 * e + m]
                )
            )
            saves[-1].start()
    for copy in saves:
        copy.wait()


def run_expert_grads(place, first, second):
    return pl.pallas_call(
        expert_grads,
        out_shape=jax.ShapeDtypeStruct((16, 2 * E, 48, D), bf16),
        in_specs=[SMEM] + [HBM] * 8,
        out_specs=HBM,
        scratch_shapes=[
            pltpu.VMEM((4, E, 2 * SLOTS, D), bf16),
            pltpu.VMEM((16, 2 * E, 48, D), bf16),
            DMA((E,)),
            DMA((2 * E,)),
        ],
        compiler_params=pltpu.CompilerParams(vmem_limit_bytes=LIMIT),
        cost_estimate=pl.CostEstimate(
            flops=2_200_000_000, bytes_accessed=16_000_000, transcendentals=0
        ),
        name="expert_grads",
    )(place, *first, *second)


def attention_grads(section, place, *refs):
    attention, small, refs = refs[:4], refs[4:7], refs[7:]
    wide = jnp.concatenate([attention_pieces(*attention), small_grads(*small)], axis=1)
    if section == 1:
        refs[0][...] = wide
    else:
        other, mine, send = refs
        leading = place[2] == 0
        mine[...] = jnp.where(leading, wide, other[...])
        send[...] = jnp.where(leading, other[...], wide)


def run_attention_grads(section, place, *operands):
    outs = 1 if section == 1 else 2
    return pl.pallas_call(
        functools.partial(attention_grads, section),
        out_shape=[jax.ShapeDtypeStruct((D, WIDE), bf16)] * outs,
        in_specs=[SMEM] + [VMEM] * len(operands),
        out_specs=[VMEM] * outs,
        compiler_params=pltpu.CompilerParams(vmem_limit_bytes=SHORT),
        cost_estimate=pl.CostEstimate(
            flops=400_000_000, bytes_accessed=4_000_000, transcendentals=0
        ),
        name="attention_grads",
    )(place, *operands)


def between_heads(x):
    received = [
        lax.ppermute(x, "tensor", [(i, (i + k) % 4) for i in range(4)]) for k in range(1, 4)
    ]
    return [x] + received


def swapped(x):
    return lax.ppermute(x, "pipe", [(0, 1), (1, 0)])


def add_up(xs):
    a, b, c, d = (x.astype(f32) for x in xs)
    return (a + b) + (c + d)


def on_device(
    inputs,
    out_grad,
    routes,
    positions,
    norm1_gain,
    norm1_bias,
    qkv_weight,
    proj_weight,
    norm2_gain,
    norm2_bias,
    router_weight,
    expert_in,
    expert_out,
):
    core = lax.axis_index("pipe")
    leading = core == 0
    at = lax.axis_index("dp")
    place = jnp.stack([at // 4, at % 4, core]).astype(jnp.int32)

    def own_image(x):
        x = lax.dynamic_index_in_dim(x, core, 0, keepdims=False)
        return jnp.pad(x.reshape(SEQ, D), ((0, ROWS - SEQ), (0, 0)))

    own_qkv = qkv_weight[0].transpose(0, 2, 1)
    w_qkv = (own_qkv, swapped(own_qkv))
    w_proj = (proj_weight[0], swapped(proj_weight[0]))
    route = routes[0].reshape(2, SEQ, 2)
    slot = route * SLOTS + positions[0].reshape(2, SEQ, 2)
    lines = jnp.concatenate([route, slot], axis=-1).transpose(0, 2, 1)
    lines = jnp.pad(lines, ((0, 0), (0, 0), (0, ROWS - SEQ)), constant_values=-64)
    lines = jnp.pad(lines.astype(f32), ((0, 0), (0, 0), (0, D - ROWS)))
    vectors = [norm1_gain, norm1_bias, norm2_gain, norm2_bias, router_weight[0].T]
    rest = jnp.zeros((4, D), f32)

    def packed(image):
        return jnp.concatenate(vectors + [lines[image], rest])

    own = jnp.where(leading, packed(0), packed(1))
    other = swapped(jnp.where(leading, packed(1), packed(0)))
    params = [jnp.where(leading, own, other), jnp.where(leading, other, own)]
    columns = [p[ROUTES_AT : ROUTES_AT + 4, :ROWS].T.astype(jnp.int32) for p in params]
    wait_for = (w_qkv[1], w_proj[1], other)
    own_in, own_out, *_ = lax.optimization_barrier((expert_in[0], expert_out[0], *wait_for))
    w_in = (expert_in[0], swapped(own_in))
    w_out = (expert_out[0], swapped(own_out))

    def forward(section, source, x):
        part, n1, triple, weights, attended, *more = run_attention_forward(
            section, place, source, params[section], w_qkv, w_proj
        )
        x = more[0] if more else x
        mix, hidden, n2, prob, y0, y1, slope, kept = run_experts_forward(
            section, place, x, between_heads(part), params[section], columns[section], w_in, w_out
        )
        stored = (x, n1, triple, weights, attended, hidden, n2, prob, y0, y1, slope)
        return hidden, between_heads(mix), [kept, swapped(kept)], stored

    def backward(section, upstream, stored, later_operands, later_narrow):
        x, n1, triple, weights, attended, hidden, n2, prob, y0, y1, slope = stored
        partial, kept, *more = run_experts_backward(
            section,
            place,
            upstream,
            prob,
            y0,
            y1,
            params[section],
            columns[section],
            slope,
            w_in,
            w_out,
        )
        grad = more[0] if more else upstream[0]
        parts = between_heads(partial)
        operands = [kept, swapped(kept)]
        wide = None
        if section == 0:
            wide = run_expert_grads(
                place, first_operands + operands, second_operands + later_operands
            )
            grad, wide = lax.optimization_barrier((grad, wide))
        part, grad_hidden, branch, grad_triple, logit, rows = run_attention_backward(
            section,
            place,
            grad,
            *parts,
            hidden,
            prob,
            params[section],
            columns[section],
            weights,
            triple,
            x,
            *w_qkv,
            *w_proj,
        )
        narrow = run_attention_grads(
            section, place, n1, grad_triple, branch, attended, n2, logit, rows, *later_narrow
        )
        return grad, between_heads(part), grad_hidden, operands, wide, narrow

    def both_images(first, second):
        mine = jnp.where(leading, first, second)[:SEQ]
        arrived = swapped(jnp.where(leading, second, first))[:SEQ]
        images = jnp.where(leading, jnp.stack([mine, arrived]), jnp.stack([arrived, mine]))
        return images.reshape(1, 2, 1, SEQ, D)

    source = own_image(inputs)
    hidden, mixes, first_operands, stored_first = forward(0, [source], source)
    hidden, mixes, second_operands, stored_second = forward(1, [hidden] + mixes, None)
    middle = stored_second[0]
    last = (hidden + add_up(mixes)).astype(bf16)
    _, parts, grad_hidden, operands, _, narrow = backward(
        1, [own_image(out_grad)], stored_second, None, []
    )
    activations = both_images(middle, last)
    parts, activations = lax.optimization_barrier((parts, activations))
    passed, parts, grad_hidden, _, wide, (mine, send) = backward(
        0, parts + [grad_hidden, middle, params[1]], stored_first, operands, narrow
    )
    wide = lax.psum_scatter(wide, "dp", scatter_dimension=0, tiled=True)
    wide = lax.optimization_barrier(wide).reshape(E, 2, 48, D).astype(f32)
    narrow = (mine.astype(f32) + swapped(send).astype(f32)).astype(bf16)
    narrow = lax.all_to_all(narrow.reshape(16, 48, WIDE), "dp", 0, 0, tiled=True)
    small = jnp.sum(narrow.astype(f32), axis=0)
    norm1 = add_up(between_heads(small[:, D : D + 2].astype(bf16)))
    entering = run_source_backward(parts, grad_hidden, source, params[0])
    input_grads = both_images(entering, passed)
    return (
        activations,
        input_grads,
        norm1[:, 0][None],
        norm1[:, 1][None],
        small[:, : 3 * LOCAL].reshape(48, 3, LOCAL).transpose(1, 0, 2)[None],
        small[:, 3 * LOCAL : D].T[None],
        small[:, D + 2][None],
        small[:, D + 3][None],
        small[:, D + ROUTER_AT : D + ROUTER_AT + E][None],
        wide[:, 0][None],
        wide[:, 1].transpose(0, 2, 1)[None],
    )


def solution(mesh):
    in_specs = (
        P(None, "dp", None, None),
        P(None, "dp", None, None),
        P("pipe", None, "dp", None, None),
        P("pipe", None, "dp", None, None),
        P("pipe", None),
        P("pipe", None),
        P("pipe", None, None, "tensor"),
        P("pipe", "tensor", None),
        P("pipe", None),
        P("pipe", None),
        P("pipe", None, None),
        P("pipe", None, None, "tensor"),
        P("pipe", None, "tensor", None),
    )
    out_specs = (
        P("pipe", None, "dp", None, None),
        P("pipe", None, "dp", None, None),
        P("pipe", "dp"),
        P("pipe", "dp"),
        P("pipe", None, "dp", "tensor"),
        P("pipe", "tensor", "dp"),
        P("pipe", "dp"),
        P("pipe", "dp"),
        P("pipe", "dp", None),
        P("pipe", None, "dp", "tensor"),
        P("pipe", None, "tensor", "dp"),
    )
    return jax.shard_map(
        on_device, mesh=mesh, in_specs=in_specs, out_specs=out_specs, check_vma=False
    )
```
